512 devices in a mesh: tm: 16 (over y_hi, z), space: 32 (over x, y_lo, core).
Axes of the slice: x: 4, y: 8 (y_hi: 2, y_lo: 4; y = y_hi * 4 + y_lo), z: 8, core: 2. Of those that a mesh axis runs over, the one named last changes fastest.
Arguments:
- forcing: float32 [256, 3, 64, 8, 128], P('tm', None, 'space'), may hold values from -6 to 6
- start_field: float32 [3, 64, 8, 128], P(None, 'space'), may hold values from -6 to 6
- iterate: float32 [256, 3, 64, 8, 128], P('tm', None, 'space'), may hold values from -12 to 12
- region: int32 [64, 8, 128], P('space'), may hold values from 0 to 2
- conductance: float32 [3], replicated, may hold values from 0.5 to 4
Outputs:
- updated: float32 [256, 3, 64, 8, 128], P('tm', None, 'space')
The draws below stay inside these ranges and needn't reach their ends.
All inputs are finite; a program needn't handle non-finite values.
Results may differ from the reference program's by a relative error of at most 0.00013.
Values sent between devices are 32-bit elements; how exact they have to be, the bound alone decides.
No kernel may reach another device: no remote copies, remote signals or barrier semaphores. Data moves between devices by JAX's collectives and lax.ppermute only.
A program may use at most 64 MiB of HBM per device.

```python
import math
import jax
import jax.numpy as jnp
from jax import lax

WINDOW = 256
NY = 8
NZ = 128
SWEEPS = 12
NX = 64


def with_ends(values, stream_key, least, top_value):
    extent = values.shape
    place = [jax.random.randint(jax.random.fold_in(stream_key, axis), (), 0, extent[axis]) for axis in range(len(extent))]
    values = values.at[tuple(place)].set(least)
    longest = extent.index(max(extent))
    place[longest] = (place[longest] + 1) % extent[longest]
    return values.at[tuple(place)].set(top_value)


def block_scale(rng, dims, split, smallest, top_value):
    loudness = 1.0
    for axis_at, parts in split:
        steps = jax.random.uniform(jax.random.fold_in(jax.random.fold_in(rng, 6), axis_at), (parts,), jnp.float32, smallest / len(split), top_value / len(split))
        loudness = loudness * jnp.repeat(jnp.exp(steps), dims[axis_at] // parts).reshape((-1,) + (1,) * (len(dims) - 1 - axis_at))
    return loudness


def gaussian(stream_key, dims, spread, limit, cuts=(), dtype=jnp.bfloat16):
    array = spread * jax.random.normal(stream_key, dims, jnp.float32)
    if cuts:
        array = array * block_scale(stream_key, dims, cuts, -0.22, 0.18)
    return jnp.clip(array, -limit, limit).astype(dtype)


def setup_inputs(seed: int = 0) -> dict:
    arg_keys = jax.random.split(jax.random.key(seed), 6)
    return {
        "forcing": gaussian(arg_keys[0], (WINDOW, 3, NX, NY, NZ), 1.0, 6.0, ((0, 16), (2, 32)), jnp.float32),
        "start_field": gaussian(arg_keys[1], (3, NX, NY, NZ), 1.0, 6.0, ((1, 32),), jnp.float32),
        "iterate": gaussian(arg_keys[2], (WINDOW, 3, NX, NY, NZ), 2.0, 12.0, ((0, 16), (2, 32)), jnp.float32),
        "region": with_ends(jax.random.randint(arg_keys[3], (NX, NY, NZ), 0, 3), jax.random.fold_in(arg_keys[3], 1), 0, 2).astype(jnp.int32),
        "conductance": jnp.clip(jnp.exp(jax.random.uniform(arg_keys[4], (3,), jnp.float32, math.log(0.5), math.log(4.0))), 0.5, 4.0),
    }


ALPHA = 0.1
LOWER = 0.02
UPPER = 1.0
SIGMA_TOP = 4.0
CURL_TOP = 12.0

def forward_step(values, axis):
    inner = lax.slice_in_dim(values, 1, values.shape[axis], axis=axis)
    border = jnp.zeros_like(lax.slice_in_dim(values, 0, 1, axis=axis))
    return jnp.concatenate([inner, border], axis) - values

def backward_step(values, axis):
    inner = lax.slice_in_dim(values, 0, values.shape[axis] - 1, axis=axis)
    border = jnp.zeros_like(lax.slice_in_dim(values, 0, 1, axis=axis))
    return jnp.concatenate([border, inner], axis) - values

def curl_forward(field):
    field_x, field_y, field_z = (field[:, 0], field[:, 1], field[:, 2])
    lead_x, lead_y, lead_z = (field_x[:, :-1], field_y[:, :-1], field_z[:, :-1])
    flux_x = forward_step(lead_z, 2) - forward_step(lead_y, 3)
    flux_y = forward_step(lead_x, 3) - (field_z[:, 1:] - field_z[:, :-1])
    flux_z = field_y[:, 1:] - field_y[:, :-1] - forward_step(lead_x, 2)
    return jnp.stack([flux_x, flux_y, flux_z], axis=1)

def curl_adjoint(flux):
    flux_x, flux_y, flux_z = (flux[:, 0], flux[:, 1], flux[:, 2])
    tail_x, tail_y, tail_z = (flux_x[:, 1:], flux_y[:, 1:], flux_z[:, 1:])
    field_x = backward_step(tail_y, 3) - backward_step(tail_z, 2)
    field_y = flux_z[:, :-1] - flux_z[:, 1:] - backward_step(tail_x, 3)
    field_z = backward_step(tail_x, 2) - (flux_y[:, :-1] - flux_y[:, 1:])
    return jnp.stack([field_x, field_y, field_z], axis=1)

def full_curl(field):
    plane = jnp.zeros_like(field[:, :, :1])
    flux = curl_forward(jnp.concatenate([field, plane], 2))
    return curl_adjoint(jnp.concatenate([jnp.zeros_like(flux[:, :, :1]), flux], 2))

def pair_terms(pairs, window):
    gamma = ALPHA ** (1.0 / window)
    angle = 2.0 * math.pi * pairs.astype(jnp.float32) / window
    plain = 1.0 - gamma * jnp.cos(angle)
    p_plus = jnp.where(pairs == 0, 1.0 - gamma, plain)
    p_minus = jnp.where(pairs == 0, 1.0 + gamma, plain)
    q_term = jnp.where(pairs == 0, 0.0, gamma * jnp.sin(angle))
    bound = jnp.sqrt(jnp.maximum(p_plus, p_minus) ** 2 + q_term ** 2) * SIGMA_TOP + CURL_TOP
    return (p_plus, p_minus, q_term, bound * bound)

def cas_rows(freqs, window):
    moments = jnp.arange(window).astype(jnp.int32)
    product = freqs[:, None] * moments[None, :] % window
    angle = 2.0 * math.pi * product.astype(jnp.float32) / window
    return jnp.cos(angle) + jnp.sin(angle)

def powers(window, sign):
    gamma = jnp.float32(ALPHA ** (sign / window))
    return jnp.power(gamma, jnp.arange(window).astype(jnp.float32))

def chebyshev_terms(count):
    center = (UPPER + LOWER) / 2.0
    radius = (UPPER - LOWER) / 2.0
    spread_ratio = center / radius
    weight_now = 1.0 / spread_ratio
    carry_terms, push_terms = ([], [])
    for _ in range(count):
        weight_next = 1.0 / (2.0 * spread_ratio - weight_now)
        carry_terms.append(weight_next * weight_now)
        push_terms.append(2.0 * weight_next / radius)
        weight_now = weight_next
    return (jnp.asarray(carry_terms, jnp.float32), jnp.asarray(push_terms, jnp.float32), center)

def reference(forcing, start_field, iterate, region, conductance):
    window = forcing.shape[0]
    half = window // 2
    sigma = jnp.zeros(region.shape, jnp.float32)
    for material in range(3):
        sigma = sigma + conductance[material] * (region == material).astype(jnp.float32)
    jump = sigma * (start_field - ALPHA * iterate[window - 1])
    rhs = forcing.at[0].add(jump)
    cells = rhs[0].size
    flat = rhs.reshape(window, cells)
    pairs = jnp.arange(half).astype(jnp.int32)
    k_plus = pairs
    k_minus = jnp.where(pairs == 0, half, window - pairs).astype(jnp.int32)
    grow = powers(window, 1.0)
    shrink = powers(window, -1.0)
    spec_plus = jnp.dot(cas_rows(k_plus, window) * grow[None, :], flat, precision=lax.Precision.HIGHEST)
    spec_minus = jnp.dot(cas_rows(k_minus, window) * grow[None, :], flat, precision=lax.Precision.HIGHEST)
    p_plus, p_minus, q_term, scale = pair_terms(pairs, window)
    carry_terms, push_terms, center = chebyshev_terms(SWEEPS - 1)
    shape = (2,) + forcing.shape[1:]

    def solve_pair(items):
        rhs_plus, rhs_minus, plus_coef, minus_coef, cross, norm_scale = items
        stacked = jnp.stack([rhs_plus, rhs_minus]).reshape(shape)
        diagonal_coef = jnp.stack([plus_coef, minus_coef]).reshape(2, 1, 1, 1, 1)

        def couple(values, sign):
            swapped = jnp.stack([-cross * values[1], cross * values[0]])
            return sigma * (diagonal_coef * values + sign * swapped)

        def normal(values):
            first = full_curl(values) + couple(values, 1.0)
            return (full_curl(first) + couple(first, -1.0)) / norm_scale
        start = (full_curl(stacked) + couple(stacked, -1.0)) / norm_scale

        def sweep(sweep_index, carry_state):
            current, residual, direction = carry_state
            current = current + direction
            residual = residual - normal(direction)
            direction = carry_terms[sweep_index] * direction + push_terms[sweep_index] * residual
            return (current, residual, direction)
        current, residual, direction = lax.fori_loop(0, SWEEPS - 1, sweep, (jnp.zeros_like(start), start, start / center))
        result = (current + direction).reshape(2, cells)
        return (result[0], result[1])
    sol_plus, sol_minus = lax.map(solve_pair, (spec_plus, spec_minus, p_plus, p_minus, q_term, scale))
    back_plus = cas_rows(k_plus, window).T * (shrink / window)[:, None]
    back_minus = cas_rows(k_minus, window).T * (shrink / window)[:, None]
    updated = jnp.dot(back_plus, sol_plus, precision=lax.Precision.HIGHEST) + jnp.dot(back_minus, sol_minus, precision=lax.Precision.HIGHEST)
    return updated.reshape(forcing.shape)
```

```python
import functools
import math

import jax
import jax.numpy as jnp
import numpy as np
from jax import lax
from jax.experimental import pallas as pl
from jax.experimental.pallas import tpu as pltpu
from jax.sharding import Mesh
from jax.sharding import PartitionSpec as P

SWEEPS = 12
ALPHA = 0.1
LOWER = 0.02
UPPER = 1.0
SIGMA_TOP = 4.0
CURL_TOP = 12.0

TM = ("yh", "z")
PAIRS = ("yl", "c", "yh", "z")
BLOCK = 16
REACH = 24
GUARD = 2


def tables(window):
    gamma = ALPHA ** (1.0 / window)
    half = window // 2
    pairs = np.arange(half)
    freqs = np.concatenate([pairs, np.where(pairs == 0, half, window - pairs)])
    moments = np.arange(window)
    angle = 2.0 * math.pi * (freqs[:, None] * moments[None, :] % window) / window
    cas = np.cos(angle) + np.sin(angle)
    forward = cas * gamma ** moments[None, :]
    inverse = cas.T * gamma ** (-moments[:, None]) / window
    return forward.astype(np.float32), inverse.astype(np.float32)


def pair_table(window):
    gamma = ALPHA ** (1.0 / window)
    pairs = np.arange(window // 2)
    theta = 2.0 * math.pi * pairs / window
    plain = 1.0 - gamma * np.cos(theta)
    p_plus = np.where(pairs == 0, 1.0 - gamma, plain)
    p_minus = np.where(pairs == 0, 1.0 + gamma, plain)
    q_term = np.where(pairs == 0, 0.0, gamma * np.sin(theta))
    bound = np.sqrt(np.maximum(p_plus, p_minus) ** 2 + q_term**2) * SIGMA_TOP + CURL_TOP
    return np.stack([p_plus, p_minus, q_term, 1.0 / bound**2]).astype(np.float32)


def chebyshev_terms(count):
    center = (UPPER + LOWER) / 2.0
    radius = (UPPER - LOWER) / 2.0
    spread_ratio = center / radius
    weight_now = 1.0 / spread_ratio
    carry_terms, push_terms = ([], [])
    for _ in range(count):
        weight_next = 1.0 / (2.0 * spread_ratio - weight_now)
        carry_terms.append(weight_next * weight_now)
        push_terms.append(2.0 * weight_next / radius)
        weight_now = weight_next
    return (carry_terms, push_terms, center)


def material(region, cond):
    return jnp.where(
        region == 0,
        cond[0],
        jnp.where(region == 1, cond[1], jnp.where(region == 2, cond[2], 0.0)),
    )


def pack_kernel(cond, forcing, start, latest, region, out):
    steps, comps, planes, ny, _ = forcing.shape
    rows = out.shape[0] // (planes * ny)
    is_first = (lax.axis_index("yh") == 0) & (lax.axis_index("z") == 0)
    for p in range(planes):
        sigma = material(region[p], cond)
        base = p * ny * rows
        for c in range(comps):
            head = forcing[0, c, p]
            head = head + jnp.where(is_first, sigma * start[c, p], 0.0)
            out[pl.ds(base + c * steps, ny, stride=rows), :] = head
            for b in range(1, steps):
                out[pl.ds(base + c * steps + b, ny, stride=rows), :] = forcing[b, c, p]
            out[pl.ds(base + comps * steps + c, ny, stride=rows), :] = -ALPHA * (
                sigma * latest[0, c, p]
            )
        for pad in range(comps * steps + comps, rows):
            out[pl.ds(base + pad, ny, stride=rows), :] = jnp.zeros_like(sigma)


def forward_kernel(cond, got, table, region, out):
    groups, _, nz = got.shape
    window = table.shape[0]
    steps = window // groups
    comps = 3
    half = window // 2
    head = lax.broadcasted_iota(jnp.int32, (window, nz), 0) == 0
    parts = []
    for c in range(comps):
        part = got[:, c * steps : (c + 1) * steps, :].reshape(window, nz)
        row = got[groups - 1, comps * steps + c : comps * steps + c + 1, :]
        parts.append(part + jnp.where(head, row, 0.0))
    spectrum = jnp.dot(
        table[...],
        jnp.concatenate(parts, axis=1),
        precision=lax.Precision.HIGHEST,
        preferred_element_type=jnp.float32,
    )
    width = comps * nz
    out[:, :width] = spectrum[:half]
    out[:, width : 2 * width] = spectrum[half:]
    line = region[lax.axis_index("yh"), pl.ds(lax.axis_index("z"), 1), :]
    out[:, 2 * width :] = jnp.broadcast_to(material(line, cond), (half, nz))


def inverse_kernel(got, table, out):
    half, wide = got.shape
    groups, rows, nz = out.shape
    steps = table.shape[0] // groups
    width = wide // 2
    dot = functools.partial(
        jnp.dot, precision=lax.Precision.HIGHEST, preferred_element_type=jnp.float32
    )
    result = dot(table[:, :half], got[:, :width]) + dot(table[:, half:], got[:, width:])
    for c in range(rows // steps):
        out[:, c * steps : (c + 1) * steps, :] = result[:, c * nz : (c + 1) * nz].reshape(
            groups, steps, nz
        )


def unpack_kernel(got, out):
    steps, comps, planes, ny, _ = out.shape
    rows = got.shape[0] // (planes * ny)
    for p in range(planes):
        for c in range(comps):
            for b in range(steps):
                out[b, c, p] = got[pl.ds(p * ny * rows + c * steps + b, ny, stride=rows), :]


def solve_kernel(terms, own, left, right, far, out, field, resid, total, sigma):
    ny, nz = field.shape[2:]
    x_at = lax.axis_index("x")
    pair = lax.axis_index(PAIRS)
    p_plus, p_minus = terms[0, pair], terms[1, pair]
    q_term, inv_scale = terms[2, pair], terms[3, pair]
    carry_terms, push_terms, center = chebyshev_terms(SWEEPS - 1)

    row = lax.broadcasted_iota(jnp.int32, (ny, nz), 0)
    lane = lax.broadcasted_iota(jnp.int32, (ny, nz), 1)
    row_first, row_last = row == 0, row == ny - 1
    lane_first, lane_last = lane == 0, lane == nz - 1

    def ahead_y(f):
        return jnp.where(row_last, 0.0, pltpu.roll(f, ny - 1, 0))

    def ahead_z(f):
        return jnp.where(lane_last, 0.0, pltpu.roll(f, nz - 1, 1))

    def behind_y(f):
        return jnp.where(row_first, 0.0, pltpu.roll(f, 1, 0))

    def behind_z(f):
        return jnp.where(lane_first, 0.0, pltpu.roll(f, 1, 1))

    def curl(now, after):
        ex, ey, ez = now
        _, ey_after, ez_after = after
        return (
            (ahead_y(ez) - ez) - (ahead_z(ey) - ey),
            (ahead_z(ex) - ex) - (ez_after - ez),
            (ey_after - ey) - (ahead_y(ex) - ex),
        )

    def adjoint(now, before):
        bx, by, bz = now
        by_before, bz_before = before
        return (
            (behind_z(by) - by) - (behind_y(bz) - bz),
            (bz_before - bz) - (behind_z(bx) - bx),
            (behind_y(bx) - bx) - (by_before - by),
        )

    def both(fn, one, two):
        return tuple(fn(one[3 * f : 3 * f + 3], two[two_at : two_at + len(two) // 2])
                     for f, two_at in ((0, 0), (1, len(two) // 2)))

    def curls(now, after):
        a, b = both(curl, now, after)
        return a + b

    def adjoints(now, before):
        a, b = both(adjoint, now, before)
        return a + b

    def tails(flux):
        return (flux[1], flux[2], flux[4], flux[5])

    def couple(values, weight, sign):
        sp, sm, sq = weight * p_plus, weight * p_minus, weight * (sign * q_term)
        up = tuple(sp * values[c] - sq * values[3 + c] for c in range(3))
        down = tuple(sm * values[3 + c] + sq * values[c] for c in range(3))
        return up + down

    def plus(a, b):
        return tuple(u + v for u, v in zip(a, b))

    def keep(flag, values):
        return tuple(jnp.where(flag, v, 0.0) for v in values)

    def load(ref, at):
        return tuple(ref[at + GUARD, k] for k in range(6))

    def store(ref, at, values):
        for k in range(6):
            ref[at + GUARD, k] = values[k]

    def fill(source, first, count):
        def one(i, _):
            line = pl.ds(pl.multiple_of(i * ny, ny), ny)
            for k in range(6):
                field[first + i + GUARD, k] = source[line, k * nz : (k + 1) * nz]
            sigma[first + i + GUARD] = source[line, 6 * nz : 7 * nz]
            return 0

        lax.fori_loop(0, count, one, 0)

    extra = far.shape[0] // ny
    low_far, high_far = REACH - BLOCK - extra, REACH + 2 * BLOCK
    blank = jnp.zeros((ny, nz), jnp.float32)
    for at in [*range(-GUARD, extra), *range(high_far, high_far + extra + GUARD)]:
        for k in range(6):
            field[at + GUARD, k] = blank
        sigma[at + GUARD] = blank
    fill(left, REACH - BLOCK, BLOCK)
    fill(own, REACH, BLOCK)
    fill(right, REACH + BLOCK, BLOCK)
    blocks = lax.axis_size("x")
    fill(far, jnp.where(x_at < blocks // 2, high_far, low_far), extra)

    grid_low = REACH - BLOCK * x_at
    grid_high = grid_low + BLOCK * blocks

    def bounds(margin):
        low = jnp.maximum(grid_low, REACH - margin)
        high = jnp.minimum(grid_high, REACH + BLOCK + margin)
        return low, high

    low, high = bounds(2 * (SWEEPS - 1))

    def start_step(i, state):
        now, before = state[:6], state[6:]
        after = load(field, i + 1)
        flux = curls(now, after)
        value = plus(adjoints(flux, before), couple(now, sigma[i + GUARD], -1.0))
        value = tuple(v * inv_scale for v in value)
        store(resid, i, value)
        store(field, i, tuple(v * (1.0 / center) for v in value))
        return after + tails(flux)

    before = tails(curls(load(field, low - 1), load(field, low)))
    before = keep(low > grid_low, before)
    lax.fori_loop(low, high, start_step, load(field, low) + before)

    def zero_total(i, _):
        for k in range(6):
            total[i, k] = blank
        return 0

    lax.fori_loop(0, BLOCK, zero_total, 0)

    for s in range(SWEEPS - 1):
        low, high = bounds(2 * (SWEEPS - 2 - s))
        keep_low, keep_high = low > grid_low, high < grid_high
        carry_term, push_term = carry_terms[s], push_terms[s]

        def add_total(i, _):
            for k in range(6):
                total[i, k] = total[i, k] + field[i + REACH + GUARD, k]
            return 0

        lax.fori_loop(0, BLOCK, add_total, 0)

        def advance(i, now, before, after):
            flux = curls(now, after)
            return plus(adjoints(flux, before), couple(now, sigma[i + GUARD], 1.0)), tails(flux)

        def finish(i, first_now, first_after, before):
            flux = curls(first_now, first_after)
            value = plus(adjoints(flux, before), couple(first_now, sigma[i + GUARD], -1.0))
            rest = tuple(r - v * inv_scale for r, v in zip(load(resid, i), value))
            store(resid, i, rest)
            store(
                field,
                i,
                tuple(carry_term * d + push_term * r for d, r in zip(load(field, i), rest)),
            )
            return tails(flux)

        def sweep_step(i, state):
            now, before, first, first_before = (
                state[:6],
                state[6:10],
                state[10:16],
                state[16:20],
            )
            after = load(field, i + 1)
            first_after, before = advance(i, now, before, after)
            first_before = finish(i - 1, first, first_after, first_before)
            return after + before + first_after + first_before

        now = load(field, low - 1)
        before = tails(curls(load(field, low - 2), now))
        after = load(field, low)
        first_low, before = advance(low - 1, now, before, after)
        before = keep(keep_low, before)
        now, after = after, load(field, low + 1)
        first, before = advance(low, now, before, after)
        first_before = keep(keep_low, tails(curls(first_low, first)))
        now, before, first, first_before = (
            lambda st: (st[:6], st[6:10], st[10:16], st[16:20])
        )(lax.fori_loop(low + 1, high, sweep_step, after + before + first + first_before))
        last, _ = advance(high, now, before, load(field, high + 1))
        finish(high - 1, first, keep(keep_high, last), first_before)

    def write(i, _):
        line = pl.ds(pl.multiple_of(i * ny, ny), ny)
        for k in range(6):
            out[line, k * nz : (k + 1) * nz] = total[i, k] + field[i + REACH + GUARD, k]
        return 0

    lax.fori_loop(0, BLOCK, write, 0)


def per_device(forcing, start_field, iterate, region, conductance):
    steps, comps, planes, ny, nz = forcing.shape
    groups = lax.axis_size(TM)
    window = steps * groups
    half = window // 2
    forward_table, inverse_table = tables(window)
    vmem = pl.BlockSpec(memory_space=pltpu.VMEM)
    smem = pl.BlockSpec(memory_space=pltpu.SMEM)
    f32 = jnp.float32
    params = pltpu.CompilerParams(vmem_limit_bytes=32 * 1024 * 1024)

    rows = comps * steps + 8
    whole = lambda shape: pl.BlockSpec(shape, lambda i: (0,) * len(shape))
    packed = pl.pallas_call(
        pack_kernel,
        out_shape=jax.ShapeDtypeStruct((groups * rows, nz), f32),
        grid=(1,),
        in_specs=[
            smem,
            whole(forcing.shape),
            whole(start_field.shape),
            pl.BlockSpec((1, comps, planes, ny, nz), lambda i: (steps - 1, 0, 0, 0, 0)),
            whole(region.shape),
        ],
        out_specs=whole((groups * rows, nz)),
        compiler_params=params,
        name="pack",
    )(conductance, forcing, start_field, iterate, region)

    got = lax.all_to_all(packed.reshape(groups, rows, nz), TM, 0, 0, tiled=True)

    spectrum = pl.pallas_call(
        forward_kernel,
        out_shape=jax.ShapeDtypeStruct((half, (2 * comps + 1) * nz), f32),
        in_specs=[smem, vmem, vmem, vmem],
        out_specs=vmem,
        compiler_params=params,
        name="forward",
    )(conductance, got, jnp.asarray(forward_table), region)

    own = lax.all_to_all(spectrum, PAIRS, 0, 0, tiled=True)

    count = lax.axis_size("x")
    x_at = lax.axis_index("x")
    left = lax.ppermute(own, "x", [(i, i + 1) for i in range(count - 1)])
    right = lax.ppermute(own, "x", [(i + 1, i) for i in range(count - 1)])
    part = lax.dynamic_slice_in_dim(
        own, jnp.where(x_at < count // 2, half // 2, 0), half // 2, 0
    )
    far = lax.ppermute(part, "x", [(i, (i + 2) % count) for i in range(count)])

    places = 2 * REACH + BLOCK + 2 * GUARD
    solved = pl.pallas_call(
        solve_kernel,
        out_shape=jax.ShapeDtypeStruct((half, 2 * comps * nz), f32),
        in_specs=[smem, vmem, vmem, vmem, vmem],
        out_specs=vmem,
        scratch_shapes=[
            pltpu.VMEM((places, 6, ny, nz), f32),
            pltpu.VMEM((places, 6, ny, nz), f32),
            pltpu.VMEM((BLOCK, 6, ny, nz), f32),
            pltpu.VMEM((places, ny, nz), f32),
        ],
        compiler_params=params,
        name="solve",
    )(jnp.asarray(pair_table(window)), own, left, right, far)

    back = lax.all_to_all(solved, PAIRS, 0, 0, tiled=True)

    pencil = pl.pallas_call(
        inverse_kernel,
        out_shape=jax.ShapeDtypeStruct((groups, comps * steps, nz), f32),
        in_specs=[vmem, vmem],
        out_specs=vmem,
        compiler_params=params,
        name="inverse",
    )(back, jnp.asarray(inverse_table))

    home = lax.all_to_all(pencil, TM, 0, 0, tiled=True)

    return pl.pallas_call(
        unpack_kernel,
        out_shape=jax.ShapeDtypeStruct(forcing.shape, f32),
        in_specs=[vmem],
        out_specs=vmem,
        compiler_params=params,
        name="unpack",
    )(home.reshape(groups * comps * steps, nz))


def solution(mesh):
    fine = Mesh(mesh.devices.reshape(2, 8, 4, 4, 2), ("yh", "z", "x", "yl", "c"))
    space = ("x", "yl", "c")
    placed = (
        P(TM, None, space, None, None),
        P(None, space, None, None),
        P(TM, None, space, None, None),
        P(space, None, None),
        P(),
    )
    return jax.shard_map(
        per_device,
        mesh=fine,
        in_specs=placed,
        out_specs=P(TM, None, space, None, None),
        check_vma=False,
    )
```

```python
import functools
import math

import jax
import jax.numpy as jnp
import numpy as np
from jax import lax
from jax.experimental import pallas as pl
from jax.experimental.pallas import tpu as pltpu
from jax.sharding import Mesh
from jax.sharding import PartitionSpec as P

SWEEPS = 12
ALPHA = 0.1
LOWER = 0.02
UPPER = 1.0
SIGMA_TOP = 4.0
CURL_TOP = 12.0

TM = ("yh", "z")
PAIRS = ("yl", "c", "yh", "z")
BLOCK = 16
REACH = 24
GUARD = 1
CHUNK = 8


def tables(window):
    gamma = ALPHA ** (1.0 / window)
    half = window // 2
    pairs = np.arange(half)
    freqs = np.concatenate([pairs, np.where(pairs == 0, half, window - pairs)])
    moments = np.arange(window)
    angle = 2.0 * math.pi * (freqs[:, None] * moments[None, :] % window) / window
    cas = np.cos(angle) + np.sin(angle)
    forward = cas * gamma ** moments[None, :]
    inverse = cas.T * gamma ** (-moments[:, None]) / window
    return forward.astype(np.float32), inverse.astype(np.float32)


def pair_table(window):
    gamma = ALPHA ** (1.0 / window)
    pairs = np.arange(window // 2)
    theta = 2.0 * math.pi * pairs / window
    plain = 1.0 - gamma * np.cos(theta)
    p_plus = np.where(pairs == 0, 1.0 - gamma, plain)
    p_minus = np.where(pairs == 0, 1.0 + gamma, plain)
    q_term = np.where(pairs == 0, 0.0, gamma * np.sin(theta))
    bound = np.sqrt(np.maximum(p_plus, p_minus) ** 2 + q_term**2) * SIGMA_TOP + CURL_TOP
    return np.stack([p_plus, p_minus, q_term, 1.0 / bound**2]).astype(np.float32)


def chebyshev_terms(count):
    center = (UPPER + LOWER) / 2.0
    radius = (UPPER - LOWER) / 2.0
    spread_ratio = center / radius
    weight_now = 1.0 / spread_ratio
    carry_terms, push_terms = ([], [])
    for _ in range(count):
        weight_next = 1.0 / (2.0 * spread_ratio - weight_now)
        carry_terms.append(weight_next * weight_now)
        push_terms.append(2.0 * weight_next / radius)
        weight_now = weight_next
    return (carry_terms, push_terms, center)


def material(region, cond):
    return jnp.where(
        region == 0,
        cond[0],
        jnp.where(region == 1, cond[1], jnp.where(region == 2, cond[2], 0.0)),
    )


def pack_kernel(cond, forcing, start, latest, region, out):
    steps, comps, planes, ny, _ = forcing.shape
    rows = out.shape[0] // (planes * ny)
    is_first = (lax.axis_index("yh") == 0) & (lax.axis_index("z") == 0)
    for p in range(planes):
        sigma = material(region[p], cond)
        base = p * ny * rows
        for c in range(comps):
            head = forcing[0, c, p]
            head = head + jnp.where(is_first, sigma * start[c, p], 0.0)
            out[pl.ds(base + c * steps, ny, stride=rows), :] = head
            for b in range(1, steps):
                out[pl.ds(base + c * steps + b, ny, stride=rows), :] = forcing[b, c, p]
            out[pl.ds(base + comps * steps + c, ny, stride=rows), :] = -ALPHA * (
                sigma * latest[0, c, p]
            )
        for pad in range(comps * steps + comps, rows):
            out[pl.ds(base + pad, ny, stride=rows), :] = jnp.zeros_like(sigma)


def forward_kernel(got, table, out):
    groups, _, nz = got.shape
    window = table.shape[0]
    steps = window // groups
    comps = 3
    half = window // 2
    head = lax.broadcasted_iota(jnp.int32, (window, nz), 0) == 0
    parts = []
    for c in range(comps):
        part = got[:, c * steps : (c + 1) * steps, :].reshape(window, nz)
        row = got[groups - 1, comps * steps + c : comps * steps + c + 1, :]
        parts.append(part + jnp.where(head, row, 0.0))
    spectrum = jnp.dot(
        table[...],
        jnp.concatenate(parts, axis=1),
        precision=lax.Precision.HIGHEST,
        preferred_element_type=jnp.float32,
    )
    width = comps * nz
    out[:, :width] = spectrum[:half]
    out[:, width:] = spectrum[half:]


def inverse_kernel(got, table, out):
    half, wide = got.shape
    groups, rows, nz = out.shape
    steps = table.shape[0] // groups
    width = wide // 2
    dot = functools.partial(
        jnp.dot, precision=lax.Precision.HIGHEST, preferred_element_type=jnp.float32
    )
    result = dot(table[:, :half], got[:, :width]) + dot(table[:, half:], got[:, width:])
    for c in range(rows // steps):
        out[:, c * steps : (c + 1) * steps, :] = result[:, c * nz : (c + 1) * nz].reshape(
            groups, steps, nz
        )


def unpack_kernel(got, out):
    steps, comps, planes, ny, _ = out.shape
    rows = got.shape[0] // (planes * ny)
    for p in range(planes):
        for c in range(comps):
            for b in range(steps):
                out[b, c, p] = got[pl.ds(p * ny * rows + c * steps + b, ny, stride=rows), :]


def solve_kernel(terms, cond, region, own, left, right, far, out, field, first, resid, total, sigma):
    ny, nz = field.shape[2:]
    x_at = lax.axis_index("x")
    pair = lax.axis_index(PAIRS)
    p_plus, p_minus = terms[0, pair], terms[1, pair]
    q_term, inv_scale = terms[2, pair], terms[3, pair]
    carry_terms, push_terms, center = chebyshev_terms(SWEEPS - 1)

    row = lax.broadcasted_iota(jnp.int32, (ny, nz), 0)
    lane = lax.broadcasted_iota(jnp.int32, (ny, nz), 1)
    row_first, row_last = row == 0, row == ny - 1
    lane_first, lane_last = lane == 0, lane == nz - 1
    blank = jnp.zeros((ny, nz), jnp.float32)

    def ahead_y(f):
        return jnp.where(row_last, 0.0, pltpu.roll(f, ny - 1, 0))

    def ahead_z(f):
        return jnp.where(lane_last, 0.0, pltpu.roll(f, nz - 1, 1))

    def behind_y(f):
        return jnp.where(row_first, 0.0, pltpu.roll(f, 1, 0))

    def behind_z(f):
        return jnp.where(lane_first, 0.0, pltpu.roll(f, 1, 1))

    def curls(now, after):
        flux = []
        for f in (0, 3):
            ex, ey, ez = now[f : f + 3]
            _, ey_after, ez_after = after[f : f + 3]
            flux += [
                (ahead_y(ez) - ez) - (ahead_z(ey) - ey),
                (ahead_z(ex) - ex) - (ez_after - ez),
                (ey_after - ey) - (ahead_y(ex) - ex),
            ]
        return flux

    def tails(now, after):
        flux = []
        for f in (0, 3):
            ex, ey, ez = now[f : f + 3]
            _, ey_after, ez_after = after[f : f + 3]
            flux += [
                (ahead_z(ex) - ex) - (ez_after - ez),
                (ey_after - ey) - (ahead_y(ex) - ex),
            ]
        return flux

    def adjoints(flux, before):
        field = []
        for f, g in ((0, 0), (3, 2)):
            bx, by, bz = flux[f : f + 3]
            by_before, bz_before = before[g : g + 2]
            field += [
                (behind_z(by) - by) - (behind_y(bz) - bz),
                (bz_before - bz) - (behind_z(bx) - bx),
                (behind_y(bx) - bx) - (by_before - by),
            ]
        return field

    def add_couple(field, values, weight, sign):
        sp, sm, sq = weight * p_plus, weight * p_minus, weight * (sign * q_term)
        return [
            field[c] + (sp * values[c] - sq * values[3 + c]) for c in range(3)
        ] + [field[3 + c] + (sm * values[3 + c] + sq * values[c]) for c in range(3)]

    def load(ref, at):
        return [ref[at + GUARD, k] for k in range(6)]

    def store(ref, at, values):
        for k in range(6):
            ref[at + GUARD, k] = values[k]

    blocks = lax.axis_size("x")
    width = 2 * REACH + BLOCK
    grid_low = REACH - BLOCK * x_at
    grid_high = grid_low + BLOCK * blocks
    top = jnp.minimum(grid_high, width)

    def fill(source, begin, count):
        def some(t, _):
            for u in range(CHUNK):
                i = t * CHUNK + u
                line = pl.ds(pl.multiple_of(i * ny, ny), ny)
                store(first, begin + i, [source[line, k * nz : (k + 1) * nz] for k in range(6)])
            return 0

        lax.fori_loop(0, count // CHUNK, some, 0)

    extra = far.shape[0] // ny
    low_far, high_far = 0, REACH + 2 * BLOCK
    for at in [*range(-1, extra), *range(high_far, high_far + extra + 1)]:
        store(first, at, [blank] * 6)
    fill(left, REACH - BLOCK, BLOCK)
    fill(own, REACH, BLOCK)
    fill(right, REACH + BLOCK, BLOCK)
    fill(far, jnp.where(x_at < blocks // 2, high_far, low_far), extra)
    store(field, top, [blank] * 6)
    store(field, -1, [blank] * 6)

    def bounds(margin):
        margin = -(-margin // CHUNK) * CHUNK
        low = jnp.maximum(grid_low, REACH - margin)
        high = jnp.minimum(grid_high, REACH + BLOCK + margin)
        return low, high

    def run(margin, source, sign, finish):
        low, high = bounds(margin)

        def some(t, _):
            begin = low + t * CHUNK
            now = load(source, begin)
            before = tails(load(source, begin - 1), now)
            before = [jnp.where(begin > grid_low, v, 0.0) for v in before]
            for u in range(CHUNK):
                i = begin + u
                after = load(source, i + 1)
                flux = curls(now, after)
                value = adjoints(flux, before)
                finish(i, add_couple(value, now, sigma[i + GUARD], sign))
                now, before = after, [flux[1], flux[2], flux[4], flux[5]]
            return 0

        lax.fori_loop(0, (high - low) // CHUNK, some, 0)

    low, high = bounds(REACH)

    def fill_sigma(t, _):
        for u in range(CHUNK):
            i = low + t * CHUNK + u
            sigma[i + GUARD] = material(region[i - grid_low], cond)
        return 0

    lax.fori_loop(0, (high - low) // CHUNK, fill_sigma, 0)

    def begin_with(i, value):
        store(resid, i, value)
        store(field, i, [v * (inv_scale * (1.0 / center)) for v in value])

    run(2 * (SWEEPS - 1), first, -1.0, begin_with)

    for s in range(SWEEPS - 1):
        margin = 2 * (SWEEPS - 2 - s)
        carry_term, push_term = carry_terms[s], push_terms[s] * inv_scale

        def add_total(t, _):
            for u in range(CHUNK):
                i = t * CHUNK + u
                for k in range(6):
                    step = field[i + REACH + GUARD, k]
                    total[i, k] = step if s == 0 else total[i, k] + step
            return 0

        lax.fori_loop(0, BLOCK // CHUNK, add_total, 0)

        def keep_first(i, value):
            store(first, i, value)

        def update(i, value):
            rest = [r - v for r, v in zip(load(resid, i), value)]
            store(resid, i, rest)
            store(
                field,
                i,
                [carry_term * d + push_term * r for d, r in zip(load(field, i), rest)],
            )

        run(margin + 1, field, 1.0, keep_first)
        run(margin, first, -1.0, update)

    def write(t, _):
        for u in range(CHUNK):
            i = t * CHUNK + u
            line = pl.ds(pl.multiple_of(i * ny, ny), ny)
            for k in range(6):
                out[line, k * nz : (k + 1) * nz] = total[i, k] + field[i + REACH + GUARD, k]
        return 0

    lax.fori_loop(0, BLOCK // CHUNK, write, 0)


def per_device(forcing, start_field, iterate, region, conductance):
    steps, comps, planes, ny, nz = forcing.shape
    groups = lax.axis_size(TM)
    window = steps * groups
    half = window // 2
    forward_table, inverse_table = tables(window)
    vmem = pl.BlockSpec(memory_space=pltpu.VMEM)
    smem = pl.BlockSpec(memory_space=pltpu.SMEM)
    f32 = jnp.float32
    params = pltpu.CompilerParams(vmem_limit_bytes=12 * 1024 * 1024)
    materials = lax.all_gather(region, ("x", "yl", "c"), axis=0, tiled=True)

    rows = comps * steps + 8
    whole = lambda shape: pl.BlockSpec(shape, lambda i: (0,) * len(shape))
    packed = pl.pallas_call(
        pack_kernel,
        out_shape=jax.ShapeDtypeStruct((groups * rows, nz), f32),
        grid=(1,),
        in_specs=[
            smem,
            whole(forcing.shape),
            whole(start_field.shape),
            pl.BlockSpec((1, comps, planes, ny, nz), lambda i: (steps - 1, 0, 0, 0, 0)),
            whole(region.shape),
        ],
        out_specs=whole((groups * rows, nz)),
        compiler_params=pltpu.CompilerParams(vmem_limit_bytes=60 * 1024 * 1024),
        name="pack",
    )(conductance, forcing, start_field, iterate, region)

    got = lax.all_to_all(packed.reshape(groups, rows, nz), TM, 0, 0, tiled=True)

    spectrum = pl.pallas_call(
        forward_kernel,
        out_shape=jax.ShapeDtypeStruct((half, 2 * comps * nz), f32),
        in_specs=[vmem, vmem],
        out_specs=vmem,
        compiler_params=params,
        name="forward",
    )(got, jnp.asarray(forward_table))

    own = lax.all_to_all(spectrum, PAIRS, 0, 0, tiled=True)
    own, materials = lax.optimization_barrier((own, materials))

    count = lax.axis_size("x")
    x_at = lax.axis_index("x")
    left = lax.ppermute(own, "x", [(i, i + 1) for i in range(count - 1)])
    right = lax.ppermute(own, "x", [(i + 1, i) for i in range(count - 1)])
    part = lax.dynamic_slice_in_dim(
        own, jnp.where(x_at < count // 2, half // 2, 0), half // 2, 0
    )
    far = lax.ppermute(part, "x", [(i, (i + 2) % count) for i in range(count)])

    places = 2 * REACH + BLOCK + 2 * GUARD
    solved = pl.pallas_call(
        solve_kernel,
        out_shape=jax.ShapeDtypeStruct((half, 2 * comps * nz), f32),
        in_specs=[smem, smem, vmem, vmem, vmem, vmem, vmem],
        out_specs=vmem,
        scratch_shapes=[
            pltpu.VMEM((places, 6, ny, nz), f32),
            pltpu.VMEM((places, 6, ny, nz), f32),
            pltpu.VMEM((places, 6, ny, nz), f32),
            pltpu.VMEM((BLOCK, 6, ny, nz), f32),
            pltpu.VMEM((places, ny, nz), f32),
        ],
        compiler_params=params,
        name="solve",
    )(jnp.asarray(pair_table(window)), conductance, materials, own, left, right, far)

    back = lax.all_to_all(solved, PAIRS, 0, 0, tiled=True)

    pencil = pl.pallas_call(
        inverse_kernel,
        out_shape=jax.ShapeDtypeStruct((groups, comps * steps, nz), f32),
        in_specs=[vmem, vmem],
        out_specs=vmem,
        compiler_params=params,
        name="inverse",
    )(back, jnp.asarray(inverse_table))

    home = lax.all_to_all(pencil, TM, 0, 0, tiled=True)

    return pl.pallas_call(
        unpack_kernel,
        out_shape=jax.ShapeDtypeStruct(forcing.shape, f32),
        in_specs=[vmem],
        out_specs=vmem,
        compiler_params=params,
        name="unpack",
    )(home.reshape(groups * comps * steps, nz))


def solution(mesh):
    fine = Mesh(mesh.devices.reshape(2, 8, 4, 4, 2), ("yh", "z", "x", "yl", "c"))
    space = ("x", "yl", "c")
    placed = (
        P(TM, None, space, None, None),
        P(None, space, None, None),
        P(TM, None, space, None, None),
        P(space, None, None),
        P(),
    )
    return jax.shard_map(
        per_device,
        mesh=fine,
        in_specs=placed,
        out_specs=P(TM, None, space, None, None),
        check_vma=False,
    )
```

```python
import functools
import math

import jax
import jax.numpy as jnp
import numpy as np
from jax import lax
from jax.experimental import pallas as pl
from jax.experimental.pallas import tpu as pltpu
from jax.sharding import Mesh
from jax.sharding import PartitionSpec as P

SWEEPS = 12
ALPHA = 0.1
LOWER = 0.02
UPPER = 1.0
SIGMA_TOP = 4.0
CURL_TOP = 12.0

TM = ("yh", "z")
PAIRS = ("yl", "c", "yh", "z")
BLOCK = 16
REACH = 24
GUARD = 1
CHUNK = 8
LONG = 16
SHORT = (8,)


def tables(window):
    gamma = ALPHA ** (1.0 / window)
    half = window // 2
    pairs = np.arange(half)
    freqs = np.concatenate([pairs, np.where(pairs == 0, half, window - pairs)])
    moments = np.arange(window)
    angle = 2.0 * math.pi * (freqs[:, None] * moments[None, :] % window) / window
    cas = np.cos(angle) + np.sin(angle)
    forward = cas * gamma ** moments[None, :]
    inverse = cas.T * gamma ** (-moments[:, None]) / window
    return forward.astype(np.float32), inverse.astype(np.float32)


def pair_table(window):
    gamma = ALPHA ** (1.0 / window)
    pairs = np.arange(window // 2)
    theta = 2.0 * math.pi * pairs / window
    plain = 1.0 - gamma * np.cos(theta)
    p_plus = np.where(pairs == 0, 1.0 - gamma, plain)
    p_minus = np.where(pairs == 0, 1.0 + gamma, plain)
    q_term = np.where(pairs == 0, 0.0, gamma * np.sin(theta))
    bound = np.sqrt(np.maximum(p_plus, p_minus) ** 2 + q_term**2) * SIGMA_TOP + CURL_TOP
    return np.stack([p_plus, p_minus, q_term, 1.0 / bound**2]).astype(np.float32)


def chebyshev_terms(count):
    center = (UPPER + LOWER) / 2.0
    radius = (UPPER - LOWER) / 2.0
    spread_ratio = center / radius
    weight_now = 1.0 / spread_ratio
    carry_terms, push_terms = ([], [])
    for _ in range(count):
        weight_next = 1.0 / (2.0 * spread_ratio - weight_now)
        carry_terms.append(weight_next * weight_now)
        push_terms.append(2.0 * weight_next / radius)
        weight_now = weight_next
    return (carry_terms, push_terms, center)


def material(region, cond):
    return jnp.where(
        region == 0,
        cond[0],
        jnp.where(region == 1, cond[1], jnp.where(region == 2, cond[2], 0.0)),
    )


def pack_kernel(cond, forcing, start, latest, region, out):
    steps, comps, planes, ny, _ = forcing.shape
    rows = out.shape[0] // (planes * ny)
    is_first = (lax.axis_index("yh") == 0) & (lax.axis_index("z") == 0)
    for p in range(planes):
        sigma = material(region[p], cond)
        base = p * ny * rows
        for c in range(comps):
            head = forcing[0, c, p]
            head = head + jnp.where(is_first, sigma * start[c, p], 0.0)
            out[pl.ds(base + c * steps, ny, stride=rows), :] = head
            for b in range(1, steps):
                out[pl.ds(base + c * steps + b, ny, stride=rows), :] = forcing[b, c, p]
            out[pl.ds(base + comps * steps + c, ny, stride=rows), :] = -ALPHA * (
                sigma * latest[0, c, p]
            )
        for pad in range(comps * steps + comps, rows):
            out[pl.ds(base + pad, ny, stride=rows), :] = jnp.zeros_like(sigma)


def forward_kernel(cond, got, table, region, out):
    groups, _, nz = got.shape
    window = table.shape[0]
    steps = window // groups
    comps = 3
    half = window // 2
    head = lax.broadcasted_iota(jnp.int32, (window, nz), 0) == 0
    parts = []
    for c in range(comps):
        part = got[:, c * steps : (c + 1) * steps, :].reshape(window, nz)
        row = got[groups - 1, comps * steps + c : comps * steps + c + 1, :]
        parts.append(part + jnp.where(head, row, 0.0))
    spectrum = jnp.dot(
        table[...],
        jnp.concatenate(parts, axis=1),
        precision=lax.Precision.HIGHEST,
        preferred_element_type=jnp.float32,
    )
    width = comps * nz
    out[:, :width] = spectrum[:half]
    out[:, width : 2 * width] = spectrum[half:]
    line = region[lax.axis_index("yh"), pl.ds(lax.axis_index("z"), 1), :]
    out[:, 2 * width :] = jnp.broadcast_to(material(line, cond), (half, nz))


def inverse_kernel(got, table, out):
    half, wide = got.shape
    groups, rows, nz = out.shape
    steps = table.shape[0] // groups
    width = wide // 2
    dot = functools.partial(
        jnp.dot, precision=lax.Precision.HIGHEST, preferred_element_type=jnp.float32
    )
    result = dot(table[:, :half], got[:, :width]) + dot(table[:, half:], got[:, width:])
    for c in range(rows // steps):
        out[:, c * steps : (c + 1) * steps, :] = result[:, c * nz : (c + 1) * nz].reshape(
            groups, steps, nz
        )


def unpack_kernel(got, out):
    steps, comps, planes, ny, _ = out.shape
    rows = got.shape[0] // (planes * ny)
    for p in range(planes):
        for c in range(comps):
            for b in range(steps):
                out[b, c, p] = got[pl.ds(p * ny * rows + c * steps + b, ny, stride=rows), :]


def solve_kernel(terms, weights, own, far, left, right, out, field, first, resid, total, sigma):
    ny, nz = field.shape[2:]
    x_at = lax.axis_index("x")
    pair = lax.axis_index(PAIRS)
    p_plus, p_minus = terms[0, pair], terms[1, pair]
    q_term, inv_scale = terms[2, pair], terms[3, pair]
    _, _, center = chebyshev_terms(SWEEPS - 1)

    row = lax.broadcasted_iota(jnp.int32, (ny, nz), 0)
    lane = lax.broadcasted_iota(jnp.int32, (ny, nz), 1)
    row_first, row_last = row == 0, row == ny - 1
    lane_first, lane_last = lane == 0, lane == nz - 1
    blank = jnp.zeros((ny, nz), jnp.float32)

    def ahead_y(f):
        return jnp.where(row_last, 0.0, pltpu.roll(f, ny - 1, 0))

    def ahead_z(f):
        return jnp.where(lane_last, 0.0, pltpu.roll(f, nz - 1, 1))

    def behind_y(f):
        return jnp.where(row_first, 0.0, pltpu.roll(f, 1, 0))

    def behind_z(f):
        return jnp.where(lane_first, 0.0, pltpu.roll(f, 1, 1))

    def curls(now, after):
        flux = []
        for f in (0, 3):
            ex, ey, ez = now[f : f + 3]
            _, ey_after, ez_after = after[f : f + 3]
            flux += [
                (ahead_y(ez) - ez) - (ahead_z(ey) - ey),
                (ahead_z(ex) - ex) - (ez_after - ez),
                (ey_after - ey) - (ahead_y(ex) - ex),
            ]
        return flux

    def tails(now, after):
        flux = []
        for f in (0, 3):
            ex, ey, ez = now[f : f + 3]
            _, ey_after, ez_after = after[f : f + 3]
            flux += [
                (ahead_z(ex) - ex) - (ez_after - ez),
                (ey_after - ey) - (ahead_y(ex) - ex),
            ]
        return flux

    def adjoints(flux, before):
        field = []
        for f, g in ((0, 0), (3, 2)):
            bx, by, bz = flux[f : f + 3]
            by_before, bz_before = before[g : g + 2]
            field += [
                (behind_z(by) - by) - (behind_y(bz) - bz),
                (bz_before - bz) - (behind_z(bx) - bx),
                (behind_y(bx) - bx) - (by_before - by),
            ]
        return field

    def add_couple(field, values, weight, sign):
        sp, sm, sq = weight * p_plus, weight * p_minus, weight * (sign * q_term)
        return [
            field[c] + (sp * values[c] - sq * values[3 + c]) for c in range(3)
        ] + [field[3 + c] + (sm * values[3 + c] + sq * values[c]) for c in range(3)]

    def load(ref, at):
        return [ref[at + GUARD, k] for k in range(6)]

    def store(ref, at, values):
        for k in range(6):
            ref[at + GUARD, k] = values[k]

    blocks = lax.axis_size("x")
    width = 2 * REACH + BLOCK
    grid_low = REACH - BLOCK * x_at
    grid_high = grid_low + BLOCK * blocks
    top = jnp.minimum(grid_high, width)

    def fill(source, begin, count):
        for i in range(count):
            line = slice(i * ny, (i + 1) * ny)
            store(first, begin + i, [source[line, k * nz : (k + 1) * nz] for k in range(6)])
            sigma[begin + i + GUARD] = source[line, 6 * nz :]

    extra = far.shape[0] // ny
    low_far, high_far = REACH - BLOCK - extra, REACH + 2 * BLOCK
    for at in [*range(-1, low_far + extra), *range(high_far, width + 1)]:
        store(first, at, [blank] * 6)
    fill(left, REACH - BLOCK, BLOCK)
    fill(own, REACH, BLOCK)
    fill(right, REACH + BLOCK, BLOCK)
    fill(far, jnp.where(x_at < blocks // 2, high_far, low_far), extra)
    store(field, top, [blank] * 6)
    store(field, -1, [blank] * 6)

    def bounds(margin):
        low = jnp.maximum(grid_low, REACH - margin)
        high = jnp.minimum(grid_high, REACH + BLOCK + margin)
        length = (high - low + CHUNK - 1) // CHUNK * CHUNK
        high = jnp.minimum(top, low + length)
        return high - length, length

    def run(margin, source, sign, finish):
        low, length = bounds(margin)

        def some(begin, planes):
            now = load(source, begin)
            before = tails(load(source, begin - 1), now)
            before = [jnp.where(begin > grid_low, v, 0.0) for v in before]
            for u in range(planes):
                i = begin + u
                after = load(source, i + 1)
                flux = curls(now, after)
                value = adjoints(flux, before)
                finish(i, add_couple(value, now, sigma[i + GUARD], sign))
                now, before = after, [flux[1], flux[2], flux[4], flux[5]]

        many = length // LONG

        def step(t, _):
            some(low + t * LONG, LONG)
            return 0

        lax.fori_loop(0, many, step, 0)
        for planes in SHORT:

            @pl.when((length - many * LONG) == planes)
            def _():
                some(low + many * LONG, planes)

    def begin_with(i, value):
        store(resid, i, value)
        store(field, i, [v * (inv_scale * (1.0 / center)) for v in value])

    run(2 * (SWEEPS - 1), first, -1.0, begin_with)

    def clear(t, _):
        for u in range(CHUNK):
            for k in range(6):
                total[t * CHUNK + u, k] = blank
        return 0

    lax.fori_loop(0, BLOCK // CHUNK, clear, 0)

    def sweep(s, _):
        margin = 2 * (SWEEPS - 2 - s)
        carry_term, push_term = weights[0, s], weights[1, s] * inv_scale

        def add_total(t, _):
            for u in range(CHUNK):
                i = t * CHUNK + u
                for k in range(6):
                    total[i, k] = total[i, k] + field[i + REACH + GUARD, k]
            return 0

        lax.fori_loop(0, BLOCK // CHUNK, add_total, 0)

        def keep_first(i, value):
            store(first, i, value)

        def update(i, value):
            rest = [r - v for r, v in zip(load(resid, i), value)]
            store(resid, i, rest)
            store(
                field,
                i,
                [carry_term * d + push_term * r for d, r in zip(load(field, i), rest)],
            )

        run(margin + 1, field, 1.0, keep_first)
        run(margin, first, -1.0, update)
        return 0

    lax.fori_loop(0, SWEEPS - 1, sweep, 0)

    def write(t, _):
        for u in range(CHUNK):
            i = t * CHUNK + u
            line = pl.ds(pl.multiple_of(i * ny, ny), ny)
            for k in range(6):
                out[line, k * nz : (k + 1) * nz] = total[i, k] + field[i + REACH + GUARD, k]
        return 0

    lax.fori_loop(0, BLOCK // CHUNK, write, 0)


def per_device(forcing, start_field, iterate, region, conductance):
    steps, comps, planes, ny, nz = forcing.shape
    groups = lax.axis_size(TM)
    window = steps * groups
    half = window // 2
    forward_table, inverse_table = tables(window)
    vmem = pl.BlockSpec(memory_space=pltpu.VMEM)
    smem = pl.BlockSpec(memory_space=pltpu.SMEM)
    f32 = jnp.float32
    params = pltpu.CompilerParams(vmem_limit_bytes=12 * 1024 * 1024)

    rows = comps * steps + 8
    whole = lambda shape: pl.BlockSpec(shape, lambda i: (0,) * len(shape))
    packed = pl.pallas_call(
        pack_kernel,
        out_shape=jax.ShapeDtypeStruct((groups * rows, nz), f32),
        grid=(1,),
        in_specs=[
            smem,
            whole(forcing.shape),
            whole(start_field.shape),
            pl.BlockSpec((1, comps, planes, ny, nz), lambda i: (steps - 1, 0, 0, 0, 0)),
            whole(region.shape),
        ],
        out_specs=whole((groups * rows, nz)),
        compiler_params=pltpu.CompilerParams(vmem_limit_bytes=60 * 1024 * 1024),
        name="pack",
    )(conductance, forcing, start_field, iterate, region)

    got = lax.all_to_all(packed.reshape(groups, rows, nz), TM, 0, 0, tiled=True)

    spectrum = pl.pallas_call(
        forward_kernel,
        out_shape=jax.ShapeDtypeStruct((half, (2 * comps + 1) * nz), f32),
        in_specs=[smem, vmem, vmem, vmem],
        out_specs=vmem,
        compiler_params=params,
        name="forward",
    )(conductance, got, jnp.asarray(forward_table), region)

    own = lax.all_to_all(spectrum, PAIRS, 0, 0, tiled=True)

    count = lax.axis_size("x")
    x_at = lax.axis_index("x")
    extra = (2 * SWEEPS - 1 - BLOCK) * ny
    part = lax.dynamic_slice_in_dim(
        own, jnp.where(x_at < count // 2, half - extra, 0), extra, 0
    )
    own, part = lax.optimization_barrier((own, part))
    far = lax.ppermute(part, "x", [(i, (i + 2) % count) for i in range(count)])
    left = lax.ppermute(own, "x", [(i, i + 1) for i in range(count - 1)])
    right = lax.ppermute(own, "x", [(i + 1, i) for i in range(count - 1)])

    places = 2 * REACH + BLOCK + 2 * GUARD
    solved = pl.pallas_call(
        solve_kernel,
        out_shape=jax.ShapeDtypeStruct((half, 2 * comps * nz), f32),
        in_specs=[smem, smem, vmem, vmem, vmem, vmem],
        out_specs=vmem,
        scratch_shapes=[
            pltpu.VMEM((places, 6, ny, nz), f32),
            pltpu.VMEM((places, 6, ny, nz), f32),
            pltpu.VMEM((places, 6, ny, nz), f32),
            pltpu.VMEM((BLOCK, 6, ny, nz), f32),
            pltpu.VMEM((places, ny, nz), f32),
        ],
        compiler_params=params,
        name="solve",
    )(
        jnp.asarray(pair_table(window)),
        jnp.asarray(np.array(chebyshev_terms(SWEEPS - 1)[:2], np.float32)),
        own,
        far,
        left,
        right,
    )

    back = lax.all_to_all(solved, PAIRS, 0, 0, tiled=True)

    pencil = pl.pallas_call(
        inverse_kernel,
        out_shape=jax.ShapeDtypeStruct((groups, comps * steps, nz), f32),
        in_specs=[vmem, vmem],
        out_specs=vmem,
        compiler_params=params,
        name="inverse",
    )(back, jnp.asarray(inverse_table))

    home = lax.all_to_all(pencil, TM, 0, 0, tiled=True)

    return pl.pallas_call(
        unpack_kernel,
        out_shape=jax.ShapeDtypeStruct(forcing.shape, f32),
        in_specs=[vmem],
        out_specs=vmem,
        compiler_params=params,
        name="unpack",
    )(home.reshape(groups * comps * steps, nz))


def solution(mesh):
    fine = Mesh(mesh.devices.reshape(2, 8, 4, 4, 2), ("yh", "z", "x", "yl", "c"))
    space = ("x", "yl", "c")
    placed = (
        P(TM, None, space, None, None),
        P(None, space, None, None),
        P(TM, None, space, None, None),
        P(space, None, None),
        P(),
    )
    return jax.shard_map(
        per_device,
        mesh=fine,
        in_specs=placed,
        out_specs=P(TM, None, space, None, None),
        check_vma=False,
    )
```

```python
import functools
import math

import jax
import jax.numpy as jnp
import numpy as np
from jax import lax
from jax.experimental import pallas as pl
from jax.experimental.pallas import tpu as pltpu
from jax.sharding import Mesh
from jax.sharding import PartitionSpec as P

SWEEPS = 12
ALPHA = 0.1
LOWER = 0.02
UPPER = 1.0
SIGMA_TOP = 4.0
CURL_TOP = 12.0

TM = ("yh", "z")
GROUP = ("xl", "yl", "yh", "z")
HALF = 32
REACH = 24
STRIPE = 2
GUARD = 1
CHUNK = 14


def pair_rows(count):
    flip = lax.axis_index("xh")
    size = count // 2
    return tuple(
        pl.ds(pl.multiple_of(at * size, size), size) for at in (flip, 1 - flip)
    )


def pair_index():
    half_at, low_at, *rest = (lax.axis_index(name) for name in ("xh",) + GROUP)
    index = (half_at + low_at) % 2
    for name, at in zip(GROUP[1:], rest):
        index = index * lax.axis_size(name) + at
    return index


def tables(window):
    gamma = ALPHA ** (1.0 / window)
    half = window // 2
    pairs = np.arange(half)
    freqs = np.concatenate([pairs, np.where(pairs == 0, half, window - pairs)])
    moments = np.arange(window)
    angle = 2.0 * math.pi * (freqs[:, None] * moments[None, :] % window) / window
    cas = np.cos(angle) + np.sin(angle)
    forward = cas * gamma ** moments[None, :]
    inverse = cas.T * gamma ** (-moments[:, None]) / window
    return forward.astype(np.float32), inverse.astype(np.float32)


def pair_table(window):
    gamma = ALPHA ** (1.0 / window)
    pairs = np.arange(window // 2)
    theta = 2.0 * math.pi * pairs / window
    plain = 1.0 - gamma * np.cos(theta)
    p_plus = np.where(pairs == 0, 1.0 - gamma, plain)
    p_minus = np.where(pairs == 0, 1.0 + gamma, plain)
    q_term = np.where(pairs == 0, 0.0, gamma * np.sin(theta))
    bound = np.sqrt(np.maximum(p_plus, p_minus) ** 2 + q_term**2) * SIGMA_TOP + CURL_TOP
    return np.stack([p_plus, p_minus, q_term, 1.0 / bound**2]).astype(np.float32)


def chebyshev_terms(count):
    center = (UPPER + LOWER) / 2.0
    radius = (UPPER - LOWER) / 2.0
    spread_ratio = center / radius
    weight_now = 1.0 / spread_ratio
    carry_terms, push_terms = ([], [])
    for _ in range(count):
        weight_next = 1.0 / (2.0 * spread_ratio - weight_now)
        carry_terms.append(weight_next * weight_now)
        push_terms.append(2.0 * weight_next / radius)
        weight_now = weight_next
    return (carry_terms, push_terms, center)


def material(region, cond):
    return jnp.where(
        region == 0,
        cond[0],
        jnp.where(region == 1, cond[1], jnp.where(region == 2, cond[2], 0.0)),
    )


def pack_kernel(cond, forcing, start, latest, region, out):
    steps, comps, planes, ny, _ = forcing.shape
    rows = out.shape[0] // (planes * ny)
    is_first = (lax.axis_index("yh") == 0) & (lax.axis_index("z") == 0)
    for p in range(planes):
        sigma = material(region[p], cond)
        base = p * ny * rows
        for c in range(comps):
            head = forcing[0, c, p]
            head = head + jnp.where(is_first, sigma * start[c, p], 0.0)
            out[pl.ds(base + c * steps, ny, stride=rows), :] = head
            for b in range(1, steps):
                out[pl.ds(base + c * steps + b, ny, stride=rows), :] = forcing[b, c, p]
            out[pl.ds(base + comps * steps + c, ny, stride=rows), :] = -ALPHA * (
                sigma * latest[0, c, p]
            )
        for pad in range(comps * steps + comps, rows):
            out[pl.ds(base + pad, ny, stride=rows), :] = jnp.zeros_like(sigma)


def forward_kernel(cond, got, table, region, out):
    groups, _, nz = got.shape
    window = table.shape[0]
    steps = window // groups
    comps = 3
    half = window // 2
    head = lax.broadcasted_iota(jnp.int32, (window, nz), 0) == 0
    parts = []
    for c in range(comps):
        part = got[:, c * steps : (c + 1) * steps, :].reshape(window, nz)
        row = got[groups - 1, comps * steps + c : comps * steps + c + 1, :]
        parts.append(part + jnp.where(head, row, 0.0))
    spectrum = jnp.dot(
        table[...],
        jnp.concatenate(parts, axis=1),
        precision=lax.Precision.HIGHEST,
        preferred_element_type=jnp.float32,
    )
    width = comps * nz
    for at, rows in enumerate(pair_rows(half)):
        lines = slice(at * (half // 2), (at + 1) * (half // 2))
        out[rows, :width] = spectrum[:half][lines]
        out[rows, width : 2 * width] = spectrum[half:][lines]
    line = region[lax.axis_index("yh"), pl.ds(lax.axis_index("z"), 1), :]
    out[:, 2 * width :] = jnp.broadcast_to(material(line, cond), (half, nz))


def inverse_kernel(got, table, out):
    half, wide = got.shape
    groups, rows, nz = out.shape
    steps = table.shape[0] // groups
    width = wide // 2
    dot = functools.partial(
        jnp.dot, precision=lax.Precision.HIGHEST, preferred_element_type=jnp.float32
    )
    solved = jnp.concatenate([got[rows, :] for rows in pair_rows(half)], axis=0)
    result = dot(table[:, :half], solved[:, :width]) + dot(table[:, half:], solved[:, width:])
    for c in range(rows // steps):
        out[:, c * steps : (c + 1) * steps, :] = result[:, c * nz : (c + 1) * nz].reshape(
            groups, steps, nz
        )


def unpack_kernel(got, out):
    steps, comps, planes, ny, _ = out.shape
    rows = got.shape[0] // (planes * ny)
    for p in range(planes):
        for c in range(comps):
            for b in range(steps):
                out[b, c, p] = got[pl.ds(p * ny * rows + c * steps + b, ny, stride=rows), :]


def solve_kernel(terms, weights, mine, mate, part, part_mate, out, field, first, resid, total, sigma, flux_a, flux_b):
    ny, nz = field.shape[2:]
    half_at = lax.axis_index("xh")
    core_at = lax.axis_index("c")
    pair = pair_index()
    p_plus, p_minus = terms[0, pair], terms[1, pair]
    q_term, inv_scale = terms[2, pair], terms[3, pair]
    _, _, center = chebyshev_terms(SWEEPS - 1)

    row = lax.broadcasted_iota(jnp.int32, (ny, nz), 0)
    lane = lax.broadcasted_iota(jnp.int32, (ny, nz), 1)
    row_first, row_last = row == 0, row == ny - 1
    lane_first, lane_last = lane == 0, lane == nz - 1
    blank = jnp.zeros((ny, nz), jnp.float32)

    def ahead_y(f):
        return jnp.where(row_last, 0.0, pltpu.roll(f, ny - 1, 0))

    def ahead_z(f):
        return jnp.where(lane_last, 0.0, pltpu.roll(f, nz - 1, 1))

    def behind_y(f):
        return jnp.where(row_first, 0.0, pltpu.roll(f, 1, 0))

    def behind_z(f):
        return jnp.where(lane_first, 0.0, pltpu.roll(f, 1, 1))

    def curls(now, after):
        flux = []
        for f in (0, 3):
            ex, ey, ez = now[f : f + 3]
            _, ey_after, ez_after = after[f : f + 3]
            flux += [
                (ahead_y(ez) - ez) - (ahead_z(ey) - ey),
                (ahead_z(ex) - ex) - (ez_after - ez),
                (ey_after - ey) - (ahead_y(ex) - ex),
            ]
        return flux

    def tails(now, after):
        flux = []
        for f in (0, 3):
            ex, ey, ez = now[f : f + 3]
            _, ey_after, ez_after = after[f : f + 3]
            flux += [
                (ahead_z(ex) - ex) - (ez_after - ez),
                (ey_after - ey) - (ahead_y(ex) - ex),
            ]
        return flux

    def adjoints(flux, before):
        field = []
        for f, g in ((0, 0), (3, 2)):
            bx, by, bz = flux[f : f + 3]
            by_before, bz_before = before[g : g + 2]
            field += [
                (behind_z(by) - by) - (behind_y(bz) - bz),
                (bz_before - bz) - (behind_z(bx) - bx),
                (behind_y(bx) - bx) - (by_before - by),
            ]
        return field

    def add_couple(field, values, weight, sign):
        sp, sm, sq = weight * p_plus, weight * p_minus, weight * (sign * q_term)
        return [
            field[c] + (sp * values[c] - sq * values[3 + c]) for c in range(3)
        ] + [field[3 + c] + (sm * values[3 + c] + sq * values[c]) for c in range(3)]

    def load(ref, at):
        return [ref[at + GUARD, k] for k in range(6)]

    def store(ref, at, values):
        for k in range(6):
            ref[at + GUARD, k] = values[k]

    own_low = REACH * half_at
    halo_low = HALF * (1 - half_at)
    grid_low = -(HALF - REACH) * half_at
    grid_high = grid_low + 2 * HALF
    width = HALF + REACH

    def fill(source, begin):
        for at in range(source.shape[0] // ny):
            i = begin + (at // STRIPE) * (2 * STRIPE) + at % STRIPE
            line = slice(at * ny, (at + 1) * ny)
            store(first, i, [source[line, k * nz : (k + 1) * nz] for k in range(6)])
            sigma[i + GUARD] = source[line, 6 * nz :]

    for ref in (first, field):
        store(ref, -1, [blank] * 6)
        store(ref, width, [blank] * 6)
    mine_at, mate_at = STRIPE * core_at, STRIPE * (1 - core_at)
    fill(mine, own_low + mine_at)
    fill(mate, own_low + mate_at)
    fill(part, halo_low + mine_at)
    fill(part_mate, halo_low + mate_at)

    def bounds(margin):
        low = jnp.maximum(grid_low, own_low - margin)
        high = jnp.minimum(grid_high, own_low + HALF + margin)
        length = (high - low + CHUNK - 1) // CHUNK * CHUNK
        high = jnp.minimum(width, low + length)
        return high - length, length // CHUNK

    def lift(flux, source, begin):
        now = load(source, begin)
        before = tails(load(source, begin - 1), now)
        for k, v in zip((1, 2, 4, 5), before):
            flux[0, k] = jnp.where(begin > grid_low, v, 0.0)
        for u in range(CHUNK):
            after = load(source, begin + u + 1)
            for k, v in enumerate(curls(now, after)):
                flux[u + 1, k] = v
            now = after

    def drop(flux, source, begin, sign, finish):
        before = [flux[0, k] for k in (1, 2, 4, 5)]
        for u in range(CHUNK):
            i = begin + u
            now = [flux[u + 1, k] for k in range(6)]
            value = adjoints(now, before)
            finish(i, add_couple(value, load(source, i), sigma[i + GUARD], sign))
            before = [now[k] for k in (1, 2, 4, 5)]

    def run(margin, flux, source, sign, finish, other_margin, other_flux, other_source):
        low, count = bounds(margin)

        def step(t, _):
            begin = low + t * CHUNK
            drop(flux, source, begin, sign, finish)
            lift(flux, source, begin + CHUNK)
            return 0

        lax.fori_loop(0, count - 1, step, 0)
        lift(other_flux, other_source, bounds(other_margin)[0])
        drop(flux, source, low + (count - 1) * CHUNK, sign, finish)

    def begin_with(i, value):
        store(resid, i, value)
        store(field, i, [v * (inv_scale * (1.0 / center)) for v in value])

    reach = 2 * (SWEEPS - 1)
    lift(flux_b, first, bounds(reach)[0])
    run(reach, flux_b, first, -1.0, begin_with, reach - 1, flux_a, field)

    own_planes = [(at // STRIPE) * (2 * STRIPE) + at % STRIPE for at in range(HALF // 2)]
    own_begin = own_low + mine_at

    def sweep(s, _):
        margin = reach - 2 - 2 * s
        carry_term, push_term = weights[0, s], weights[1, s] * inv_scale

        for at, h in enumerate(own_planes):
            for k in range(6):
                step = field[own_begin + h + GUARD, k]
                total[at, k] = jnp.where(s == 0, step, total[at, k] + step)

        def keep_first(i, value):
            store(first, i, value)

        def update(i, value):
            rest = [r - v for r, v in zip(load(resid, i), value)]
            store(resid, i, rest)
            store(
                field,
                i,
                [carry_term * d + push_term * r for d, r in zip(load(field, i), rest)],
            )

        run(margin + 1, flux_a, field, 1.0, keep_first, margin, flux_b, first)
        run(margin, flux_b, first, -1.0, update, jnp.maximum(margin - 1, 0), flux_a, field)
        return 0

    lax.fori_loop(0, SWEEPS - 1, sweep, 0)

    for at, h in enumerate(own_planes):
        for k in range(6):
            out[at * ny : (at + 1) * ny, k * nz : (k + 1) * nz] = (
                total[at, k] + field[own_begin + h + GUARD, k]
            )


def per_device(forcing, start_field, iterate, region, conductance):
    steps, comps, planes, ny, nz = forcing.shape
    groups = lax.axis_size(TM)
    window = steps * groups
    half = window // 2
    forward_table, inverse_table = tables(window)
    vmem = pl.BlockSpec(memory_space=pltpu.VMEM)
    smem = pl.BlockSpec(memory_space=pltpu.SMEM)
    f32 = jnp.float32
    params = pltpu.CompilerParams(vmem_limit_bytes=12 * 1024 * 1024)

    rows = comps * steps + 8
    whole = lambda shape: pl.BlockSpec(shape, lambda i: (0,) * len(shape))
    packed = pl.pallas_call(
        pack_kernel,
        out_shape=jax.ShapeDtypeStruct((groups * rows, nz), f32),
        grid=(1,),
        in_specs=[
            smem,
            whole(forcing.shape),
            whole(start_field.shape),
            pl.BlockSpec((1, comps, planes, ny, nz), lambda i: (steps - 1, 0, 0, 0, 0)),
            whole(region.shape),
        ],
        out_specs=whole((groups * rows, nz)),
        compiler_params=pltpu.CompilerParams(vmem_limit_bytes=60 * 1024 * 1024),
        name="pack",
    )(conductance, forcing, start_field, iterate, region)

    got = lax.all_to_all(packed.reshape(groups, rows, nz), TM, 0, 0, tiled=True)

    spectrum = pl.pallas_call(
        forward_kernel,
        out_shape=jax.ShapeDtypeStruct((half, (2 * comps + 1) * nz), f32),
        in_specs=[smem, vmem, vmem, vmem],
        out_specs=vmem,
        compiler_params=params,
        name="forward",
    )(conductance, got, jnp.asarray(forward_table), region)

    mine = lax.all_to_all(spectrum, GROUP, 0, 0, tiled=True)

    rows_sent = half * REACH // HALF
    part = lax.dynamic_slice_in_dim(
        mine, (1 - lax.axis_index("xh")) * (half - rows_sent), rows_sent, 0
    )
    blocks = lax.axis_size(("xh", "xl"))
    part = lax.ppermute(part, ("xh", "xl"), [(i, blocks - 1 - i) for i in range(blocks)])
    mate = lax.ppermute(mine, "c", [(0, 1), (1, 0)])
    part_mate = lax.ppermute(part, "c", [(0, 1), (1, 0)])

    places = HALF + REACH + 2 * GUARD
    window_shape = pltpu.VMEM((places, 2 * comps, ny, nz), f32)
    flux_shape = pltpu.VMEM((CHUNK + 1, 2 * comps, ny, nz), f32)
    solved = pl.pallas_call(
        solve_kernel,
        out_shape=jax.ShapeDtypeStruct((half, 2 * comps * nz), f32),
        in_specs=[smem, smem, vmem, vmem, vmem, vmem],
        out_specs=vmem,
        scratch_shapes=[
            window_shape,
            window_shape,
            window_shape,
            pltpu.VMEM((HALF // 2, 2 * comps, ny, nz), f32),
            pltpu.VMEM((places, ny, nz), f32),
            flux_shape,
            flux_shape,
        ],
        compiler_params=params,
        name="solve",
    )(
        jnp.asarray(pair_table(window)),
        jnp.asarray(np.array(chebyshev_terms(SWEEPS - 1)[:2], np.float32)),
        mine,
        mate,
        part,
        part_mate,
    )

    back = lax.all_to_all(solved, GROUP, 0, 0, tiled=True)

    pencil = pl.pallas_call(
        inverse_kernel,
        out_shape=jax.ShapeDtypeStruct((groups, comps * steps, nz), f32),
        in_specs=[vmem, vmem],
        out_specs=vmem,
        compiler_params=params,
        name="inverse",
    )(back, jnp.asarray(inverse_table))

    home = lax.all_to_all(pencil, TM, 0, 0, tiled=True)

    return pl.pallas_call(
        unpack_kernel,
        out_shape=jax.ShapeDtypeStruct(forcing.shape, f32),
        in_specs=[vmem],
        out_specs=vmem,
        compiler_params=params,
        name="unpack",
    )(home.reshape(groups * comps * steps, nz))


def solution(mesh):
    names = ("yh", "z", "xh", "xl", "yl", "c")
    fine = Mesh(mesh.devices.reshape(2, 8, 2, 2, 4, 2), names)
    space = ("xh", "xl", "yl", "c")
    placed = (
        P(TM, None, space, None, None),
        P(None, space, None, None),
        P(TM, None, space, None, None),
        P(space, None, None),
        P(),
    )
    return jax.shard_map(
        per_device,
        mesh=fine,
        in_specs=placed,
        out_specs=P(TM, None, space, None, None),
        check_vma=False,
    )
```

```python
import functools
import math

import jax
import jax.numpy as jnp
import numpy as np
from jax import lax
from jax.experimental import pallas as pl
from jax.experimental.pallas import tpu as pltpu
from jax.sharding import Mesh
from jax.sharding import PartitionSpec as P

SWEEPS = 12
ALPHA = 0.1
LOWER = 0.02
UPPER = 1.0
SIGMA_TOP = 4.0
CURL_TOP = 12.0

TM = ("yh", "z")
GROUP = ("xl", "yl", "yh", "z")
HALF = 32
REACH = 24
STRIPE = 2
GUARD = 1
CHUNK = 14


def pair_index():
    half_at, low_at, *rest = (lax.axis_index(name) for name in ("xh",) + GROUP)
    index = (half_at + low_at) % 2
    for name, at in zip(GROUP[1:], rest):
        index = index * lax.axis_size(name) + at
    return index


def tables(window):
    gamma = ALPHA ** (1.0 / window)
    half = window // 2
    pairs = np.arange(half)
    freqs = np.concatenate([pairs, np.where(pairs == 0, half, window - pairs)])
    moments = np.arange(window)
    angle = 2.0 * math.pi * (freqs[:, None] * moments[None, :] % window) / window
    cas = np.cos(angle) + np.sin(angle)
    forward = cas * gamma ** moments[None, :]
    inverse = cas.T * gamma ** (-moments[:, None]) / window
    return forward.astype(np.float32), inverse.astype(np.float32)


def pair_table(window):
    gamma = ALPHA ** (1.0 / window)
    pairs = np.arange(window // 2)
    theta = 2.0 * math.pi * pairs / window
    plain = 1.0 - gamma * np.cos(theta)
    p_plus = np.where(pairs == 0, 1.0 - gamma, plain)
    p_minus = np.where(pairs == 0, 1.0 + gamma, plain)
    q_term = np.where(pairs == 0, 0.0, gamma * np.sin(theta))
    bound = np.sqrt(np.maximum(p_plus, p_minus) ** 2 + q_term**2) * SIGMA_TOP + CURL_TOP
    return np.stack([p_plus, p_minus, q_term, 1.0 / bound**2]).astype(np.float32)


def chebyshev_terms(count):
    center = (UPPER + LOWER) / 2.0
    radius = (UPPER - LOWER) / 2.0
    spread_ratio = center / radius
    weight_now = 1.0 / spread_ratio
    carry_terms, push_terms = ([], [])
    for _ in range(count):
        weight_next = 1.0 / (2.0 * spread_ratio - weight_now)
        carry_terms.append(weight_next * weight_now)
        push_terms.append(2.0 * weight_next / radius)
        weight_now = weight_next
    return (carry_terms, push_terms, center)


def material(region, cond):
    return jnp.where(
        region == 0,
        cond[0],
        jnp.where(region == 1, cond[1], jnp.where(region == 2, cond[2], 0.0)),
    )


def pack_kernel(cond, forcing, start, latest, region, out):
    steps, comps, _, ny, _ = forcing.shape
    rows = out.shape[0] // ny
    is_first = (lax.axis_index("yh") == 0) & (lax.axis_index("z") == 0)
    sigma = material(region[0], cond)
    for c in range(comps):
        head = forcing[0, c, 0]
        head = head + jnp.where(is_first, sigma * start[c, 0], 0.0)
        out[pl.ds(c * steps, ny, stride=rows), :] = head
        for b in range(1, steps):
            out[pl.ds(c * steps + b, ny, stride=rows), :] = forcing[b, c, 0]
        out[pl.ds(comps * steps + c, ny, stride=rows), :] = -ALPHA * (sigma * latest[0, c, 0])
    for pad in range(comps * steps + comps, rows):
        out[pl.ds(pad, ny, stride=rows), :] = jnp.zeros_like(sigma)


def forward_kernel(cond, got, tables, region, out):
    groups, _, nz = got.shape
    window = tables.shape[1]
    steps = window // groups
    comps = 3
    half = window // 2
    head = lax.broadcasted_iota(jnp.int32, (window, nz), 0) == 0
    parts = []
    for c in range(comps):
        part = got[:, c * steps : (c + 1) * steps, :].reshape(window, nz)
        row = got[groups - 1, comps * steps + c : comps * steps + c + 1, :]
        parts.append(part + jnp.where(head, row, 0.0))
    spectrum = jnp.dot(
        tables[0],
        jnp.concatenate(parts, axis=1),
        precision=lax.Precision.HIGHEST,
        preferred_element_type=jnp.float32,
    )
    width = comps * nz
    flip = lax.axis_index("xh")
    line = region[lax.axis_index("yh"), pl.ds(lax.axis_index("z"), 1), :]
    weight = jnp.broadcast_to(material(line, cond), (8, nz))
    cols = out.shape[0] // half
    for at in range(half // 8):
        lower = at < half // 16
        begin = at * 8 + (flip if lower else -flip) * (half // 2)
        for k in range(2 * comps):
            block = spectrum[
                k // comps * half + at * 8 : k // comps * half + at * 8 + 8,
                k % comps * nz : (k % comps + 1) * nz,
            ]
            out[pl.ds(begin * cols + k, 8, stride=cols), :] = block
        out[pl.ds(begin * cols + 2 * comps, 8, stride=cols), :] = weight


def inverse_kernel(got, tables, out):
    groups, rows, nz = out.shape
    _, window, _ = tables.shape
    half = window // 2
    steps = window // groups
    cols = got.shape[0] // half
    dot = functools.partial(
        jnp.dot, precision=lax.Precision.HIGHEST, preferred_element_type=jnp.float32
    )
    flip = lax.axis_index("xh")
    size = half // 2

    def member(f):
        return jnp.concatenate(
            [
                jnp.concatenate(
                    [got[pl.ds(at * size * cols + k, size, stride=cols), :] for at in (flip, 1 - flip)],
                    axis=0,
                )
                for k in range(f * cols // 2, (f + 1) * cols // 2)
            ],
            axis=1,
        )

    table = tables.at[1]
    result = dot(table[:, :half], member(0)) + dot(table[:, half:], member(1))
    for c in range(rows // steps):
        out[:, c * steps : (c + 1) * steps, :] = result[:, c * nz : (c + 1) * nz].reshape(
            groups, steps, nz
        )


def unpack_kernel(got, out):
    steps, comps, _, ny, _ = out.shape
    rows = got.shape[0] // ny
    for c in range(comps):
        for b in range(steps):
            out[b, c, 0] = got[pl.ds(c * steps + b, ny, stride=rows), :]


def solve_kernel(terms, weights, mine, mate, part, part_mate, out, field, first, resid, total, sigma, flux_a, flux_b):
    ny, nz = field.shape[2:]
    half_at = lax.axis_index("xh")
    core_at = lax.axis_index("c")
    pair = pair_index()
    p_plus, p_minus = terms[0, pair], terms[1, pair]
    q_term, inv_scale = terms[2, pair], terms[3, pair]
    _, _, center = chebyshev_terms(SWEEPS - 1)

    row = lax.broadcasted_iota(jnp.int32, (ny, nz), 0)
    lane = lax.broadcasted_iota(jnp.int32, (ny, nz), 1)
    row_first, row_last = row == 0, row == ny - 1
    lane_first, lane_last = lane == 0, lane == nz - 1
    blank = jnp.zeros((ny, nz), jnp.float32)

    def ahead_y(f):
        return jnp.where(row_last, 0.0, pltpu.roll(f, ny - 1, 0))

    def ahead_z(f):
        return jnp.where(lane_last, 0.0, pltpu.roll(f, nz - 1, 1))

    def behind_y(f):
        return jnp.where(row_first, 0.0, pltpu.roll(f, 1, 0))

    def behind_z(f):
        return jnp.where(lane_first, 0.0, pltpu.roll(f, 1, 1))

    def curls(now, after):
        flux = []
        for f in (0, 3):
            ex, ey, ez = now[f : f + 3]
            _, ey_after, ez_after = after[f : f + 3]
            flux += [
                (ahead_y(ez) - ez) - (ahead_z(ey) - ey),
                (ahead_z(ex) - ex) - (ez_after - ez),
                (ey_after - ey) - (ahead_y(ex) - ex),
            ]
        return flux

    def tails(now, after):
        flux = []
        for f in (0, 3):
            ex, ey, ez = now[f : f + 3]
            _, ey_after, ez_after = after[f : f + 3]
            flux += [
                (ahead_z(ex) - ex) - (ez_after - ez),
                (ey_after - ey) - (ahead_y(ex) - ex),
            ]
        return flux

    def adjoints(flux, before):
        field = []
        for f, g in ((0, 0), (3, 2)):
            bx, by, bz = flux[f : f + 3]
            by_before, bz_before = before[g : g + 2]
            field += [
                (behind_z(by) - by) - (behind_y(bz) - bz),
                (bz_before - bz) - (behind_z(bx) - bx),
                (behind_y(bx) - bx) - (by_before - by),
            ]
        return field

    def add_couple(field, values, weight, sign):
        sp, sm, sq = weight * p_plus, weight * p_minus, weight * (sign * q_term)
        return [
            field[c] + (sp * values[c] - sq * values[3 + c]) for c in range(3)
        ] + [field[3 + c] + (sm * values[3 + c] + sq * values[c]) for c in range(3)]

    def load(ref, at):
        return [ref[at + GUARD, k] for k in range(6)]

    def store(ref, at, values):
        for k in range(6):
            ref[at + GUARD, k] = values[k]

    own_low = REACH * half_at
    halo_low = HALF * (1 - half_at)
    grid_low = -(HALF - REACH) * half_at
    grid_high = grid_low + 2 * HALF
    width = HALF + REACH

    def fill(source, begin):
        for at in range(source.shape[0] // (7 * ny)):
            i = begin + (at // STRIPE) * (2 * STRIPE) + at % STRIPE
            parts = [source[pl.ds(at * 7 * ny + k, ny, stride=7), :] for k in range(7)]
            store(first, i, parts[:6])
            sigma[i + GUARD] = parts[6]

    for ref in (first, field):
        store(ref, -1, [blank] * 6)
        store(ref, width, [blank] * 6)
    mine_at, mate_at = STRIPE * core_at, STRIPE * (1 - core_at)
    fill(mine, own_low + mine_at)
    fill(mate, own_low + mate_at)
    fill(part, halo_low + mine_at)
    fill(part_mate, halo_low + mate_at)

    def bounds(margin):
        low = jnp.maximum(grid_low, own_low - margin)
        high = jnp.minimum(grid_high, own_low + HALF + margin)
        length = (high - low + CHUNK - 1) // CHUNK * CHUNK
        high = jnp.minimum(width, low + length)
        return high - length, length // CHUNK

    def lift(flux, source, begin):
        now = load(source, begin)
        before = tails(load(source, begin - 1), now)
        for k, v in zip((1, 2, 4, 5), before):
            flux[0, k] = jnp.where(begin > grid_low, v, 0.0)
        for u in range(CHUNK):
            after = load(source, begin + u + 1)
            for k, v in enumerate(curls(now, after)):
                flux[u + 1, k] = v
            now = after

    def drop(flux, source, begin, sign, finish):
        before = [flux[0, k] for k in (1, 2, 4, 5)]
        for u in range(CHUNK):
            i = begin + u
            now = [flux[u + 1, k] for k in range(6)]
            value = adjoints(now, before)
            finish(i, add_couple(value, load(source, i), sigma[i + GUARD], sign))
            before = [now[k] for k in (1, 2, 4, 5)]

    def run(margin, flux, source, sign, finish, other_margin, other_flux, other_source):
        low, count = bounds(margin)

        def step(t, _):
            begin = low + t * CHUNK
            drop(flux, source, begin, sign, finish)
            lift(flux, source, begin + CHUNK)
            return 0

        lax.fori_loop(0, count - 1, step, 0)
        lift(other_flux, other_source, bounds(other_margin)[0])
        drop(flux, source, low + (count - 1) * CHUNK, sign, finish)

    def begin_with(i, value):
        store(resid, i, value)
        store(field, i, [v * (inv_scale * (1.0 / center)) for v in value])

    reach = 2 * (SWEEPS - 1)
    lift(flux_b, first, bounds(reach)[0])
    run(reach, flux_b, first, -1.0, begin_with, reach - 1, flux_a, field)

    own_planes = [(at // STRIPE) * (2 * STRIPE) + at % STRIPE for at in range(HALF // 2)]
    own_begin = own_low + mine_at

    def sweep(s, _):
        margin = reach - 2 - 2 * s
        carry_term, push_term = weights[0, s], weights[1, s] * inv_scale

        for at, h in enumerate(own_planes):
            for k in range(6):
                step = field[own_begin + h + GUARD, k]
                total[at, k] = jnp.where(s == 0, step, total[at, k] + step)

        def keep_first(i, value):
            store(first, i, value)

        def update(i, value):
            rest = [r - v for r, v in zip(load(resid, i), value)]
            store(resid, i, rest)
            store(
                field,
                i,
                [carry_term * d + push_term * r for d, r in zip(load(field, i), rest)],
            )

        run(margin + 1, flux_a, field, 1.0, keep_first, margin, flux_b, first)
        run(margin, flux_b, first, -1.0, update, jnp.maximum(margin - 1, 0), flux_a, field)
        return 0

    lax.fori_loop(0, SWEEPS - 1, sweep, 0)

    for at, h in enumerate(own_planes):
        for k in range(6):
            out[pl.ds(at * 6 * ny + k, ny, stride=6), :] = (
                total[at, k] + field[own_begin + h + GUARD, k]
            )


def per_device(forcing, start_field, iterate, region, conductance):
    steps, comps, planes, ny, nz = forcing.shape
    groups = lax.axis_size(TM)
    window = steps * groups
    half = window // 2
    both = jnp.asarray(np.stack(tables(window)))
    vmem = pl.BlockSpec(memory_space=pltpu.VMEM)
    smem = pl.BlockSpec(memory_space=pltpu.SMEM)
    f32 = jnp.float32
    params = pltpu.CompilerParams(vmem_limit_bytes=12 * 1024 * 1024)

    rows = comps * steps + 8
    plane_of = pl.BlockSpec((steps, comps, 1, ny, nz), lambda p: (0, 0, p, 0, 0))
    packed = pl.pallas_call(
        pack_kernel,
        out_shape=jax.ShapeDtypeStruct((groups * rows, nz), f32),
        grid=(planes,),
        in_specs=[
            smem,
            plane_of,
            pl.BlockSpec((comps, 1, ny, nz), lambda p: (0, p, 0, 0)),
            pl.BlockSpec((1, comps, 1, ny, nz), lambda p: (steps - 1, 0, p, 0, 0)),
            pl.BlockSpec((1, ny, nz), lambda p: (p, 0, 0)),
        ],
        out_specs=pl.BlockSpec((ny * rows, nz), lambda p: (p, 0)),
        compiler_params=pltpu.CompilerParams(vmem_limit_bytes=60 * 1024 * 1024),
        name="pack",
    )(conductance, forcing, start_field, iterate, region)

    got = lax.all_to_all(packed.reshape(groups, rows, nz), TM, 0, 0, tiled=True)

    spectrum = pl.pallas_call(
        forward_kernel,
        out_shape=jax.ShapeDtypeStruct((half * (2 * comps + 1), nz), f32),
        in_specs=[smem, vmem, vmem, vmem],
        out_specs=vmem,
        compiler_params=params,
        name="forward",
    )(conductance, got, both, region)

    mine = lax.all_to_all(
        spectrum.reshape(half, 1, (2 * comps + 1) * nz), GROUP, 0, 0, tiled=True
    )

    rows_sent = half * REACH // HALF
    part = lax.dynamic_slice_in_dim(
        mine, (1 - lax.axis_index("xh")) * (half - rows_sent), rows_sent, 0
    ).reshape(rows_sent * (2 * comps + 1), nz)
    mine = mine.reshape(half * (2 * comps + 1), nz)
    blocks = lax.axis_size(("xh", "xl"))
    part = lax.ppermute(part, ("xh", "xl"), [(i, blocks - 1 - i) for i in range(blocks)])
    mate = lax.ppermute(mine, "c", [(0, 1), (1, 0)])
    part_mate = lax.ppermute(part, "c", [(0, 1), (1, 0)])

    places = HALF + REACH + 2 * GUARD
    window_shape = pltpu.VMEM((places, 2 * comps, ny, nz), f32)
    flux_shape = pltpu.VMEM((CHUNK + 1, 2 * comps, ny, nz), f32)
    solved = pl.pallas_call(
        solve_kernel,
        out_shape=jax.ShapeDtypeStruct((half * 2 * comps, nz), f32),
        in_specs=[smem, smem, vmem, vmem, vmem, vmem],
        out_specs=vmem,
        scratch_shapes=[
            window_shape,
            window_shape,
            window_shape,
            pltpu.VMEM((HALF // 2, 2 * comps, ny, nz), f32),
            pltpu.VMEM((places, ny, nz), f32),
            flux_shape,
            flux_shape,
        ],
        compiler_params=params,
        name="solve",
    )(
        jnp.asarray(pair_table(window)),
        jnp.asarray(np.array(chebyshev_terms(SWEEPS - 1)[:2], np.float32)),
        mine,
        mate,
        part,
        part_mate,
    )

    back = lax.all_to_all(
        solved.reshape(half, 1, 2 * comps * nz), GROUP, 0, 0, tiled=True
    ).reshape(half * 2 * comps, nz)

    pencil = pl.pallas_call(
        inverse_kernel,
        out_shape=jax.ShapeDtypeStruct((groups, comps * steps, nz), f32),
        in_specs=[vmem, vmem],
        out_specs=vmem,
        compiler_params=params,
        name="inverse",
    )(back, both)

    home = lax.all_to_all(pencil, TM, 0, 0, tiled=True)

    return pl.pallas_call(
        unpack_kernel,
        out_shape=jax.ShapeDtypeStruct(forcing.shape, f32),
        grid=(planes,),
        in_specs=[pl.BlockSpec((ny * comps * steps, nz), lambda p: (p, 0))],
        out_specs=plane_of,
        compiler_params=params,
        name="unpack",
    )(home.reshape(groups * comps * steps, nz))


def solution(mesh):
    names = ("yh", "z", "xh", "xl", "yl", "c")
    fine = Mesh(mesh.devices.reshape(2, 8, 2, 2, 4, 2), names)
    space = ("xh", "xl", "yl", "c")
    placed = (
        P(TM, None, space, None, None),
        P(None, space, None, None),
        P(TM, None, space, None, None),
        P(space, None, None),
        P(),
    )
    return jax.shard_map(
        per_device,
        mesh=fine,
        in_specs=placed,
        out_specs=P(TM, None, space, None, None),
        check_vma=False,
    )
```

```python
import functools
import math

import jax
import jax.numpy as jnp
import numpy as np
from jax import lax
from jax.experimental import pallas as pl
from jax.experimental.pallas import tpu as pltpu
from jax.sharding import Mesh
from jax.sharding import PartitionSpec as P

SWEEPS = 12
ALPHA = 0.1
LOWER = 0.02
UPPER = 1.0
SIGMA_TOP = 4.0
CURL_TOP = 12.0

TM = ("yh", "z")
GROUP = ("xl", "yl", "yh", "z")
HALF = 32
REACH = 24
STRIPE = 2
GUARD = 1
INNER = 8
OUTER = 12


def pair_index():
    half_at, low_at, *rest = (lax.axis_index(name) for name in ("xh",) + GROUP)
    index = (half_at + low_at) % 2
    for name, at in zip(GROUP[1:], rest):
        index = index * lax.axis_size(name) + at
    return index


def tables(window):
    gamma = ALPHA ** (1.0 / window)
    half = window // 2
    pairs = np.arange(half)
    freqs = np.concatenate([pairs, np.where(pairs == 0, half, window - pairs)])
    moments = np.arange(window)
    angle = 2.0 * math.pi * (freqs[:, None] * moments[None, :] % window) / window
    cas = np.cos(angle) + np.sin(angle)
    forward = cas * gamma ** moments[None, :]
    inverse = cas.T * gamma ** (-moments[:, None]) / window
    return forward.astype(np.float32), inverse.astype(np.float32)


def pair_table(window):
    gamma = ALPHA ** (1.0 / window)
    pairs = np.arange(window // 2)
    theta = 2.0 * math.pi * pairs / window
    plain = 1.0 - gamma * np.cos(theta)
    p_plus = np.where(pairs == 0, 1.0 - gamma, plain)
    p_minus = np.where(pairs == 0, 1.0 + gamma, plain)
    q_term = np.where(pairs == 0, 0.0, gamma * np.sin(theta))
    bound = np.sqrt(np.maximum(p_plus, p_minus) ** 2 + q_term**2) * SIGMA_TOP + CURL_TOP
    return np.stack([p_plus, p_minus, q_term, 1.0 / bound**2]).astype(np.float32)


def chebyshev_terms(count):
    center = (UPPER + LOWER) / 2.0
    radius = (UPPER - LOWER) / 2.0
    spread_ratio = center / radius
    weight_now = 1.0 / spread_ratio
    carry_terms, push_terms = ([], [])
    for _ in range(count):
        weight_next = 1.0 / (2.0 * spread_ratio - weight_now)
        carry_terms.append(weight_next * weight_now)
        push_terms.append(2.0 * weight_next / radius)
        weight_now = weight_next
    return (carry_terms, push_terms, center)


def material(region, cond):
    return jnp.where(
        region == 0,
        cond[0],
        jnp.where(region == 1, cond[1], jnp.where(region == 2, cond[2], 0.0)),
    )


def pack_kernel(cond, forcing, start, latest, region, out):
    steps, comps, _, ny, _ = forcing.shape
    rows = out.shape[0] // ny
    is_first = (lax.axis_index("yh") == 0) & (lax.axis_index("z") == 0)
    sigma = material(region[0], cond)
    for c in range(comps):
        head = forcing[0, c, 0]
        head = head + jnp.where(is_first, sigma * start[c, 0], 0.0)
        out[pl.ds(c * steps, ny, stride=rows), :] = head
        for b in range(1, steps):
            out[pl.ds(c * steps + b, ny, stride=rows), :] = forcing[b, c, 0]
        out[pl.ds(comps * steps + c, ny, stride=rows), :] = -ALPHA * (sigma * latest[0, c, 0])
    for pad in range(comps * steps + comps, rows):
        out[pl.ds(pad, ny, stride=rows), :] = jnp.zeros_like(sigma)


def forward_kernel(cond, got, tables, region, out):
    groups, _, nz = got.shape
    window = tables.shape[1]
    steps = window // groups
    comps = 3
    half = window // 2
    head = lax.broadcasted_iota(jnp.int32, (window, nz), 0) == 0
    parts = []
    for c in range(comps):
        part = got[:, c * steps : (c + 1) * steps, :].reshape(window, nz)
        row = got[groups - 1, comps * steps + c : comps * steps + c + 1, :]
        parts.append(part + jnp.where(head, row, 0.0))
    spectrum = jnp.dot(
        tables[0],
        jnp.concatenate(parts, axis=1),
        precision=lax.Precision.HIGHEST,
        preferred_element_type=jnp.float32,
    )
    width = comps * nz
    flip = lax.axis_index("xh")
    line = region[lax.axis_index("yh"), pl.ds(lax.axis_index("z"), 1), :]
    weight = jnp.broadcast_to(material(line, cond), (8, nz))
    cols = out.shape[0] // half
    for at in range(half // 8):
        lower = at < half // 16
        begin = at * 8 + (flip if lower else -flip) * (half // 2)
        for k in range(2 * comps):
            block = spectrum[
                k // comps * half + at * 8 : k // comps * half + at * 8 + 8,
                k % comps * nz : (k % comps + 1) * nz,
            ]
            out[pl.ds(begin * cols + k, 8, stride=cols), :] = block
        out[pl.ds(begin * cols + 2 * comps, 8, stride=cols), :] = weight


def inverse_kernel(got, tables, out):
    groups, rows, nz = out.shape
    _, window, _ = tables.shape
    half = window // 2
    steps = window // groups
    cols = got.shape[0] // half
    dot = functools.partial(
        jnp.dot, precision=lax.Precision.HIGHEST, preferred_element_type=jnp.float32
    )
    flip = lax.axis_index("xh")
    size = half // 2

    def member(f):
        return jnp.concatenate(
            [
                jnp.concatenate(
                    [got[pl.ds(at * size * cols + k, size, stride=cols), :] for at in (flip, 1 - flip)],
                    axis=0,
                )
                for k in range(f * cols // 2, (f + 1) * cols // 2)
            ],
            axis=1,
        )

    table = tables.at[1]
    result = dot(table[:, :half], member(0)) + dot(table[:, half:], member(1))
    for c in range(rows // steps):
        out[:, c * steps : (c + 1) * steps, :] = result[:, c * nz : (c + 1) * nz].reshape(
            groups, steps, nz
        )


def unpack_kernel(got, out):
    steps, comps, _, ny, _ = out.shape
    rows = got.shape[0] // ny
    for c in range(comps):
        for b in range(steps):
            out[b, c, 0] = got[pl.ds(c * steps + b, ny, stride=rows), :]


def operator(terms, sigma):
    ny, nz = sigma.shape[1:]
    pair = pair_index()
    p_plus, p_minus, q_term = terms[0, pair], terms[1, pair], terms[2, pair]

    row = lax.broadcasted_iota(jnp.int32, (ny, nz), 0)
    lane = lax.broadcasted_iota(jnp.int32, (ny, nz), 1)
    row_first, row_last = row == 0, row == ny - 1
    lane_first, lane_last = lane == 0, lane == nz - 1

    def ahead_y(f):
        return jnp.where(row_last, 0.0, pltpu.roll(f, ny - 1, 0))

    def ahead_z(f):
        return jnp.where(lane_last, 0.0, pltpu.roll(f, nz - 1, 1))

    def behind_y(f):
        return jnp.where(row_first, 0.0, pltpu.roll(f, 1, 0))

    def behind_z(f):
        return jnp.where(lane_first, 0.0, pltpu.roll(f, 1, 1))

    def curls(now, after):
        flux = []
        for f in (0, 3):
            ex, ey, ez = now[f : f + 3]
            _, ey_after, ez_after = after[f : f + 3]
            flux += [
                (ahead_y(ez) - ez) - (ahead_z(ey) - ey),
                (ahead_z(ex) - ex) - (ez_after - ez),
                (ey_after - ey) - (ahead_y(ex) - ex),
            ]
        return flux

    def tails(now, after):
        flux = []
        for f in (0, 3):
            ex, ey, ez = now[f : f + 3]
            _, ey_after, ez_after = after[f : f + 3]
            flux += [
                (ahead_z(ex) - ex) - (ez_after - ez),
                (ey_after - ey) - (ahead_y(ex) - ex),
            ]
        return flux

    def adjoints(flux, before):
        field = []
        for f, g in ((0, 0), (3, 2)):
            bx, by, bz = flux[f : f + 3]
            by_before, bz_before = before[g : g + 2]
            field += [
                (behind_z(by) - by) - (behind_y(bz) - bz),
                (bz_before - bz) - (behind_z(bx) - bx),
                (behind_y(bx) - bx) - (by_before - by),
            ]
        return field

    def add_couple(field, values, weight, sign):
        sp, sm, sq = weight * p_plus, weight * p_minus, weight * (sign * q_term)
        return [
            field[c] + (sp * values[c] - sq * values[3 + c]) for c in range(3)
        ] + [field[3 + c] + (sm * values[3 + c] + sq * values[c]) for c in range(3)]

    def lift(flux, source, begin, edge):
        now = load(source, begin)
        before = tails(load(source, begin - 1), now)
        for k, v in zip((1, 2, 4, 5), before):
            flux[0, k] = v if edge is None else jnp.where(edge, 0.0, v)
        for u in range(flux.shape[0] - 1):
            after = load(source, begin + u + 1)
            for k, v in enumerate(curls(now, after)):
                flux[u + 1, k] = v
            now = after

    def drop(flux, source, begin, sign, finish):
        before = [flux[0, k] for k in (1, 2, 4, 5)]
        for u in range(flux.shape[0] - 1):
            i = begin + u
            now = [flux[u + 1, k] for k in range(6)]
            value = adjoints(now, before)
            finish(i, add_couple(value, load(source, i), sigma[i + GUARD], sign))
            before = [now[k] for k in (1, 2, 4, 5)]

    return lift, drop


def load(ref, at):
    return [ref[at + GUARD, k] for k in range(6)]


def store(ref, at, values):
    for k in range(6):
        ref[at + GUARD, k] = values[k]


def finishers(terms, field, first, resid, total, place):
    inv_scale = terms[3, pair_index()]
    center = chebyshev_terms(SWEEPS - 1)[2]

    def begin_with(i, value):
        step = [v * (inv_scale * (1.0 / center)) for v in value]
        store(resid, place(i), value)
        store(field, place(i), step)
        store(total, place(i), step)

    def keep_first(i, value):
        store(first, place(i), value)

    def update(carry_term, push_term):
        push_term = push_term * inv_scale

        def do(i, value):
            rest = [r - v for r, v in zip(load(resid, i), value)]
            step = [carry_term * d + push_term * r for d, r in zip(load(field, i), rest)]
            store(resid, place(i), rest)
            store(field, place(i), step)
            store(total, place(i), [x + d for x, d in zip(load(total, i), step)])

        return do

    return begin_with, keep_first, update


def fill(first, sigma, source, begin):
    ny, nz = sigma.shape[1:]
    cols = 7
    for at in range(source.shape[0] // (cols * ny)):
        i = begin + (at // STRIPE) * (2 * STRIPE) + at % STRIPE
        parts = [source[pl.ds(at * cols * ny + k, ny, stride=cols), :] for k in range(cols)]
        store(first, i, parts[:6])
        sigma[i + GUARD] = parts[6]


def inner_kernel(terms, weights, mine, mate, field, first, resid, total, sigma, flux_a, flux_b):
    ny, nz = sigma.shape[1:]
    blank = jnp.zeros((ny, nz), jnp.float32)
    half_at, core_at = lax.axis_index("xh"), lax.axis_index("c")
    lift, drop = operator(terms, sigma)
    size = flux_a.shape[0] - 1

    for ref in (first, field):
        store(ref, -1, [blank] * 6)
        store(ref, HALF, [blank] * 6)
    fill(first, sigma, mine, STRIPE * core_at)
    fill(first, sigma, mate, STRIPE * (1 - core_at))

    def begin_of(level):
        count = (HALF - level + size - 1) // size
        return half_at * (HALF - count * size), count

    def run(level, flux, source, sign, finish, other_flux, other_source, beside):
        low, count = begin_of(level)
        other_low, _ = begin_of(level + 1)

        def at_edge(begin):
            return (begin == 0) & (half_at == 0)

        def step(t, _):
            begin = low + t * size
            drop(flux, source, begin, sign, finish)
            lift(flux, source, begin + size, None)
            return 0

        lax.fori_loop(0, count - 1, step, 0)
        if beside:
            lift(other_flux, other_source, other_low, at_edge(other_low))
        drop(flux, source, low + (count - 1) * size, sign, finish)
        if not beside:
            lift(other_flux, other_source, other_low, at_edge(other_low))

    def placed(level):
        low, high = half_at * level, HALF - level + half_at * level
        return lambda i: jnp.where((i >= low) & (i < high), i, HALF + 1)

    begin_with, _, _ = finishers(terms, field, first, resid, total, placed(1))
    lift(flux_b, first, begin_of(1)[0], half_at == 0)
    run(1, flux_b, first, -1.0, begin_with, flux_a, field, True)

    def sweep(s, beside):
        _, keep_first, _ = finishers(terms, field, first, resid, total, placed(2 + 2 * s))
        _, _, update = finishers(terms, field, first, resid, total, placed(3 + 2 * s))
        run(2 + 2 * s, flux_a, field, 1.0, keep_first, flux_b, first, beside)
        run(
            3 + 2 * s,
            flux_b,
            first,
            -1.0,
            update(weights[0, s], weights[1, s]),
            flux_a,
            field,
            beside,
        )

    def early(s, _):
        sweep(s, True)
        return 0

    def late(s, _):
        sweep(s, False)
        return 0

    apart = max(s for s in range(SWEEPS) if (HALF - 4 - 2 * s + size - 1) // size >= 3) + 1
    lax.fori_loop(0, apart, early, 0)
    lax.fori_loop(apart, SWEEPS - 1, late, 0)


def outer_kernel(
    terms, weights, part, part_mate, *refs
):
    given, out, state, (flux_a, flux_b) = refs[:5], refs[5], refs[6:11], refs[11:]
    field, first, resid, total, sigma = state
    ny, nz = sigma.shape[1:]
    half_at, core_at = lax.axis_index("xh"), lax.axis_index("c")
    lift, drop = operator(terms, sigma)
    size = flux_a.shape[0] - 1

    own_low = REACH * half_at
    for ref, old in zip(state[:4], given[:4]):
        for i in range(HALF):
            store(ref, own_low + i, load(old, i))
    for i in range(HALF):
        sigma[own_low + i + GUARD] = given[4][i + GUARD]
    halo_low = HALF * (1 - half_at)
    fill(first, sigma, part, halo_low + STRIPE * core_at)
    fill(first, sigma, part_mate, halo_low + STRIPE * (1 - core_at))

    def begin_of(level, turn):
        low = jnp.where(half_at == 0, HALF - level, level)
        return low + jnp.where(half_at == 0, turn, 1 - turn) * size

    def run(level, source, sign, finish, other_source):
        lift(flux_b, source, begin_of(level, 1), None)
        drop(flux_a, source, begin_of(level, 0), sign, finish)
        lift(flux_a, other_source, begin_of(level + 1, 0), None)
        drop(flux_b, source, begin_of(level, 1), sign, finish)

    begin_with, keep_first, update = finishers(terms, field, first, resid, total, lambda i: i)
    lift(flux_a, first, begin_of(1, 0), None)
    run(1, first, -1.0, begin_with, field)

    def sweep(s, _):
        run(2 + 2 * s, field, 1.0, keep_first, first)
        run(3 + 2 * s, first, -1.0, update(weights[0, s], weights[1, s]), field)
        return 0

    lax.fori_loop(0, SWEEPS - 1, sweep, 0)

    own_begin = own_low + STRIPE * core_at
    for at in range(HALF // 2):
        i = own_begin + (at // STRIPE) * (2 * STRIPE) + at % STRIPE
        for k, v in enumerate(load(total, i)):
            out[pl.ds(at * 6 * ny + k, ny, stride=6), :] = v


def per_device(forcing, start_field, iterate, region, conductance):
    steps, comps, planes, ny, nz = forcing.shape
    groups = lax.axis_size(TM)
    window = steps * groups
    half = window // 2
    both = jnp.asarray(np.stack(tables(window)))
    vmem = pl.BlockSpec(memory_space=pltpu.VMEM)
    smem = pl.BlockSpec(memory_space=pltpu.SMEM)
    f32 = jnp.float32
    params = pltpu.CompilerParams(vmem_limit_bytes=14 * 1024 * 1024)

    rows = comps * steps + 8
    plane_of = pl.BlockSpec((steps, comps, 1, ny, nz), lambda p: (0, 0, p, 0, 0))
    packed = pl.pallas_call(
        pack_kernel,
        out_shape=jax.ShapeDtypeStruct((groups * rows, nz), f32),
        grid=(planes,),
        in_specs=[
            smem,
            plane_of,
            pl.BlockSpec((comps, 1, ny, nz), lambda p: (0, p, 0, 0)),
            pl.BlockSpec((1, comps, 1, ny, nz), lambda p: (steps - 1, 0, p, 0, 0)),
            pl.BlockSpec((1, ny, nz), lambda p: (p, 0, 0)),
        ],
        out_specs=pl.BlockSpec((ny * rows, nz), lambda p: (p, 0)),
        compiler_params=pltpu.CompilerParams(vmem_limit_bytes=60 * 1024 * 1024),
        name="pack",
    )(conductance, forcing, start_field, iterate, region)

    got = lax.all_to_all(packed.reshape(groups, rows, nz), TM, 0, 0, tiled=True)

    spectrum = pl.pallas_call(
        forward_kernel,
        out_shape=jax.ShapeDtypeStruct((half * (2 * comps + 1), nz), f32),
        in_specs=[smem, vmem, vmem, vmem],
        out_specs=vmem,
        compiler_params=params,
        name="forward",
    )(conductance, got, both, region)

    mine = lax.all_to_all(
        spectrum.reshape(half, 1, (2 * comps + 1) * nz), GROUP, 0, 0, tiled=True
    )

    rows_sent = half * REACH // HALF
    part = lax.dynamic_slice_in_dim(
        mine, (1 - lax.axis_index("xh")) * (half - rows_sent), rows_sent, 0
    ).reshape(rows_sent * (2 * comps + 1), nz)
    mine = mine.reshape(half * (2 * comps + 1), nz)
    blocks, cores = lax.axis_size(("xh", "xl")), lax.axis_size("c")
    chips = [(i, blocks - 1 - i) for i in range(blocks)]
    across = [
        (i * cores + c, j * cores + cores - 1 - c) for i, j in chips for c in range(cores)
    ]
    part_mate = lax.ppermute(part, ("xh", "xl", "c"), across)
    part = lax.ppermute(part, ("xh", "xl"), chips)
    mate = lax.ppermute(mine, "c", [(0, 1), (1, 0)])

    terms = jnp.asarray(pair_table(window))
    weights = jnp.asarray(np.array(chebyshev_terms(SWEEPS - 1)[:2], np.float32))

    def state(places):
        return [(places, 2 * comps, ny, nz)] * 4 + [(places, ny, nz)]

    def flux(planes):
        return pltpu.VMEM((planes + 1, 2 * comps, ny, nz), f32)

    inner = pl.pallas_call(
        inner_kernel,
        out_shape=[jax.ShapeDtypeStruct(shape, f32) for shape in state(HALF + 3 * GUARD)],
        in_specs=[smem, smem, vmem, vmem],
        out_specs=[vmem] * 5,
        scratch_shapes=[flux(INNER)] * 2,
        compiler_params=params,
        cost_estimate=pl.CostEstimate(
            flops=10**10, bytes_accessed=2 * 10**7, transcendentals=0
        ),
        name="inner",
    )(terms, weights, mine, mate)
    solved = pl.pallas_call(
        outer_kernel,
        out_shape=jax.ShapeDtypeStruct((half * 2 * comps, nz), f32),
        in_specs=[smem, smem] + [vmem] * 7,
        out_specs=vmem,
        scratch_shapes=[pltpu.VMEM(shape, f32) for shape in state(HALF + REACH + 2 * GUARD)]
        + [flux(OUTER)] * 2,
        compiler_params=params,
        name="outer",
    )(terms, weights, part, part_mate, *inner)

    back = lax.all_to_all(
        solved.reshape(half, 1, 2 * comps * nz), GROUP, 0, 0, tiled=True
    ).reshape(half * 2 * comps, nz)

    pencil = pl.pallas_call(
        inverse_kernel,
        out_shape=jax.ShapeDtypeStruct((groups, comps * steps, nz), f32),
        in_specs=[vmem, vmem],
        out_specs=vmem,
        compiler_params=params,
        name="inverse",
    )(back, both)

    home = lax.all_to_all(pencil, TM, 0, 0, tiled=True)

    return pl.pallas_call(
        unpack_kernel,
        out_shape=jax.ShapeDtypeStruct(forcing.shape, f32),
        grid=(planes,),
        in_specs=[pl.BlockSpec((ny * comps * steps, nz), lambda p: (p, 0))],
        out_specs=plane_of,
        compiler_params=params,
        name="unpack",
    )(home.reshape(groups * comps * steps, nz))


def solution(mesh):
    names = ("yh", "z", "xh", "xl", "yl", "c")
    fine = Mesh(mesh.devices.reshape(2, 8, 2, 2, 4, 2), names)
    space = ("xh", "xl", "yl", "c")
    placed = (
        P(TM, None, space, None, None),
        P(None, space, None, None),
        P(TM, None, space, None, None),
        P(space, None, None),
        P(),
    )
    return jax.shard_map(
        per_device,
        mesh=fine,
        in_specs=placed,
        out_specs=P(TM, None, space, None, None),
        check_vma=False,
    )
```

```python
import math

import jax
import jax.numpy as jnp
import numpy as np
from jax import lax
from jax.experimental import pallas as pl
from jax.experimental.pallas import tpu as pltpu
from jax.sharding import Mesh
from jax.sharding import PartitionSpec as P

SWEEPS = 12
ALPHA = 0.1
LOWER = 0.02
UPPER = 1.0
SIGMA_TOP = 4.0
CURL_TOP = 12.0

TM = ("yh", "z")
GROUP = ("xl", "yl", "yh", "z")
HALF = 32
REACH = 24
STRIPE = 2
GUARD = 1
INNER = 8
OUTER = 12


def pair_index():
    half_at, low_at, *rest = (lax.axis_index(name) for name in ("xh",) + GROUP)
    index = (half_at + low_at) % 2
    for name, at in zip(GROUP[1:], rest):
        index = index * lax.axis_size(name) + at
    return index


def tables(window):
    gamma = ALPHA ** (1.0 / window)
    half = window // 2
    pairs = np.arange(half)
    freqs = np.concatenate([pairs, np.where(pairs == 0, half, window - pairs)])
    moments = np.arange(window)
    angle = 2.0 * math.pi * (freqs[:, None] * moments[None, :] % window) / window
    cas = np.cos(angle) + np.sin(angle)
    forward = cas * gamma ** moments[None, :]
    inverse = cas.T * gamma ** (-moments[:, None]) / window
    return forward.astype(np.float32), inverse.astype(np.float32)


def product(table, values):
    def parts(array):
        high = array.astype(jnp.bfloat16)
        return high, (array - high.astype(jnp.float32)).astype(jnp.bfloat16)

    (table_high, table_low), (high, low) = parts(table), parts(values)
    return jnp.dot(
        jnp.concatenate([table_high, table_low, table_high], axis=1),
        jnp.concatenate([high, high, low], axis=0),
        preferred_element_type=jnp.float32,
    )


def pair_table(window):
    gamma = ALPHA ** (1.0 / window)
    pairs = np.arange(window // 2)
    theta = 2.0 * math.pi * pairs / window
    plain = 1.0 - gamma * np.cos(theta)
    p_plus = np.where(pairs == 0, 1.0 - gamma, plain)
    p_minus = np.where(pairs == 0, 1.0 + gamma, plain)
    q_term = np.where(pairs == 0, 0.0, gamma * np.sin(theta))
    bound = np.sqrt(np.maximum(p_plus, p_minus) ** 2 + q_term**2) * SIGMA_TOP + CURL_TOP
    return np.stack([p_plus, p_minus, q_term, 1.0 / bound**2]).astype(np.float32)


def chebyshev_terms(count):
    center = (UPPER + LOWER) / 2.0
    radius = (UPPER - LOWER) / 2.0
    spread_ratio = center / radius
    weight_now = 1.0 / spread_ratio
    carry_terms, push_terms = ([], [])
    for _ in range(count):
        weight_next = 1.0 / (2.0 * spread_ratio - weight_now)
        carry_terms.append(weight_next * weight_now)
        push_terms.append(2.0 * weight_next / radius)
        weight_now = weight_next
    return (carry_terms, push_terms, center)


def material(region, cond):
    return jnp.where(
        region == 0,
        cond[0],
        jnp.where(region == 1, cond[1], jnp.where(region == 2, cond[2], 0.0)),
    )


def pack_kernel(cond, forcing, start, latest, region, out):
    steps, comps, _, ny, _ = forcing.shape
    rows = out.shape[0] // ny
    is_first = (lax.axis_index("yh") == 0) & (lax.axis_index("z") == 0)
    sigma = material(region[0], cond)
    for c in range(comps):
        head = forcing[0, c, 0]
        head = head + jnp.where(is_first, sigma * start[c, 0], 0.0)
        out[pl.ds(c * steps, ny, stride=rows), :] = head
        for b in range(1, steps):
            out[pl.ds(c * steps + b, ny, stride=rows), :] = forcing[b, c, 0]
        out[pl.ds(comps * steps + c, ny, stride=rows), :] = -ALPHA * (sigma * latest[0, c, 0])
    for pad in range(comps * steps + comps, rows):
        out[pl.ds(pad, ny, stride=rows), :] = jnp.zeros_like(sigma)


def forward_kernel(cond, got, tables, region, out):
    groups, _, nz = got.shape
    window = tables.shape[1]
    steps = window // groups
    comps = 3
    half = window // 2
    head = lax.broadcasted_iota(jnp.int32, (window, nz), 0) == 0
    parts = []
    for c in range(comps):
        part = got[:, c * steps : (c + 1) * steps, :].reshape(window, nz)
        row = got[groups - 1, comps * steps + c : comps * steps + c + 1, :]
        parts.append(part + jnp.where(head, row, 0.0))
    spectrum = product(tables[0], jnp.concatenate(parts, axis=1))
    width = comps * nz
    flip = lax.axis_index("xh")
    line = region[lax.axis_index("yh"), pl.ds(lax.axis_index("z"), 1), :]
    weight = jnp.broadcast_to(material(line, cond), (8, nz))
    cols = out.shape[0] // half
    for at in range(half // 8):
        lower = at < half // 16
        begin = at * 8 + (flip if lower else -flip) * (half // 2)
        for k in range(2 * comps):
            block = spectrum[
                k // comps * half + at * 8 : k // comps * half + at * 8 + 8,
                k % comps * nz : (k % comps + 1) * nz,
            ]
            out[pl.ds(begin * cols + k, 8, stride=cols), :] = block
        out[pl.ds(begin * cols + 2 * comps, 8, stride=cols), :] = weight


def inverse_kernel(got, tables, out):
    groups, rows, nz = out.shape
    _, window, _ = tables.shape
    half = window // 2
    steps = window // groups
    cols = got.shape[0] // half
    flip = lax.axis_index("xh")
    size = half // 2

    def member(f):
        return jnp.concatenate(
            [
                jnp.concatenate(
                    [got[pl.ds(at * size * cols + k, size, stride=cols), :] for at in (flip, 1 - flip)],
                    axis=0,
                )
                for k in range(f * cols // 2, (f + 1) * cols // 2)
            ],
            axis=1,
        )

    result = product(tables[1], jnp.concatenate([member(0), member(1)], axis=0))
    for c in range(rows // steps):
        out[:, c * steps : (c + 1) * steps, :] = result[:, c * nz : (c + 1) * nz].reshape(
            groups, steps, nz
        )


def unpack_kernel(got, out):
    steps, comps, _, ny, _ = out.shape
    rows = got.shape[0] // ny
    for c in range(comps):
        for b in range(steps):
            out[b, c, 0] = got[pl.ds(c * steps + b, ny, stride=rows), :]


def operator(terms, sigma):
    ny, nz = sigma.shape[1:]
    pair = pair_index()
    p_plus, p_minus, q_term = terms[0, pair], terms[1, pair], terms[2, pair]

    row = lax.broadcasted_iota(jnp.int32, (ny, nz), 0)
    lane = lax.broadcasted_iota(jnp.int32, (ny, nz), 1)
    row_first, row_last = row == 0, row == ny - 1
    lane_first, lane_last = lane == 0, lane == nz - 1

    def ahead_y(f):
        return jnp.where(row_last, 0.0, pltpu.roll(f, ny - 1, 0))

    def ahead_z(f):
        return jnp.where(lane_last, 0.0, pltpu.roll(f, nz - 1, 1))

    def behind_y(f):
        return jnp.where(row_first, 0.0, pltpu.roll(f, 1, 0))

    def behind_z(f):
        return jnp.where(lane_first, 0.0, pltpu.roll(f, 1, 1))

    def curls(now, after):
        flux = []
        for f in (0, 3):
            ex, ey, ez = now[f : f + 3]
            _, ey_after, ez_after = after[f : f + 3]
            flux += [
                (ahead_y(ez) - ez) - (ahead_z(ey) - ey),
                (ahead_z(ex) - ex) - (ez_after - ez),
                (ey_after - ey) - (ahead_y(ex) - ex),
            ]
        return flux

    def tails(now, after):
        flux = []
        for f in (0, 3):
            ex, ey, ez = now[f : f + 3]
            _, ey_after, ez_after = after[f : f + 3]
            flux += [
                (ahead_z(ex) - ex) - (ez_after - ez),
                (ey_after - ey) - (ahead_y(ex) - ex),
            ]
        return flux

    def adjoints(flux, before):
        field = []
        for f, g in ((0, 0), (3, 2)):
            bx, by, bz = flux[f : f + 3]
            by_before, bz_before = before[g : g + 2]
            field += [
                (behind_z(by) - by) - (behind_y(bz) - bz),
                (bz_before - bz) - (behind_z(bx) - bx),
                (behind_y(bx) - bx) - (by_before - by),
            ]
        return field

    def add_couple(field, values, weight, sign):
        sp, sm, sq = weight * p_plus, weight * p_minus, weight * (sign * q_term)
        return [
            field[c] + (sp * values[c] - sq * values[3 + c]) for c in range(3)
        ] + [field[3 + c] + (sm * values[3 + c] + sq * values[c]) for c in range(3)]

    def lift(flux, source, begin, edge):
        now = load(source, begin)
        before = tails(load(source, begin - 1), now)
        for k, v in zip((1, 2, 4, 5), before):
            flux[0, k] = v if edge is None else jnp.where(edge, 0.0, v)
        for u in range(flux.shape[0] - 1):
            after = load(source, begin + u + 1)
            for k, v in enumerate(curls(now, after)):
                flux[u + 1, k] = v
            now = after

    def drop(flux, source, begin, sign, finish):
        before = [flux[0, k] for k in (1, 2, 4, 5)]
        for u in range(flux.shape[0] - 1):
            i = begin + u
            now = [flux[u + 1, k] for k in range(6)]
            value = adjoints(now, before)
            finish(i, add_couple(value, load(source, i), sigma[i + GUARD], sign))
            before = [now[k] for k in (1, 2, 4, 5)]

    return lift, drop


def load(ref, at):
    return [ref[at + GUARD, k] for k in range(6)]


def store(ref, at, values):
    for k in range(6):
        ref[at + GUARD, k] = values[k]


def finishers(terms, field, first, resid, total, place):
    inv_scale = terms[3, pair_index()]
    center = chebyshev_terms(SWEEPS - 1)[2]

    def begin_with(i, value):
        step = [v * (inv_scale * (1.0 / center)) for v in value]
        store(resid, place(i), value)
        store(field, place(i), step)
        store(total, place(i), step)

    def keep_first(i, value):
        store(first, place(i), value)

    def update(carry_term, push_term):
        push_term = push_term * inv_scale

        def do(i, value):
            rest = [r - v for r, v in zip(load(resid, i), value)]
            step = [carry_term * d + push_term * r for d, r in zip(load(field, i), rest)]
            store(resid, place(i), rest)
            store(field, place(i), step)
            store(total, place(i), [x + d for x, d in zip(load(total, i), step)])

        return do

    return begin_with, keep_first, update


def fill(first, sigma, source, begin):
    ny, nz = sigma.shape[1:]
    cols = 7
    for at in range(source.shape[0] // (cols * ny)):
        i = begin + (at // STRIPE) * (2 * STRIPE) + at % STRIPE
        parts = [source[pl.ds(at * cols * ny + k, ny, stride=cols), :] for k in range(cols)]
        store(first, i, parts[:6])
        sigma[i + GUARD] = parts[6]


def inner_kernel(terms, weights, mine, mate, field, first, resid, total, sigma, flux_a, flux_b):
    ny, nz = sigma.shape[1:]
    blank = jnp.zeros((ny, nz), jnp.float32)
    half_at, core_at = lax.axis_index("xh"), lax.axis_index("c")
    lift, drop = operator(terms, sigma)
    size = flux_a.shape[0] - 1

    for ref in (first, field):
        store(ref, -1, [blank] * 6)
        store(ref, HALF, [blank] * 6)
    fill(first, sigma, mine, STRIPE * core_at)
    fill(first, sigma, mate, STRIPE * (1 - core_at))

    def begin_of(level):
        count = (HALF - level + size - 1) // size
        return half_at * (HALF - count * size), count

    def run(level, flux, source, sign, finish, other_flux, other_source, beside):
        low, count = begin_of(level)
        other_low, _ = begin_of(level + 1)

        def at_edge(begin):
            return (begin == 0) & (half_at == 0)

        def step(t, _):
            begin = low + t * size
            drop(flux, source, begin, sign, finish)
            lift(flux, source, begin + size, None)
            return 0

        lax.fori_loop(0, count - 1, step, 0)
        if beside:
            lift(other_flux, other_source, other_low, at_edge(other_low))
        drop(flux, source, low + (count - 1) * size, sign, finish)
        if not beside:
            lift(other_flux, other_source, other_low, at_edge(other_low))

    def placed(level):
        low, high = half_at * level, HALF - level + half_at * level
        return lambda i: jnp.where((i >= low) & (i < high), i, HALF + 1)

    begin_with, _, _ = finishers(terms, field, first, resid, total, placed(1))
    lift(flux_b, first, begin_of(1)[0], half_at == 0)
    run(1, flux_b, first, -1.0, begin_with, flux_a, field, True)

    def sweep(s, beside):
        _, keep_first, _ = finishers(terms, field, first, resid, total, placed(2 + 2 * s))
        _, _, update = finishers(terms, field, first, resid, total, placed(3 + 2 * s))
        run(2 + 2 * s, flux_a, field, 1.0, keep_first, flux_b, first, beside)
        run(
            3 + 2 * s,
            flux_b,
            first,
            -1.0,
            update(weights[0, s], weights[1, s]),
            flux_a,
            field,
            beside,
        )

    def early(s, _):
        sweep(s, True)
        return 0

    def late(s, _):
        sweep(s, False)
        return 0

    apart = max(s for s in range(SWEEPS) if (HALF - 4 - 2 * s + size - 1) // size >= 3) + 1
    lax.fori_loop(0, apart, early, 0)
    lax.fori_loop(apart, SWEEPS - 1, late, 0)


def outer_kernel(
    terms, weights, part, part_mate, *refs
):
    given, out, state, (flux_a, flux_b) = refs[:5], refs[5], refs[6:11], refs[11:]
    field, first, resid, total, sigma = state
    ny, nz = sigma.shape[1:]
    half_at, core_at = lax.axis_index("xh"), lax.axis_index("c")
    lift, drop = operator(terms, sigma)
    size = flux_a.shape[0] - 1

    own_low = REACH * half_at
    for ref, old in zip(state[:4], given[:4]):
        for i in range(HALF):
            store(ref, own_low + i, load(old, i))
    for i in range(HALF):
        sigma[own_low + i + GUARD] = given[4][i + GUARD]
    halo_low = HALF * (1 - half_at)
    fill(first, sigma, part, halo_low + STRIPE * core_at)
    fill(first, sigma, part_mate, halo_low + STRIPE * (1 - core_at))

    def begin_of(level, turn):
        low = jnp.where(half_at == 0, HALF - level, level)
        return low + jnp.where(half_at == 0, turn, 1 - turn) * size

    def run(level, source, sign, finish, other_source):
        drop(flux_a, source, begin_of(level, 0), sign, finish)
        lift(flux_b, source, begin_of(level, 1), None)
        lift(flux_a, other_source, begin_of(level + 1, 0), None)
        drop(flux_b, source, begin_of(level, 1), sign, finish)

    begin_with, keep_first, update = finishers(terms, field, first, resid, total, lambda i: i)
    lift(flux_a, first, begin_of(1, 0), None)
    run(1, first, -1.0, begin_with, field)

    def sweep(s, _):
        run(2 + 2 * s, field, 1.0, keep_first, first)
        run(3 + 2 * s, first, -1.0, update(weights[0, s], weights[1, s]), field)
        return 0

    lax.fori_loop(0, SWEEPS - 1, sweep, 0)

    own_begin = own_low + STRIPE * core_at
    for at in range(HALF // 2):
        i = own_begin + (at // STRIPE) * (2 * STRIPE) + at % STRIPE
        for k, v in enumerate(load(total, i)):
            out[pl.ds(at * 6 * ny + k, ny, stride=6), :] = v


def per_device(forcing, start_field, iterate, region, conductance):
    steps, comps, planes, ny, nz = forcing.shape
    groups = lax.axis_size(TM)
    window = steps * groups
    half = window // 2
    both = jnp.asarray(np.stack(tables(window)))
    vmem = pl.BlockSpec(memory_space=pltpu.VMEM)
    smem = pl.BlockSpec(memory_space=pltpu.SMEM)
    f32 = jnp.float32
    params = pltpu.CompilerParams(vmem_limit_bytes=14 * 1024 * 1024)

    rows = comps * steps + 8
    plane_of = pl.BlockSpec((steps, comps, 1, ny, nz), lambda p: (0, 0, p, 0, 0))
    packed = pl.pallas_call(
        pack_kernel,
        out_shape=jax.ShapeDtypeStruct((groups * rows, nz), f32),
        grid=(planes,),
        in_specs=[
            smem,
            plane_of,
            pl.BlockSpec((comps, 1, ny, nz), lambda p: (0, p, 0, 0)),
            pl.BlockSpec((1, comps, 1, ny, nz), lambda p: (steps - 1, 0, p, 0, 0)),
            pl.BlockSpec((1, ny, nz), lambda p: (p, 0, 0)),
        ],
        out_specs=pl.BlockSpec((ny * rows, nz), lambda p: (p, 0)),
        compiler_params=pltpu.CompilerParams(vmem_limit_bytes=60 * 1024 * 1024),
        name="pack",
    )(conductance, forcing, start_field, iterate, region)

    got = lax.all_to_all(packed.reshape(groups, rows, nz), TM, 0, 0, tiled=True)

    spectrum = pl.pallas_call(
        forward_kernel,
        out_shape=jax.ShapeDtypeStruct((half * (2 * comps + 1), nz), f32),
        in_specs=[smem, vmem, vmem, vmem],
        out_specs=vmem,
        compiler_params=params,
        name="forward",
    )(conductance, got, both, region)

    mine = lax.all_to_all(
        spectrum.reshape(half, 1, (2 * comps + 1) * nz), GROUP, 0, 0, tiled=True
    )

    rows_sent = half * REACH // HALF
    part = lax.dynamic_slice_in_dim(
        mine, (1 - lax.axis_index("xh")) * (half - rows_sent), rows_sent, 0
    ).reshape(rows_sent * (2 * comps + 1), nz)
    mine = mine.reshape(half * (2 * comps + 1), nz)
    blocks, cores = lax.axis_size(("xh", "xl")), lax.axis_size("c")
    chips = [(i, blocks - 1 - i) for i in range(blocks)]
    across = [
        (i * cores + c, j * cores + cores - 1 - c) for i, j in chips for c in range(cores)
    ]
    part_mate = lax.ppermute(part, ("xh", "xl", "c"), across)
    part = lax.ppermute(part, ("xh", "xl"), chips)
    mate = lax.ppermute(mine, "c", [(0, 1), (1, 0)])

    terms = jnp.asarray(pair_table(window))
    weights = jnp.asarray(np.array(chebyshev_terms(SWEEPS - 1)[:2], np.float32))

    def state(places):
        return [(places, 2 * comps, ny, nz)] * 4 + [(places, ny, nz)]

    def flux(planes):
        return pltpu.VMEM((planes + 1, 2 * comps, ny, nz), f32)

    inner = pl.pallas_call(
        inner_kernel,
        out_shape=[jax.ShapeDtypeStruct(shape, f32) for shape in state(HALF + 3 * GUARD)],
        in_specs=[smem, smem, vmem, vmem],
        out_specs=[vmem] * 5,
        scratch_shapes=[flux(INNER)] * 2,
        compiler_params=params,
        cost_estimate=pl.CostEstimate(
            flops=10**10, bytes_accessed=2 * 10**7, transcendentals=0
        ),
        name="inner",
    )(terms, weights, mine, mate)
    solved = pl.pallas_call(
        outer_kernel,
        out_shape=jax.ShapeDtypeStruct((half * 2 * comps, nz), f32),
        in_specs=[smem, smem] + [vmem] * 7,
        out_specs=vmem,
        scratch_shapes=[pltpu.VMEM(shape, f32) for shape in state(HALF + REACH + 2 * GUARD)]
        + [flux(OUTER)] * 2,
        compiler_params=params,
        name="outer",
    )(terms, weights, part, part_mate, *inner)

    back = lax.all_to_all(
        solved.reshape(half, 1, 2 * comps * nz), GROUP, 0, 0, tiled=True
    ).reshape(half * 2 * comps, nz)

    pencil = pl.pallas_call(
        inverse_kernel,
        out_shape=jax.ShapeDtypeStruct((groups, comps * steps, nz), f32),
        in_specs=[vmem, vmem],
        out_specs=vmem,
        compiler_params=params,
        name="inverse",
    )(back, both)

    home = lax.all_to_all(pencil, TM, 0, 0, tiled=True)

    return pl.pallas_call(
        unpack_kernel,
        out_shape=jax.ShapeDtypeStruct(forcing.shape, f32),
        grid=(planes,),
        in_specs=[pl.BlockSpec((ny * comps * steps, nz), lambda p: (p, 0))],
        out_specs=plane_of,
        compiler_params=params,
        name="unpack",
    )(home.reshape(groups * comps * steps, nz))


def solution(mesh):
    names = ("yh", "z", "xh", "xl", "yl", "c")
    fine = Mesh(mesh.devices.reshape(2, 8, 2, 2, 4, 2), names)
    space = ("xh", "xl", "yl", "c")
    placed = (
        P(TM, None, space, None, None),
        P(None, space, None, None),
        P(TM, None, space, None, None),
        P(space, None, None),
        P(),
    )
    return jax.shard_map(
        per_device,
        mesh=fine,
        in_specs=placed,
        out_specs=P(TM, None, space, None, None),
        check_vma=False,
    )
```

```python
import itertools
import math

import jax
import jax.numpy as jnp
import numpy as np
from jax import lax
from jax.experimental import pallas as pl
from jax.experimental.pallas import tpu as pltpu
from jax.sharding import Mesh
from jax.sharding import PartitionSpec as P

SWEEPS = 12
ALPHA = 0.1
LOWER = 0.02
UPPER = 1.0
SIGMA_TOP = 4.0
CURL_TOP = 12.0

TM = ("yh", "z")
GROUP = ("yl", "yh", "xl", "z")
HALF = 32
REACH = 24
STRIPE = 2
GUARD = 1
INNER = 8
OUTER = 12


def pair_index():
    index = 0
    for name in GROUP:
        at = lax.axis_index(name)
        if name == "xl":
            at = (at + lax.axis_index("xh")) % 2
        index = index * lax.axis_size(name) + at
    return index


def place_of(block):
    flip = lax.axis_index("xh")
    return block + (flip if block % 2 == 0 else -flip)


def tables(window):
    gamma = ALPHA ** (1.0 / window)
    half = window // 2
    pairs = np.arange(half)
    freqs = np.concatenate([pairs, np.where(pairs == 0, half, window - pairs)])
    moments = np.arange(window)
    angle = 2.0 * math.pi * (freqs[:, None] * moments[None, :] % window) / window
    cas = np.cos(angle) + np.sin(angle)
    forward = cas * gamma ** moments[None, :]
    inverse = cas.T * gamma ** (-moments[:, None]) / window
    return forward.astype(np.float32), inverse.astype(np.float32)


def product(table, values):
    def parts(array):
        high = array.astype(jnp.bfloat16)
        return high, (array - high.astype(jnp.float32)).astype(jnp.bfloat16)

    (table_high, table_low), (high, low) = parts(table), parts(values)
    return jnp.dot(
        jnp.concatenate([table_high, table_low, table_high], axis=1),
        jnp.concatenate([high, high, low], axis=0),
        preferred_element_type=jnp.float32,
    )


def pair_table(window):
    gamma = ALPHA ** (1.0 / window)
    pairs = np.arange(window // 2)
    theta = 2.0 * math.pi * pairs / window
    plain = 1.0 - gamma * np.cos(theta)
    p_plus = np.where(pairs == 0, 1.0 - gamma, plain)
    p_minus = np.where(pairs == 0, 1.0 + gamma, plain)
    q_term = np.where(pairs == 0, 0.0, gamma * np.sin(theta))
    bound = np.sqrt(np.maximum(p_plus, p_minus) ** 2 + q_term**2) * SIGMA_TOP + CURL_TOP
    return np.stack([p_plus, p_minus, q_term, 1.0 / bound**2]).astype(np.float32)


def chebyshev_terms(count):
    center = (UPPER + LOWER) / 2.0
    radius = (UPPER - LOWER) / 2.0
    spread_ratio = center / radius
    weight_now = 1.0 / spread_ratio
    carry_terms, push_terms = ([], [])
    for _ in range(count):
        weight_next = 1.0 / (2.0 * spread_ratio - weight_now)
        carry_terms.append(weight_next * weight_now)
        push_terms.append(2.0 * weight_next / radius)
        weight_now = weight_next
    return (carry_terms, push_terms, center)


def material(region, cond):
    return jnp.where(
        region == 0,
        cond[0],
        jnp.where(region == 1, cond[1], jnp.where(region == 2, cond[2], 0.0)),
    )


def pack_kernel(cond, forcing, start, latest, region, out):
    steps, comps, _, ny, _ = forcing.shape
    rows = out.shape[0] // ny
    is_first = (lax.axis_index("yh") == 0) & (lax.axis_index("z") == 0)
    sigma = material(region[0], cond)
    for c in range(comps):
        head = forcing[0, c, 0]
        head = head + jnp.where(is_first, sigma * start[c, 0], 0.0)
        out[pl.ds(c * steps, ny, stride=rows), :] = head
        for b in range(1, steps):
            out[pl.ds(c * steps + b, ny, stride=rows), :] = forcing[b, c, 0]
        out[pl.ds(comps * steps + c, ny, stride=rows), :] = -ALPHA * (sigma * latest[0, c, 0])
    for pad in range(comps * steps + comps, rows):
        out[pl.ds(pad, ny, stride=rows), :] = jnp.zeros_like(sigma)


def forward_kernel(cond, got, tables, region, out):
    groups, _, nz = got.shape
    window = tables.shape[1]
    steps = window // groups
    comps = 3
    half = window // 2
    head = lax.broadcasted_iota(jnp.int32, (window, nz), 0) == 0
    parts = []
    for c in range(comps):
        part = got[:, c * steps : (c + 1) * steps, :].reshape(window, nz)
        row = got[groups - 1, comps * steps + c : comps * steps + c + 1, :]
        parts.append(part + jnp.where(head, row, 0.0))
    spectrum = product(tables[0], jnp.concatenate(parts, axis=1))
    width = comps * nz
    line = region[lax.axis_index("yh"), pl.ds(lax.axis_index("z"), 1), :]
    weight = jnp.broadcast_to(material(line, cond), (8, nz))
    cols = out.shape[0] // half
    for at in range(half // 8):
        begin = place_of(at) * 8
        for k in range(2 * comps):
            block = spectrum[
                k // comps * half + at * 8 : k // comps * half + at * 8 + 8,
                k % comps * nz : (k % comps + 1) * nz,
            ]
            out[pl.ds(begin * cols + k, 8, stride=cols), :] = block
        out[pl.ds(begin * cols + 2 * comps, 8, stride=cols), :] = weight


def inverse_kernel(got, tables, out):
    groups, rows, nz = out.shape
    _, window, _ = tables.shape
    half = window // 2
    steps = window // groups
    cols = got.shape[0] // half
    def member(f):
        return jnp.concatenate(
            [
                jnp.concatenate(
                    [
                        got[pl.ds(place_of(at) * 8 * cols + k, 8, stride=cols), :]
                        for at in range(half // 8)
                    ],
                    axis=0,
                )
                for k in range(f * cols // 2, (f + 1) * cols // 2)
            ],
            axis=1,
        )

    result = product(tables[1], jnp.concatenate([member(0), member(1)], axis=0))
    for c in range(rows // steps):
        out[:, c * steps : (c + 1) * steps, :] = result[:, c * nz : (c + 1) * nz].reshape(
            groups, steps, nz
        )


def unpack_kernel(got, out):
    steps, comps, _, ny, _ = out.shape
    rows = got.shape[0] // ny
    for c in range(comps):
        for b in range(steps):
            out[b, c, 0] = got[pl.ds(c * steps + b, ny, stride=rows), :]


def operator(terms, sigma):
    ny, nz = sigma.shape[1:]
    pair = pair_index()
    p_plus, p_minus, q_term = terms[0, pair], terms[1, pair], terms[2, pair]

    row = lax.broadcasted_iota(jnp.int32, (ny, nz), 0)
    lane = lax.broadcasted_iota(jnp.int32, (ny, nz), 1)
    row_first, row_last = row == 0, row == ny - 1
    lane_first, lane_last = lane == 0, lane == nz - 1

    def ahead_y(f):
        return jnp.where(row_last, 0.0, pltpu.roll(f, ny - 1, 0))

    def ahead_z(f):
        return jnp.where(lane_last, 0.0, pltpu.roll(f, nz - 1, 1))

    def behind_y(f):
        return jnp.where(row_first, 0.0, pltpu.roll(f, 1, 0))

    def behind_z(f):
        return jnp.where(lane_first, 0.0, pltpu.roll(f, 1, 1))

    def curls(now, after):
        flux = []
        for f in (0, 3):
            ex, ey, ez = now[f : f + 3]
            _, ey_after, ez_after = after[f : f + 3]
            flux += [
                (ahead_y(ez) - ez) - (ahead_z(ey) - ey),
                (ahead_z(ex) - ex) - (ez_after - ez),
                (ey_after - ey) - (ahead_y(ex) - ex),
            ]
        return flux

    def tails(now, after):
        flux = []
        for f in (0, 3):
            ex, ey, ez = now[f : f + 3]
            _, ey_after, ez_after = after[f : f + 3]
            flux += [
                (ahead_z(ex) - ex) - (ez_after - ez),
                (ey_after - ey) - (ahead_y(ex) - ex),
            ]
        return flux

    def adjoints(flux, before):
        field = []
        for f, g in ((0, 0), (3, 2)):
            bx, by, bz = flux[f : f + 3]
            by_before, bz_before = before[g : g + 2]
            field += [
                (behind_z(by) - by) - (behind_y(bz) - bz),
                (bz_before - bz) - (behind_z(bx) - bx),
                (behind_y(bx) - bx) - (by_before - by),
            ]
        return field

    def add_couple(field, values, weight, sign):
        sp, sm, sq = weight * p_plus, weight * p_minus, weight * (sign * q_term)
        return [
            field[c] + (sp * values[c] - sq * values[3 + c]) for c in range(3)
        ] + [field[3 + c] + (sm * values[3 + c] + sq * values[c]) for c in range(3)]

    def lift(flux, source, begin, edge):
        now = load(source, begin)
        before = tails(load(source, begin - 1), now)
        for k, v in zip((1, 2, 4, 5), before):
            flux[0, k] = v if edge is None else jnp.where(edge, 0.0, v)
        for u in range(flux.shape[0] - 1):
            after = load(source, begin + u + 1)
            for k, v in enumerate(curls(now, after)):
                flux[u + 1, k] = v
            now = after

    def drop(flux, source, begin, sign, finish):
        before = [flux[0, k] for k in (1, 2, 4, 5)]
        for u in range(flux.shape[0] - 1):
            i = begin + u
            now = [flux[u + 1, k] for k in range(6)]
            value = adjoints(now, before)
            finish(i, add_couple(value, load(source, i), sigma[i + GUARD], sign))
            before = [now[k] for k in (1, 2, 4, 5)]

    return lift, drop


def load(ref, at):
    return [ref[at + GUARD, k] for k in range(6)]


def store(ref, at, values):
    for k in range(6):
        ref[at + GUARD, k] = values[k]


def finishers(terms, field, first, resid, total, place):
    inv_scale = terms[3, pair_index()]
    center = chebyshev_terms(SWEEPS - 1)[2]

    def begin_with(i, value):
        step = [v * (inv_scale * (1.0 / center)) for v in value]
        store(resid, place(i), value)
        store(field, place(i), step)
        store(total, place(i), step)

    def keep_first(i, value):
        store(first, place(i), value)

    def update(carry_term, push_term):
        push_term = push_term * inv_scale

        def do(i, value):
            rest = [r - v for r, v in zip(load(resid, i), value)]
            step = [carry_term * d + push_term * r for d, r in zip(load(field, i), rest)]
            store(resid, place(i), rest)
            store(field, place(i), step)
            store(total, place(i), [x + d for x, d in zip(load(total, i), step)])

        return do

    return begin_with, keep_first, update


def fill(first, sigma, source, rows, begins):
    ny, nz = sigma.shape[1:]
    cols = 7
    for row, (x_at, y_at, p) in rows:
        i = begins[x_at] + 2 * STRIPE * y_at + p
        parts = [source[pl.ds(row * cols * ny + k, ny, stride=cols), :] for k in range(cols)]
        store(first, i, parts[:6])
        sigma[i + GUARD] = parts[6]


def brick_rows():
    order = itertools.product(range(4), range(STRIPE), range(2))
    return [(row, (x_at, y_at, p)) for row, (y_at, p, x_at) in enumerate(order)]


def halo_rows():
    order = [(0, y_at, p) for y_at in range(4) for p in range(STRIPE)]
    order += [(1, y_at, p) for y_at in range(2) for p in range(STRIPE)]
    return list(enumerate(order))


def inner_kernel(terms, weights, mine, mate, field, first, resid, total, sigma, flux_a, flux_b):
    ny, nz = sigma.shape[1:]
    blank = jnp.zeros((ny, nz), jnp.float32)
    half_at, core_at = lax.axis_index("xh"), lax.axis_index("c")
    lift, drop = operator(terms, sigma)
    size = flux_a.shape[0] - 1

    for ref in (first, field):
        store(ref, -1, [blank] * 6)
        store(ref, HALF, [blank] * 6)
    for source, core in ((mine, core_at), (mate, 1 - core_at)):
        begin = STRIPE * core
        fill(first, sigma, source, brick_rows(), (begin, begin + HALF // 2))

    def begin_of(level):
        count = (HALF - level + size - 1) // size
        return half_at * (HALF - count * size), count

    def run(level, flux, source, sign, finish, other_flux, other_source, beside):
        low, count = begin_of(level)
        other_low, _ = begin_of(level + 1)

        def at_edge(begin):
            return (begin == 0) & (half_at == 0)

        def step(t, _):
            begin = low + t * size
            drop(flux, source, begin, sign, finish)
            lift(flux, source, begin + size, None)
            return 0

        lax.fori_loop(0, count - 1, step, 0)
        if beside:
            lift(other_flux, other_source, other_low, at_edge(other_low))
        drop(flux, source, low + (count - 1) * size, sign, finish)
        if not beside:
            lift(other_flux, other_source, other_low, at_edge(other_low))

    def placed(level):
        low, high = half_at * level, HALF - level + half_at * level
        return lambda i: jnp.where((i >= low) & (i < high), i, HALF + 1)

    begin_with, _, _ = finishers(terms, field, first, resid, total, placed(1))
    lift(flux_b, first, begin_of(1)[0], half_at == 0)
    run(1, flux_b, first, -1.0, begin_with, flux_a, field, True)

    def sweep(s, beside):
        _, keep_first, _ = finishers(terms, field, first, resid, total, placed(2 + 2 * s))
        _, _, update = finishers(terms, field, first, resid, total, placed(3 + 2 * s))
        run(2 + 2 * s, flux_a, field, 1.0, keep_first, flux_b, first, beside)
        run(
            3 + 2 * s,
            flux_b,
            first,
            -1.0,
            update(weights[0, s], weights[1, s]),
            flux_a,
            field,
            beside,
        )

    def early(s, _):
        sweep(s, True)
        return 0

    def late(s, _):
        sweep(s, False)
        return 0

    apart = max(s for s in range(SWEEPS) if (HALF - 4 - 2 * s + size - 1) // size >= 3) + 1
    lax.fori_loop(0, apart, early, 0)
    lax.fori_loop(apart, SWEEPS - 1, late, 0)


def outer_kernel(
    terms, weights, part, part_mate, *refs
):
    given, out, state, (flux_a, flux_b) = refs[:5], refs[5], refs[6:11], refs[11:]
    field, first, resid, total, sigma = state
    ny, nz = sigma.shape[1:]
    half_at, core_at = lax.axis_index("xh"), lax.axis_index("c")
    lift, drop = operator(terms, sigma)
    size = flux_a.shape[0] - 1

    own_low = REACH * half_at
    for ref, old in zip(state[:4], given[:4]):
        for i in range(HALF):
            store(ref, own_low + i, load(old, i))
    for i in range(HALF):
        sigma[own_low + i + GUARD] = given[4][i + GUARD]
    halo_low = HALF * (1 - half_at)
    for source, core in ((part, core_at), (part_mate, 1 - core_at)):
        begin = halo_low + STRIPE * core
        whole_x = begin + (REACH - HALF // 2) * half_at
        half_x = begin + HALF // 2 * (1 - half_at)
        fill(first, sigma, source, halo_rows(), (whole_x, half_x))

    def begin_of(level, turn):
        low = jnp.where(half_at == 0, HALF - level, level)
        return low + jnp.where(half_at == 0, turn, 1 - turn) * size

    def run(level, source, sign, finish, other_source):
        drop(flux_a, source, begin_of(level, 0), sign, finish)
        lift(flux_b, source, begin_of(level, 1), None)
        lift(flux_a, other_source, begin_of(level + 1, 0), None)
        drop(flux_b, source, begin_of(level, 1), sign, finish)

    begin_with, keep_first, update = finishers(terms, field, first, resid, total, lambda i: i)
    lift(flux_a, first, begin_of(1, 0), None)
    run(1, first, -1.0, begin_with, field)

    def sweep(s, _):
        run(2 + 2 * s, field, 1.0, keep_first, first)
        run(3 + 2 * s, first, -1.0, update(weights[0, s], weights[1, s]), field)
        return 0

    lax.fori_loop(0, SWEEPS - 1, sweep, 0)

    own_begin = own_low + STRIPE * core_at
    for row, (x_at, y_at, p) in brick_rows():
        i = own_begin + HALF // 2 * x_at + 2 * STRIPE * y_at + p
        for k, v in enumerate(load(total, i)):
            out[pl.ds(row * 6 * ny + k, ny, stride=6), :] = v


def per_device(forcing, start_field, iterate, region, conductance):
    steps, comps, planes, ny, nz = forcing.shape
    groups = lax.axis_size(TM)
    window = steps * groups
    half = window // 2
    both = jnp.asarray(np.stack(tables(window)))
    vmem = pl.BlockSpec(memory_space=pltpu.VMEM)
    smem = pl.BlockSpec(memory_space=pltpu.SMEM)
    f32 = jnp.float32
    params = pltpu.CompilerParams(vmem_limit_bytes=14 * 1024 * 1024)

    rows = comps * steps + 8
    plane_of = pl.BlockSpec((steps, comps, 1, ny, nz), lambda p: (0, 0, p, 0, 0))
    packed = pl.pallas_call(
        pack_kernel,
        out_shape=jax.ShapeDtypeStruct((groups * rows, nz), f32),
        grid=(planes,),
        in_specs=[
            smem,
            plane_of,
            pl.BlockSpec((comps, 1, ny, nz), lambda p: (0, p, 0, 0)),
            pl.BlockSpec((1, comps, 1, ny, nz), lambda p: (steps - 1, 0, p, 0, 0)),
            pl.BlockSpec((1, ny, nz), lambda p: (p, 0, 0)),
        ],
        out_specs=pl.BlockSpec((ny * rows, nz), lambda p: (p, 0)),
        compiler_params=pltpu.CompilerParams(vmem_limit_bytes=60 * 1024 * 1024),
        name="pack",
    )(conductance, forcing, start_field, iterate, region)

    got = lax.all_to_all(packed.reshape(groups, rows, nz), TM, 0, 0, tiled=True)

    spectrum = pl.pallas_call(
        forward_kernel,
        out_shape=jax.ShapeDtypeStruct((half * (2 * comps + 1), nz), f32),
        in_specs=[smem, vmem, vmem, vmem],
        out_specs=vmem,
        compiler_params=params,
        name="forward",
    )(conductance, got, both, region)

    mine = lax.all_to_all(
        spectrum.reshape(half, 1, (2 * comps + 1) * nz), GROUP, 0, 0, tiled=True
    )

    half_at = lax.axis_index("xh")
    bricks = mine.reshape(4, planes, 2, ny * (2 * comps + 1), nz)
    near = lax.dynamic_index_in_dim(bricks, 1 - half_at, 2, keepdims=False)
    beyond = lax.dynamic_slice(
        bricks, (2 * (1 - half_at), 0, half_at, 0, 0), (2, planes, 1) + bricks.shape[3:]
    )
    part = jnp.concatenate([near, beyond[:, :, 0]], axis=0).reshape(-1, nz)
    mine = mine.reshape(half * (2 * comps + 1), nz)
    blocks, cores = lax.axis_size(("xh", "xl")), lax.axis_size("c")
    chips = [(i, blocks - 1 - i) for i in range(blocks)]
    across = [
        (i * cores + c, j * cores + cores - 1 - c) for i, j in chips for c in range(cores)
    ]
    part_mate = lax.ppermute(part, ("xh", "xl", "c"), across)
    part = lax.ppermute(part, ("xh", "xl"), chips)
    mate = lax.ppermute(mine, "c", [(0, 1), (1, 0)])

    terms = jnp.asarray(pair_table(window))
    weights = jnp.asarray(np.array(chebyshev_terms(SWEEPS - 1)[:2], np.float32))

    def state(places):
        return [(places, 2 * comps, ny, nz)] * 4 + [(places, ny, nz)]

    def flux(planes):
        return pltpu.VMEM((planes + 1, 2 * comps, ny, nz), f32)

    inner = pl.pallas_call(
        inner_kernel,
        out_shape=[jax.ShapeDtypeStruct(shape, f32) for shape in state(HALF + 3 * GUARD)],
        in_specs=[smem, smem, vmem, vmem],
        out_specs=[vmem] * 5,
        scratch_shapes=[flux(INNER)] * 2,
        compiler_params=params,
        cost_estimate=pl.CostEstimate(
            flops=10**10, bytes_accessed=2 * 10**7, transcendentals=0
        ),
        name="inner",
    )(terms, weights, mine, mate)
    solved = pl.pallas_call(
        outer_kernel,
        out_shape=jax.ShapeDtypeStruct((half * 2 * comps, nz), f32),
        in_specs=[smem, smem] + [vmem] * 7,
        out_specs=vmem,
        scratch_shapes=[pltpu.VMEM(shape, f32) for shape in state(HALF + REACH + 2 * GUARD)]
        + [flux(OUTER)] * 2,
        compiler_params=params,
        name="outer",
    )(terms, weights, part, part_mate, *inner)

    back = lax.all_to_all(
        solved.reshape(half, 1, 2 * comps * nz), GROUP, 0, 0, tiled=True
    ).reshape(half * 2 * comps, nz)

    pencil = pl.pallas_call(
        inverse_kernel,
        out_shape=jax.ShapeDtypeStruct((groups, comps * steps, nz), f32),
        in_specs=[vmem, vmem],
        out_specs=vmem,
        compiler_params=params,
        name="inverse",
    )(back, both)

    home = lax.all_to_all(pencil, TM, 0, 0, tiled=True)

    return pl.pallas_call(
        unpack_kernel,
        out_shape=jax.ShapeDtypeStruct(forcing.shape, f32),
        grid=(planes,),
        in_specs=[pl.BlockSpec((ny * comps * steps, nz), lambda p: (p, 0))],
        out_specs=plane_of,
        compiler_params=params,
        name="unpack",
    )(home.reshape(groups * comps * steps, nz))


def solution(mesh):
    names = ("yh", "z", "xh", "xl", "yl", "c")
    fine = Mesh(mesh.devices.reshape(2, 8, 2, 2, 4, 2), names)
    space = ("xh", "xl", "yl", "c")
    placed = (
        P(TM, None, space, None, None),
        P(None, space, None, None),
        P(TM, None, space, None, None),
        P(space, None, None),
        P(),
    )
    return jax.shard_map(
        per_device,
        mesh=fine,
        in_specs=placed,
        out_specs=P(TM, None, space, None, None),
        check_vma=False,
    )
```

```python
import functools
import itertools
import math

import jax
import jax.numpy as jnp
import numpy as np
from jax import lax
from jax.experimental import pallas as pl
from jax.experimental.pallas import tpu as pltpu
from jax.sharding import Mesh
from jax.sharding import PartitionSpec as P

SWEEPS = 12
ALPHA = 0.1
LOWER = 0.02
UPPER = 1.0
SIGMA_TOP = 4.0
CURL_TOP = 12.0

TM = ("yh", "z")
GROUP = ("yl", "yh", "xl", "z")
HALF = 32
REACH = 24
STRIPE = 2
GUARD = 1
INNER = 8
OUTER = 12
EARLY = 5


def pair_index():
    index = 0
    for name in GROUP:
        at = lax.axis_index(name)
        if name == "xl":
            at = (at + lax.axis_index("xh")) % 2
        index = index * lax.axis_size(name) + at
    return index


def place_of(block):
    flip = lax.axis_index("xh")
    return block + (flip if block % 2 == 0 else -flip)


def tables(window):
    gamma = ALPHA ** (1.0 / window)
    half = window // 2
    pairs = np.arange(half)
    freqs = np.concatenate([pairs, np.where(pairs == 0, half, window - pairs)])
    moments = np.arange(window)
    angle = 2.0 * math.pi * (freqs[:, None] * moments[None, :] % window) / window
    cas = np.cos(angle) + np.sin(angle)
    forward = cas * gamma ** moments[None, :]
    inverse = cas.T * gamma ** (-moments[:, None]) / window
    return forward.astype(np.float32), inverse.astype(np.float32)


def product(table, values):
    def parts(array):
        high = array.astype(jnp.bfloat16)
        return high, (array - high.astype(jnp.float32)).astype(jnp.bfloat16)

    (table_high, table_low), (high, low) = parts(table), parts(values)
    return jnp.dot(
        jnp.concatenate([table_high, table_low, table_high], axis=1),
        jnp.concatenate([high, high, low], axis=0),
        preferred_element_type=jnp.float32,
    )


def pair_table(window):
    gamma = ALPHA ** (1.0 / window)
    pairs = np.arange(window // 2)
    theta = 2.0 * math.pi * pairs / window
    plain = 1.0 - gamma * np.cos(theta)
    p_plus = np.where(pairs == 0, 1.0 - gamma, plain)
    p_minus = np.where(pairs == 0, 1.0 + gamma, plain)
    q_term = np.where(pairs == 0, 0.0, gamma * np.sin(theta))
    bound = np.sqrt(np.maximum(p_plus, p_minus) ** 2 + q_term**2) * SIGMA_TOP + CURL_TOP
    return np.stack([p_plus, p_minus, q_term, 1.0 / bound**2]).astype(np.float32)


def chebyshev_terms(count):
    center = (UPPER + LOWER) / 2.0
    radius = (UPPER - LOWER) / 2.0
    spread_ratio = center / radius
    weight_now = 1.0 / spread_ratio
    carry_terms, push_terms = ([], [])
    for _ in range(count):
        weight_next = 1.0 / (2.0 * spread_ratio - weight_now)
        carry_terms.append(weight_next * weight_now)
        push_terms.append(2.0 * weight_next / radius)
        weight_now = weight_next
    return (carry_terms, push_terms, center)


def material(region, cond):
    return jnp.where(
        region == 0,
        cond[0],
        jnp.where(region == 1, cond[1], jnp.where(region == 2, cond[2], 0.0)),
    )


def pack_kernel(cond, forcing, start, latest, region, out):
    steps, comps, _, ny, _ = forcing.shape
    rows = out.shape[0] // ny
    is_first = (lax.axis_index("yh") == 0) & (lax.axis_index("z") == 0)
    sigma = material(region[0], cond)
    for c in range(comps):
        head = forcing[0, c, 0]
        head = head + jnp.where(is_first, sigma * start[c, 0], 0.0)
        out[pl.ds(c * steps, ny, stride=rows), :] = head
        for b in range(1, steps):
            out[pl.ds(c * steps + b, ny, stride=rows), :] = forcing[b, c, 0]
        out[pl.ds(comps * steps + c, ny, stride=rows), :] = -ALPHA * (sigma * latest[0, c, 0])
    for pad in range(comps * steps + comps, rows):
        out[pl.ds(pad, ny, stride=rows), :] = jnp.zeros_like(sigma)


def forward_kernel(cond, got, tables, region, out):
    groups, _, nz = got.shape
    window = tables.shape[1]
    steps = window // groups
    comps = 3
    half = window // 2
    head = lax.broadcasted_iota(jnp.int32, (window, nz), 0) == 0
    parts = []
    for c in range(comps):
        part = got[:, c * steps : (c + 1) * steps, :].reshape(window, nz)
        row = got[groups - 1, comps * steps + c : comps * steps + c + 1, :]
        parts.append(part + jnp.where(head, row, 0.0))
    spectrum = product(tables[0], jnp.concatenate(parts, axis=1))
    width = comps * nz
    line = region[lax.axis_index("yh"), pl.ds(lax.axis_index("z"), 1), :]
    weight = jnp.broadcast_to(material(line, cond), (8, nz))
    cols = out.shape[0] // half
    for at in range(half // 8):
        begin = place_of(at) * 8
        for k in range(2 * comps):
            block = spectrum[
                k // comps * half + at * 8 : k // comps * half + at * 8 + 8,
                k % comps * nz : (k % comps + 1) * nz,
            ]
            out[pl.ds(begin * cols + k, 8, stride=cols), :] = block
        out[pl.ds(begin * cols + 2 * comps, 8, stride=cols), :] = weight


def inverse_kernel(got, tables, out):
    groups, rows, nz = out.shape
    _, window, _ = tables.shape
    half = window // 2
    steps = window // groups
    cols = got.shape[0] // half
    def member(f):
        return jnp.concatenate(
            [
                jnp.concatenate(
                    [
                        got[pl.ds(place_of(at) * 8 * cols + k, 8, stride=cols), :]
                        for at in range(half // 8)
                    ],
                    axis=0,
                )
                for k in range(f * cols // 2, (f + 1) * cols // 2)
            ],
            axis=1,
        )

    result = product(tables[1], jnp.concatenate([member(0), member(1)], axis=0))
    for c in range(rows // steps):
        out[:, c * steps : (c + 1) * steps, :] = result[:, c * nz : (c + 1) * nz].reshape(
            groups, steps, nz
        )


def unpack_kernel(got, out):
    steps, comps, _, ny, _ = out.shape
    rows = got.shape[0] // ny
    for c in range(comps):
        for b in range(steps):
            out[b, c, 0] = got[pl.ds(c * steps + b, ny, stride=rows), :]


def operator(terms, sigma):
    ny, nz = sigma.shape[1:]
    pair = pair_index()
    p_plus, p_minus, q_term = terms[0, pair], terms[1, pair], terms[2, pair]

    row = lax.broadcasted_iota(jnp.int32, (ny, nz), 0)
    lane = lax.broadcasted_iota(jnp.int32, (ny, nz), 1)
    row_first, row_last = row == 0, row == ny - 1
    lane_first, lane_last = lane == 0, lane == nz - 1

    def ahead_y(f):
        return jnp.where(row_last, 0.0, pltpu.roll(f, ny - 1, 0))

    def ahead_z(f):
        return jnp.where(lane_last, 0.0, pltpu.roll(f, nz - 1, 1))

    def behind_y(f):
        return jnp.where(row_first, 0.0, pltpu.roll(f, 1, 0))

    def behind_z(f):
        return jnp.where(lane_first, 0.0, pltpu.roll(f, 1, 1))

    def curls(now, after):
        flux = []
        for f in (0, 3):
            ex, ey, ez = now[f : f + 3]
            _, ey_after, ez_after = after[f : f + 3]
            flux += [
                (ahead_y(ez) - ez) - (ahead_z(ey) - ey),
                (ahead_z(ex) - ex) - (ez_after - ez),
                (ey_after - ey) - (ahead_y(ex) - ex),
            ]
        return flux

    def tails(now, after):
        flux = []
        for f in (0, 3):
            ex, ey, ez = now[f : f + 3]
            _, ey_after, ez_after = after[f : f + 3]
            flux += [
                (ahead_z(ex) - ex) - (ez_after - ez),
                (ey_after - ey) - (ahead_y(ex) - ex),
            ]
        return flux

    def adjoints(flux, before):
        field = []
        for f, g in ((0, 0), (3, 2)):
            bx, by, bz = flux[f : f + 3]
            by_before, bz_before = before[g : g + 2]
            field += [
                (behind_z(by) - by) - (behind_y(bz) - bz),
                (bz_before - bz) - (behind_z(bx) - bx),
                (behind_y(bx) - bx) - (by_before - by),
            ]
        return field

    def add_couple(field, values, weight, sign):
        sp, sm, sq = weight * p_plus, weight * p_minus, weight * (sign * q_term)
        return [
            field[c] + (sp * values[c] - sq * values[3 + c]) for c in range(3)
        ] + [field[3 + c] + (sm * values[3 + c] + sq * values[c]) for c in range(3)]

    def lift(flux, source, begin, edge):
        now = load(source, begin)
        before = tails(load(source, begin - 1), now)
        for k, v in zip((1, 2, 4, 5), before):
            flux[0, k] = v if edge is None else jnp.where(edge, 0.0, v)
        for u in range(flux.shape[0] - 1):
            after = load(source, begin + u + 1)
            for k, v in enumerate(curls(now, after)):
                flux[u + 1, k] = v
            now = after

    def drop(flux, source, begin, sign, finish):
        before = [flux[0, k] for k in (1, 2, 4, 5)]
        for u in range(flux.shape[0] - 1):
            i = begin + u
            now = [flux[u + 1, k] for k in range(6)]
            value = adjoints(now, before)
            finish(i, add_couple(value, load(source, i), sigma[i + GUARD], sign))
            before = [now[k] for k in (1, 2, 4, 5)]

    return lift, drop


def load(ref, at):
    return [ref[at + GUARD, k] for k in range(6)]


def store(ref, at, values):
    for k in range(6):
        ref[at + GUARD, k] = values[k]


def finishers(terms, field, first, resid, total, place):
    inv_scale = terms[3, pair_index()]
    center = chebyshev_terms(SWEEPS - 1)[2]

    def begin_with(i, value):
        step = [v * (inv_scale * (1.0 / center)) for v in value]
        store(resid, place(i), value)
        store(field, place(i), step)
        store(total, place(i), step)

    def keep_first(i, value):
        store(first, place(i), value)

    def update(carry_term, push_term):
        push_term = push_term * inv_scale

        def do(i, value):
            rest = [r - v for r, v in zip(load(resid, i), value)]
            step = [carry_term * d + push_term * r for d, r in zip(load(field, i), rest)]
            store(resid, place(i), rest)
            store(field, place(i), step)
            store(total, place(i), [x + d for x, d in zip(load(total, i), step)])

        return do

    return begin_with, keep_first, update


def fill(first, sigma, source, rows, begins):
    ny, nz = sigma.shape[1:]
    cols = 7
    for row, (x_at, y_at, p) in rows:
        i = begins[x_at] + 2 * STRIPE * y_at + p
        parts = [source[pl.ds(row * cols * ny + k, ny, stride=cols), :] for k in range(cols)]
        store(first, i, parts[:6])
        sigma[i + GUARD] = parts[6]


def brick_rows():
    order = itertools.product(range(4), range(STRIPE), range(2))
    return [(row, (x_at, y_at, p)) for row, (y_at, p, x_at) in enumerate(order)]


def halo_rows():
    order = [(0, y_at, p) for y_at in range(4) for p in range(STRIPE)]
    order += [(1, y_at, p) for y_at in range(2) for p in range(STRIPE)]
    return list(enumerate(order))


def inner_kernel(sweeps, terms, weights, *refs):
    *given, field, first, resid, total, sigma, flux_a, flux_b = refs
    ny, nz = sigma.shape[1:]
    blank = jnp.zeros((ny, nz), jnp.float32)
    half_at, core_at = lax.axis_index("xh"), lax.axis_index("c")
    lift, drop = operator(terms, sigma)
    size = flux_a.shape[0] - 1

    begins_all = sweeps.start == 0
    for ref in (first, field):
        store(ref, -1, [blank] * 6)
        store(ref, HALF, [blank] * 6)
    if begins_all:
        for source, core in zip(given, (core_at, 1 - core_at)):
            begin = STRIPE * core
            fill(first, sigma, source, brick_rows(), (begin, begin + HALF // 2))
    else:
        for ref, old in zip((field, first, resid, total), given):
            for i in range(HALF):
                store(ref, i, load(old, i))
        for i in range(HALF):
            sigma[i + GUARD] = given[4][i + GUARD]

    def begin_of(level):
        count = (HALF - level + size - 1) // size
        return half_at * (HALF - count * size), count

    def run(level, flux, source, sign, finish, other_flux, other_source, beside):
        low, count = begin_of(level)
        other_low, _ = begin_of(level + 1)

        def at_edge(begin):
            return (begin == 0) & (half_at == 0)

        def step(t, _):
            begin = low + t * size
            drop(flux, source, begin, sign, finish)
            lift(flux, source, begin + size, None)
            return 0

        lax.fori_loop(0, count - 1, step, 0)
        if beside:
            lift(other_flux, other_source, other_low, at_edge(other_low))
        drop(flux, source, low + (count - 1) * size, sign, finish)
        if not beside:
            lift(other_flux, other_source, other_low, at_edge(other_low))

    def placed(level):
        low, high = half_at * level, HALF - level + half_at * level
        return lambda i: jnp.where((i >= low) & (i < high), i, HALF + 1)

    begin_with, _, _ = finishers(terms, field, first, resid, total, placed(1))
    if begins_all:
        lift(flux_b, first, begin_of(1)[0], half_at == 0)
        run(1, flux_b, first, -1.0, begin_with, flux_a, field, True)
    else:
        low, _ = begin_of(2 + 2 * sweeps.start)
        lift(flux_a, field, low, (low == 0) & (half_at == 0))

    def sweep(s, beside):
        _, keep_first, _ = finishers(terms, field, first, resid, total, placed(2 + 2 * s))
        _, _, update = finishers(terms, field, first, resid, total, placed(3 + 2 * s))
        run(2 + 2 * s, flux_a, field, 1.0, keep_first, flux_b, first, beside)
        run(
            3 + 2 * s,
            flux_b,
            first,
            -1.0,
            update(weights[0, s], weights[1, s]),
            flux_a,
            field,
            beside,
        )

    def early(s, _):
        sweep(s, True)
        return 0

    def late(s, _):
        sweep(s, False)
        return 0

    apart = max(s for s in range(SWEEPS) if (HALF - 4 - 2 * s + size - 1) // size >= 3) + 1
    between = min(max(apart, sweeps.start), sweeps.stop)
    lax.fori_loop(sweeps.start, between, early, 0)
    lax.fori_loop(between, sweeps.stop, late, 0)


def outer_kernel(
    terms, weights, part, part_mate, *refs
):
    given, out, state, (flux_a, flux_b) = refs[:5], refs[5], refs[6:11], refs[11:]
    field, first, resid, total, sigma = state
    ny, nz = sigma.shape[1:]
    half_at, core_at = lax.axis_index("xh"), lax.axis_index("c")
    lift, drop = operator(terms, sigma)
    size = flux_a.shape[0] - 1

    own_low = REACH * half_at
    for ref, old in zip(state[:4], given[:4]):
        for i in range(HALF):
            store(ref, own_low + i, load(old, i))
    for i in range(HALF):
        sigma[own_low + i + GUARD] = given[4][i + GUARD]
    halo_low = HALF * (1 - half_at)
    for source, core in ((part, core_at), (part_mate, 1 - core_at)):
        begin = halo_low + STRIPE * core
        whole_x = begin + (REACH - HALF // 2) * half_at
        half_x = begin + HALF // 2 * (1 - half_at)
        fill(first, sigma, source, halo_rows(), (whole_x, half_x))

    def begin_of(level, turn):
        low = jnp.where(half_at == 0, HALF - level, level)
        return low + jnp.where(half_at == 0, turn, 1 - turn) * size

    def run(level, source, sign, finish, other_source):
        drop(flux_a, source, begin_of(level, 0), sign, finish)
        lift(flux_b, source, begin_of(level, 1), None)
        lift(flux_a, other_source, begin_of(level + 1, 0), None)
        drop(flux_b, source, begin_of(level, 1), sign, finish)

    begin_with, keep_first, update = finishers(terms, field, first, resid, total, lambda i: i)
    lift(flux_a, first, begin_of(1, 0), None)
    run(1, first, -1.0, begin_with, field)

    def sweep(s, _):
        run(2 + 2 * s, field, 1.0, keep_first, first)
        run(3 + 2 * s, first, -1.0, update(weights[0, s], weights[1, s]), field)
        return 0

    lax.fori_loop(0, SWEEPS - 1, sweep, 0)

    own_begin = own_low + STRIPE * core_at
    for row, (x_at, y_at, p) in brick_rows():
        i = own_begin + HALF // 2 * x_at + 2 * STRIPE * y_at + p
        for k, v in enumerate(load(total, i)):
            out[pl.ds(row * 6 * ny + k, ny, stride=6), :] = v


def per_device(forcing, start_field, iterate, region, conductance):
    steps, comps, planes, ny, nz = forcing.shape
    groups = lax.axis_size(TM)
    window = steps * groups
    half = window // 2
    both = jnp.asarray(np.stack(tables(window)))
    vmem = pl.BlockSpec(memory_space=pltpu.VMEM)
    smem = pl.BlockSpec(memory_space=pltpu.SMEM)
    f32 = jnp.float32
    params = pltpu.CompilerParams(vmem_limit_bytes=14 * 1024 * 1024)

    rows = comps * steps + 8
    plane_of = pl.BlockSpec((steps, comps, 1, ny, nz), lambda p: (0, 0, p, 0, 0))
    packed = pl.pallas_call(
        pack_kernel,
        out_shape=jax.ShapeDtypeStruct((groups * rows, nz), f32),
        grid=(planes,),
        in_specs=[
            smem,
            plane_of,
            pl.BlockSpec((comps, 1, ny, nz), lambda p: (0, p, 0, 0)),
            pl.BlockSpec((1, comps, 1, ny, nz), lambda p: (steps - 1, 0, p, 0, 0)),
            pl.BlockSpec((1, ny, nz), lambda p: (p, 0, 0)),
        ],
        out_specs=pl.BlockSpec((ny * rows, nz), lambda p: (p, 0)),
        compiler_params=pltpu.CompilerParams(vmem_limit_bytes=60 * 1024 * 1024),
        name="pack",
    )(conductance, forcing, start_field, iterate, region)

    got = lax.all_to_all(packed.reshape(groups, rows, nz), TM, 0, 0, tiled=True)

    spectrum = pl.pallas_call(
        forward_kernel,
        out_shape=jax.ShapeDtypeStruct((half * (2 * comps + 1), nz), f32),
        in_specs=[smem, vmem, vmem, vmem],
        out_specs=vmem,
        compiler_params=params,
        name="forward",
    )(conductance, got, both, region)

    mine = lax.all_to_all(
        spectrum.reshape(half, 1, (2 * comps + 1) * nz), GROUP, 0, 0, tiled=True
    )

    half_at = lax.axis_index("xh")
    bricks = mine.reshape(4, planes, 2, ny * (2 * comps + 1), nz)
    near = lax.dynamic_index_in_dim(bricks, 1 - half_at, 2, keepdims=False)
    beyond = lax.dynamic_slice(
        bricks, (2 * (1 - half_at), 0, half_at, 0, 0), (2, planes, 1) + bricks.shape[3:]
    )
    part = jnp.concatenate([near, beyond[:, :, 0]], axis=0).reshape(-1, nz)
    mine = mine.reshape(half * (2 * comps + 1), nz)
    blocks = lax.axis_size(("xh", "xl"))
    part = lax.ppermute(part, ("xh", "xl"), [(i, blocks - 1 - i) for i in range(blocks)])
    mate = lax.ppermute(mine, "c", [(0, 1), (1, 0)])

    terms = jnp.asarray(pair_table(window))
    weights = jnp.asarray(np.array(chebyshev_terms(SWEEPS - 1)[:2], np.float32))

    def state(places):
        return [(places, 2 * comps, ny, nz)] * 4 + [(places, ny, nz)]

    def flux(planes):
        return pltpu.VMEM((planes + 1, 2 * comps, ny, nz), f32)

    def inner(sweeps, given):
        return pl.pallas_call(
            functools.partial(inner_kernel, sweeps),
            out_shape=[jax.ShapeDtypeStruct(shape, f32) for shape in state(HALF + 3 * GUARD)],
            in_specs=[smem, smem] + [vmem] * len(given),
            out_specs=[vmem] * 5,
            scratch_shapes=[flux(INNER)] * 2,
            compiler_params=params,
            cost_estimate=pl.CostEstimate(
                flops=10**10, bytes_accessed=2 * 10**7, transcendentals=0
            ),
            name="inner",
        )(terms, weights, *given)

    early = inner(range(0, EARLY), (mine, mate))
    part, early = lax.optimization_barrier((part, early))
    part_mate = lax.ppermute(part, "c", [(0, 1), (1, 0)])
    late = inner(range(EARLY, SWEEPS - 1), early)
    solved = pl.pallas_call(
        outer_kernel,
        out_shape=jax.ShapeDtypeStruct((half * 2 * comps, nz), f32),
        in_specs=[smem, smem] + [vmem] * 7,
        out_specs=vmem,
        scratch_shapes=[pltpu.VMEM(shape, f32) for shape in state(HALF + REACH + 2 * GUARD)]
        + [flux(OUTER)] * 2,
        compiler_params=params,
        name="outer",
    )(terms, weights, part, part_mate, *late)

    back = lax.all_to_all(
        solved.reshape(half, 1, 2 * comps * nz), GROUP, 0, 0, tiled=True
    ).reshape(half * 2 * comps, nz)

    pencil = pl.pallas_call(
        inverse_kernel,
        out_shape=jax.ShapeDtypeStruct((groups, comps * steps, nz), f32),
        in_specs=[vmem, vmem],
        out_specs=vmem,
        compiler_params=params,
        name="inverse",
    )(back, both)

    home = lax.all_to_all(pencil, TM, 0, 0, tiled=True)

    return pl.pallas_call(
        unpack_kernel,
        out_shape=jax.ShapeDtypeStruct(forcing.shape, f32),
        grid=(planes,),
        in_specs=[pl.BlockSpec((ny * comps * steps, nz), lambda p: (p, 0))],
        out_specs=plane_of,
        compiler_params=params,
        name="unpack",
    )(home.reshape(groups * comps * steps, nz))


def solution(mesh):
    names = ("yh", "z", "xh", "xl", "yl", "c")
    fine = Mesh(mesh.devices.reshape(2, 8, 2, 2, 4, 2), names)
    space = ("xh", "xl", "yl", "c")
    placed = (
        P(TM, None, space, None, None),
        P(None, space, None, None),
        P(TM, None, space, None, None),
        P(space, None, None),
        P(),
    )
    return jax.shard_map(
        per_device,
        mesh=fine,
        in_specs=placed,
        out_specs=P(TM, None, space, None, None),
        check_vma=False,
    )
```

```python
import functools
import itertools
import math

import jax
import jax.numpy as jnp
import numpy as np
from jax import lax
from jax.experimental import pallas as pl
from jax.experimental.pallas import tpu as pltpu
from jax.sharding import Mesh
from jax.sharding import PartitionSpec as P

SWEEPS = 12
ALPHA = 0.1
LOWER = 0.02
UPPER = 1.0
SIGMA_TOP = 4.0
CURL_TOP = 12.0

TM = ("yh", "z")
GROUP = ("yl", "yh", "xl", "z")
HALF = 32
REACH = 24
STRIPE = 2
GUARD = 1
INNER = 8
OUTER = 12
EARLY = 8


def pair_index():
    index = 0
    for name in GROUP:
        at = lax.axis_index(name)
        if name == "xl":
            at = (at + lax.axis_index("xh")) % 2
        index = index * lax.axis_size(name) + at
    return index


def place_of(block):
    flip = lax.axis_index("xh")
    return block + (flip if block % 2 == 0 else -flip)


def tables(window):
    gamma = ALPHA ** (1.0 / window)
    half = window // 2
    pairs = np.arange(half)
    freqs = np.concatenate([pairs, np.where(pairs == 0, half, window - pairs)])
    moments = np.arange(window)
    angle = 2.0 * math.pi * (freqs[:, None] * moments[None, :] % window) / window
    cas = np.cos(angle) + np.sin(angle)
    forward = cas * gamma ** moments[None, :]
    inverse = cas.T * gamma ** (-moments[:, None]) / window
    return forward.astype(np.float32), inverse.astype(np.float32)


def product(table, values):
    def parts(array):
        high = array.astype(jnp.bfloat16)
        return high, (array - high.astype(jnp.float32)).astype(jnp.bfloat16)

    (table_high, table_low), (high, low) = parts(table), parts(values)
    return jnp.dot(
        jnp.concatenate([table_high, table_low, table_high], axis=1),
        jnp.concatenate([high, high, low], axis=0),
        preferred_element_type=jnp.float32,
    )


def pair_table(window):
    gamma = ALPHA ** (1.0 / window)
    pairs = np.arange(window // 2)
    theta = 2.0 * math.pi * pairs / window
    plain = 1.0 - gamma * np.cos(theta)
    p_plus = np.where(pairs == 0, 1.0 - gamma, plain)
    p_minus = np.where(pairs == 0, 1.0 + gamma, plain)
    q_term = np.where(pairs == 0, 0.0, gamma * np.sin(theta))
    bound = np.sqrt(np.maximum(p_plus, p_minus) ** 2 + q_term**2) * SIGMA_TOP + CURL_TOP
    return np.stack([p_plus, p_minus, q_term, 1.0 / bound**2]).astype(np.float32)


def chebyshev_terms(count):
    center = (UPPER + LOWER) / 2.0
    radius = (UPPER - LOWER) / 2.0
    spread_ratio = center / radius
    weight_now = 1.0 / spread_ratio
    carry_terms, push_terms = ([], [])
    for _ in range(count):
        weight_next = 1.0 / (2.0 * spread_ratio - weight_now)
        carry_terms.append(weight_next * weight_now)
        push_terms.append(2.0 * weight_next / radius)
        weight_now = weight_next
    return (carry_terms, push_terms, center)


def material(region, cond):
    return jnp.where(
        region == 0,
        cond[0],
        jnp.where(region == 1, cond[1], jnp.where(region == 2, cond[2], 0.0)),
    )


def pack_kernel(cond, forcing, start, latest, region, out):
    steps, comps, _, ny, _ = forcing.shape
    rows = out.shape[0] // ny
    is_first = (lax.axis_index("yh") == 0) & (lax.axis_index("z") == 0)
    sigma = material(region[0], cond)
    for c in range(comps):
        head = forcing[0, c, 0]
        head = head + jnp.where(is_first, sigma * start[c, 0], 0.0)
        out[pl.ds(c * steps, ny, stride=rows), :] = head
        for b in range(1, steps):
            out[pl.ds(c * steps + b, ny, stride=rows), :] = forcing[b, c, 0]
        out[pl.ds(comps * steps + c, ny, stride=rows), :] = -ALPHA * (sigma * latest[0, c, 0])
    for pad in range(comps * steps + comps, rows):
        out[pl.ds(pad, ny, stride=rows), :] = jnp.zeros_like(sigma)


def forward_kernel(cond, got, tables, region, out):
    groups, _, nz = got.shape
    window = tables.shape[1]
    steps = window // groups
    comps = 3
    half = window // 2
    head = lax.broadcasted_iota(jnp.int32, (window, nz), 0) == 0
    parts = []
    for c in range(comps):
        part = got[:, c * steps : (c + 1) * steps, :].reshape(window, nz)
        row = got[groups - 1, comps * steps + c : comps * steps + c + 1, :]
        parts.append(part + jnp.where(head, row, 0.0))
    spectrum = product(tables[0], jnp.concatenate(parts, axis=1))
    width = comps * nz
    line = region[lax.axis_index("yh"), pl.ds(lax.axis_index("z"), 1), :]
    weight = jnp.broadcast_to(material(line, cond), (8, nz))
    cols = out.shape[0] // half
    for at in range(half // 8):
        begin = place_of(at) * 8
        for k in range(2 * comps):
            block = spectrum[
                k // comps * half + at * 8 : k // comps * half + at * 8 + 8,
                k % comps * nz : (k % comps + 1) * nz,
            ]
            out[pl.ds(begin * cols + k, 8, stride=cols), :] = block
        out[pl.ds(begin * cols + 2 * comps, 8, stride=cols), :] = weight


def inverse_kernel(got, tables, out):
    groups, rows, nz = out.shape
    _, window, _ = tables.shape
    half = window // 2
    steps = window // groups
    cols = got.shape[0] // half
    def member(f):
        return jnp.concatenate(
            [
                jnp.concatenate(
                    [
                        got[pl.ds(place_of(at) * 8 * cols + k, 8, stride=cols), :]
                        for at in range(half // 8)
                    ],
                    axis=0,
                )
                for k in range(f * cols // 2, (f + 1) * cols // 2)
            ],
            axis=1,
        )

    result = product(tables[1], jnp.concatenate([member(0), member(1)], axis=0))
    for c in range(rows // steps):
        out[:, c * steps : (c + 1) * steps, :] = result[:, c * nz : (c + 1) * nz].reshape(
            groups, steps, nz
        )


def unpack_kernel(got, out):
    steps, comps, _, ny, _ = out.shape
    rows = got.shape[0] // ny
    for c in range(comps):
        for b in range(steps):
            out[b, c, 0] = got[pl.ds(c * steps + b, ny, stride=rows), :]


def operator(terms, sigma):
    ny, nz = sigma.shape[1:]
    pair = pair_index()
    p_plus, p_minus, q_term = terms[0, pair], terms[1, pair], terms[2, pair]

    row = lax.broadcasted_iota(jnp.int32, (ny, nz), 0)
    lane = lax.broadcasted_iota(jnp.int32, (ny, nz), 1)
    row_first, row_last = row == 0, row == ny - 1
    lane_first, lane_last = lane == 0, lane == nz - 1

    def ahead_y(f):
        return jnp.where(row_last, 0.0, pltpu.roll(f, ny - 1, 0))

    def ahead_z(f):
        return jnp.where(lane_last, 0.0, pltpu.roll(f, nz - 1, 1))

    def behind_y(f):
        return jnp.where(row_first, 0.0, pltpu.roll(f, 1, 0))

    def behind_z(f):
        return jnp.where(lane_first, 0.0, pltpu.roll(f, 1, 1))

    def curls(now, after):
        flux = []
        for f in (0, 3):
            ex, ey, ez = now[f : f + 3]
            _, ey_after, ez_after = after[f : f + 3]
            flux += [
                (ahead_y(ez) - ez) - (ahead_z(ey) - ey),
                (ahead_z(ex) - ex) - (ez_after - ez),
                (ey_after - ey) - (ahead_y(ex) - ex),
            ]
        return flux

    def tails(now, after):
        flux = []
        for f in (0, 3):
            ex, ey, ez = now[f : f + 3]
            _, ey_after, ez_after = after[f : f + 3]
            flux += [
                (ahead_z(ex) - ex) - (ez_after - ez),
                (ey_after - ey) - (ahead_y(ex) - ex),
            ]
        return flux

    def adjoints(flux, before):
        field = []
        for f, g in ((0, 0), (3, 2)):
            bx, by, bz = flux[f : f + 3]
            by_before, bz_before = before[g : g + 2]
            field += [
                (behind_z(by) - by) - (behind_y(bz) - bz),
                (bz_before - bz) - (behind_z(bx) - bx),
                (behind_y(bx) - bx) - (by_before - by),
            ]
        return field

    def add_couple(field, values, weight, sign):
        sp, sm, sq = weight * p_plus, weight * p_minus, weight * (sign * q_term)
        return [
            field[c] + (sp * values[c] - sq * values[3 + c]) for c in range(3)
        ] + [field[3 + c] + (sm * values[3 + c] + sq * values[c]) for c in range(3)]

    def lift(flux, source, begin, edge):
        now = load(source, begin)
        before = tails(load(source, begin - 1), now)
        for k, v in zip((1, 2, 4, 5), before):
            flux[0, k] = v if edge is None else jnp.where(edge, 0.0, v)
        for u in range(flux.shape[0] - 1):
            after = load(source, begin + u + 1)
            for k, v in enumerate(curls(now, after)):
                flux[u + 1, k] = v
            now = after

    def drop(flux, source, begin, sign, finish):
        before = [flux[0, k] for k in (1, 2, 4, 5)]
        for u in range(flux.shape[0] - 1):
            i = begin + u
            now = [flux[u + 1, k] for k in range(6)]
            value = adjoints(now, before)
            finish(i, add_couple(value, load(source, i), sigma[i + GUARD], sign))
            before = [now[k] for k in (1, 2, 4, 5)]

    return lift, drop


def load(ref, at):
    return [ref[at + GUARD, k] for k in range(6)]


def store(ref, at, values):
    for k in range(6):
        ref[at + GUARD, k] = values[k]


def finishers(terms, field, first, resid, total, place):
    inv_scale = terms[3, pair_index()]
    center = chebyshev_terms(SWEEPS - 1)[2]

    def begin_with(i, value):
        step = [v * (inv_scale * (1.0 / center)) for v in value]
        store(resid, place(i), value)
        store(field, place(i), step)
        store(total, place(i), step)

    def keep_first(i, value):
        store(first, place(i), value)

    def update(carry_term, push_term):
        push_term = push_term * inv_scale

        def do(i, value):
            rest = [r - v for r, v in zip(load(resid, i), value)]
            step = [carry_term * d + push_term * r for d, r in zip(load(field, i), rest)]
            store(resid, place(i), rest)
            store(field, place(i), step)
            store(total, place(i), [x + d for x, d in zip(load(total, i), step)])

        return do

    return begin_with, keep_first, update


def fill(first, sigma, source, rows, begins):
    ny, nz = sigma.shape[1:]
    cols = 7
    for row, (x_at, y_at, p) in rows:
        i = begins[x_at] + 2 * STRIPE * y_at + p
        parts = [source[pl.ds(row * cols * ny + k, ny, stride=cols), :] for k in range(cols)]
        store(first, i, parts[:6])
        sigma[i + GUARD] = parts[6]


def brick_rows():
    order = itertools.product(range(4), range(STRIPE), range(2))
    return [(row, (x_at, y_at, p)) for row, (y_at, p, x_at) in enumerate(order)]


def halo_rows():
    order = [(0, y_at, p) for y_at in range(4) for p in range(STRIPE)]
    order += [(1, y_at, p) for y_at in range(2) for p in range(STRIPE)]
    return list(enumerate(order))


def inner_kernel(sweeps, terms, weights, *refs):
    *given, field, first, resid, total, sigma, flux_a, flux_b = refs
    ny, nz = sigma.shape[1:]
    blank = jnp.zeros((ny, nz), jnp.float32)
    half_at, core_at = lax.axis_index("xh"), lax.axis_index("c")
    lift, drop = operator(terms, sigma)
    size = flux_a.shape[0] - 1

    begins_all = sweeps.start == 0
    for ref in (first, field):
        store(ref, -1, [blank] * 6)
        store(ref, HALF, [blank] * 6)
    if begins_all:
        for source, core in zip(given, (core_at, 1 - core_at)):
            begin = STRIPE * core
            fill(first, sigma, source, brick_rows(), (begin, begin + HALF // 2))
    else:
        for ref, old in zip((field, first, resid, total), given):
            for i in range(HALF):
                store(ref, i, load(old, i))
        for i in range(HALF):
            sigma[i + GUARD] = given[4][i + GUARD]

    def begin_of(level):
        count = (HALF - level + size - 1) // size
        return half_at * (HALF - count * size), count

    def run(level, flux, source, sign, finish, other_flux, other_source, beside):
        low, count = begin_of(level)
        other_low, _ = begin_of(level + 1)

        def at_edge(begin):
            return (begin == 0) & (half_at == 0)

        def step(t, _):
            begin = low + t * size
            drop(flux, source, begin, sign, finish)
            lift(flux, source, begin + size, None)
            return 0

        lax.fori_loop(0, count - 1, step, 0)
        if beside:
            lift(other_flux, other_source, other_low, at_edge(other_low))
        drop(flux, source, low + (count - 1) * size, sign, finish)
        if not beside:
            lift(other_flux, other_source, other_low, at_edge(other_low))

    def placed(level):
        low, high = half_at * level, HALF - level + half_at * level
        return lambda i: jnp.where((i >= low) & (i < high), i, HALF + 1)

    begin_with, _, _ = finishers(terms, field, first, resid, total, placed(1))
    if begins_all:
        lift(flux_b, first, begin_of(1)[0], half_at == 0)
        run(1, flux_b, first, -1.0, begin_with, flux_a, field, True)
    else:
        low, _ = begin_of(2 + 2 * sweeps.start)
        lift(flux_a, field, low, (low == 0) & (half_at == 0))

    def sweep(s, beside):
        _, keep_first, _ = finishers(terms, field, first, resid, total, placed(2 + 2 * s))
        _, _, update = finishers(terms, field, first, resid, total, placed(3 + 2 * s))
        run(2 + 2 * s, flux_a, field, 1.0, keep_first, flux_b, first, beside)
        run(
            3 + 2 * s,
            flux_b,
            first,
            -1.0,
            update(weights[0, s], weights[1, s]),
            flux_a,
            field,
            beside,
        )

    def early(s, _):
        sweep(s, True)
        return 0

    def late(s, _):
        sweep(s, False)
        return 0

    apart = max(s for s in range(SWEEPS) if (HALF - 4 - 2 * s + size - 1) // size >= 3) + 1
    between = min(max(apart, sweeps.start), sweeps.stop)
    lax.fori_loop(sweeps.start, between, early, 0)
    lax.fori_loop(between, sweeps.stop, late, 0)


def outer_kernel(
    terms, weights, part, part_mate, *refs
):
    given, out, state, (flux_a, flux_b) = refs[:5], refs[5], refs[6:11], refs[11:]
    field, first, resid, total, sigma = state
    ny, nz = sigma.shape[1:]
    half_at, core_at = lax.axis_index("xh"), lax.axis_index("c")
    lift, drop = operator(terms, sigma)
    size = flux_a.shape[0] - 1

    own_low = REACH * half_at
    for ref, old in zip(state[:4], given[:4]):
        for i in range(HALF):
            store(ref, own_low + i, load(old, i))
    for i in range(HALF):
        sigma[own_low + i + GUARD] = given[4][i + GUARD]
    halo_low = HALF * (1 - half_at)
    for source, core in ((part, core_at), (part_mate, 1 - core_at)):
        begin = halo_low + STRIPE * core
        whole_x = begin + (REACH - HALF // 2) * half_at
        half_x = begin + HALF // 2 * (1 - half_at)
        fill(first, sigma, source, halo_rows(), (whole_x, half_x))

    def begin_of(level, turn):
        low = jnp.where(half_at == 0, HALF - level, level)
        return low + jnp.where(half_at == 0, turn, 1 - turn) * size

    def run(level, source, sign, finish, other_source):
        drop(flux_a, source, begin_of(level, 0), sign, finish)
        lift(flux_b, source, begin_of(level, 1), None)
        lift(flux_a, other_source, begin_of(level + 1, 0), None)
        drop(flux_b, source, begin_of(level, 1), sign, finish)

    begin_with, keep_first, update = finishers(terms, field, first, resid, total, lambda i: i)
    lift(flux_a, first, begin_of(1, 0), None)
    run(1, first, -1.0, begin_with, field)

    def sweep(s, _):
        run(2 + 2 * s, field, 1.0, keep_first, first)
        run(3 + 2 * s, first, -1.0, update(weights[0, s], weights[1, s]), field)
        return 0

    lax.fori_loop(0, SWEEPS - 1, sweep, 0)

    own_begin = own_low + STRIPE * core_at
    for row, (x_at, y_at, p) in brick_rows():
        i = own_begin + HALF // 2 * x_at + 2 * STRIPE * y_at + p
        for k, v in enumerate(load(total, i)):
            out[pl.ds(row * 6 * ny + k, ny, stride=6), :] = v


def per_device(forcing, start_field, iterate, region, conductance):
    steps, comps, planes, ny, nz = forcing.shape
    groups = lax.axis_size(TM)
    window = steps * groups
    half = window // 2
    both = jnp.asarray(np.stack(tables(window)))
    vmem = pl.BlockSpec(memory_space=pltpu.VMEM)
    smem = pl.BlockSpec(memory_space=pltpu.SMEM)
    f32 = jnp.float32
    params = pltpu.CompilerParams(vmem_limit_bytes=14 * 1024 * 1024)

    rows = comps * steps + 8
    plane_of = pl.BlockSpec((steps, comps, 1, ny, nz), lambda p: (0, 0, p, 0, 0))
    packed = pl.pallas_call(
        pack_kernel,
        out_shape=jax.ShapeDtypeStruct((groups * rows, nz), f32),
        grid=(planes,),
        in_specs=[
            smem,
            plane_of,
            pl.BlockSpec((comps, 1, ny, nz), lambda p: (0, p, 0, 0)),
            pl.BlockSpec((1, comps, 1, ny, nz), lambda p: (steps - 1, 0, p, 0, 0)),
            pl.BlockSpec((1, ny, nz), lambda p: (p, 0, 0)),
        ],
        out_specs=pl.BlockSpec((ny * rows, nz), lambda p: (p, 0)),
        compiler_params=pltpu.CompilerParams(vmem_limit_bytes=60 * 1024 * 1024),
        name="pack",
    )(conductance, forcing, start_field, iterate, region)

    got = lax.all_to_all(packed.reshape(groups, rows, nz), TM, 0, 0, tiled=True)

    spectrum = pl.pallas_call(
        forward_kernel,
        out_shape=jax.ShapeDtypeStruct((half * (2 * comps + 1), nz), f32),
        in_specs=[smem, vmem, vmem, vmem],
        out_specs=vmem,
        compiler_params=params,
        name="forward",
    )(conductance, got, both, region)

    mine = lax.all_to_all(
        spectrum.reshape(half, 1, (2 * comps + 1) * nz), GROUP, 0, 0, tiled=True
    )

    half_at = lax.axis_index("xh")
    bricks = mine.reshape(4, planes, 2, ny * (2 * comps + 1), nz)
    near = lax.dynamic_index_in_dim(bricks, 1 - half_at, 2, keepdims=False)
    beyond = lax.dynamic_slice(
        bricks, (2 * (1 - half_at), 0, half_at, 0, 0), (2, planes, 1) + bricks.shape[3:]
    )
    part = jnp.concatenate([near, beyond[:, :, 0]], axis=0).reshape(-1, nz)
    mine = mine.reshape(half * (2 * comps + 1), nz)
    blocks = lax.axis_size(("xh", "xl"))
    part = lax.ppermute(part, ("xh", "xl"), [(i, blocks - 1 - i) for i in range(blocks)])
    mate = lax.ppermute(mine, "c", [(0, 1), (1, 0)])

    terms = jnp.asarray(pair_table(window))
    weights = jnp.asarray(np.array(chebyshev_terms(SWEEPS - 1)[:2], np.float32))

    def state(places):
        return [(places, 2 * comps, ny, nz)] * 4 + [(places, ny, nz)]

    def flux(planes):
        return pltpu.VMEM((planes + 1, 2 * comps, ny, nz), f32)

    def inner(sweeps, given):
        return pl.pallas_call(
            functools.partial(inner_kernel, sweeps),
            out_shape=[jax.ShapeDtypeStruct(shape, f32) for shape in state(HALF + 3 * GUARD)],
            in_specs=[smem, smem] + [vmem] * len(given),
            out_specs=[vmem] * 5,
            scratch_shapes=[flux(INNER)] * 2,
            compiler_params=params,
            cost_estimate=pl.CostEstimate(
                flops=10**10, bytes_accessed=2 * 10**7, transcendentals=0
            ),
            name="inner",
        )(terms, weights, *given)

    early = inner(range(0, EARLY), (mine, mate))
    part, early = lax.optimization_barrier((part, early))
    part_mate = lax.ppermute(part, "c", [(0, 1), (1, 0)])
    late = inner(range(EARLY, SWEEPS - 1), early)
    solved = pl.pallas_call(
        outer_kernel,
        out_shape=jax.ShapeDtypeStruct((half * 2 * comps, nz), f32),
        in_specs=[smem, smem] + [vmem] * 7,
        out_specs=vmem,
        scratch_shapes=[pltpu.VMEM(shape, f32) for shape in state(HALF + REACH + 2 * GUARD)]
        + [flux(OUTER)] * 2,
        compiler_params=params,
        name="outer",
    )(terms, weights, part, part_mate, *late)

    back = lax.all_to_all(
        solved.reshape(half, 1, 2 * comps * nz), GROUP, 0, 0, tiled=True
    ).reshape(half * 2 * comps, nz)

    pencil = pl.pallas_call(
        inverse_kernel,
        out_shape=jax.ShapeDtypeStruct((groups, comps * steps, nz), f32),
        in_specs=[vmem, vmem],
        out_specs=vmem,
        compiler_params=params,
        name="inverse",
    )(back, both)

    home = lax.all_to_all(pencil, TM, 0, 0, tiled=True)

    return pl.pallas_call(
        unpack_kernel,
        out_shape=jax.ShapeDtypeStruct(forcing.shape, f32),
        grid=(planes,),
        in_specs=[pl.BlockSpec((ny * comps * steps, nz), lambda p: (p, 0))],
        out_specs=plane_of,
        compiler_params=params,
        name="unpack",
    )(home.reshape(groups * comps * steps, nz))


def solution(mesh):
    names = ("yh", "z", "xh", "xl", "yl", "c")
    fine = Mesh(mesh.devices.reshape(2, 8, 2, 2, 4, 2), names)
    space = ("xh", "xl", "yl", "c")
    placed = (
        P(TM, None, space, None, None),
        P(None, space, None, None),
        P(TM, None, space, None, None),
        P(space, None, None),
        P(),
    )
    return jax.shard_map(
        per_device,
        mesh=fine,
        in_specs=placed,
        out_specs=P(TM, None, space, None, None),
        check_vma=False,
    )
```

```python
import functools
import itertools
import math

import jax
import jax.numpy as jnp
import numpy as np
from jax import lax
from jax.experimental import pallas as pl
from jax.experimental.pallas import tpu as pltpu
from jax.sharding import Mesh
from jax.sharding import PartitionSpec as P

SWEEPS = 12
ALPHA = 0.1
LOWER = 0.02
UPPER = 1.0
SIGMA_TOP = 4.0
CURL_TOP = 12.0

TM = ("yh", "z")
GROUP = ("yl", "yh", "xl", "z")
HALF = 32
REACH = 24
STRIPE = 2
GUARD = 1
INNER = 8
OUTER = 12
EARLY = 8


def pair_index():
    index = 0
    for name in GROUP:
        at = lax.axis_index(name)
        if name == "xl":
            at = (at + lax.axis_index("xh")) % 2
        index = index * lax.axis_size(name) + at
    return index


def place_of(block):
    flip = lax.axis_index("xh")
    return block + (flip if block % 2 == 0 else -flip)


def tables(window):
    gamma = ALPHA ** (1.0 / window)
    half = window // 2
    pairs = np.arange(half)
    freqs = np.concatenate([pairs, np.where(pairs == 0, half, window - pairs)])
    moments = np.arange(window)
    angle = 2.0 * math.pi * (freqs[:, None] * moments[None, :] % window) / window
    cas = np.cos(angle) + np.sin(angle)
    forward = cas * gamma ** moments[None, :]
    inverse = cas.T * gamma ** (-moments[:, None]) / window
    return forward.astype(np.float32), inverse.astype(np.float32)


def product(table, values):
    def parts(array):
        high = array.astype(jnp.bfloat16)
        return high, (array - high.astype(jnp.float32)).astype(jnp.bfloat16)

    (table_high, table_low), (high, low) = parts(table), parts(values)
    return jnp.dot(
        jnp.concatenate([table_high, table_low, table_high], axis=1),
        jnp.concatenate([high, high, low], axis=0),
        preferred_element_type=jnp.float32,
    )


def pair_table(window):
    gamma = ALPHA ** (1.0 / window)
    pairs = np.arange(window // 2)
    theta = 2.0 * math.pi * pairs / window
    plain = 1.0 - gamma * np.cos(theta)
    p_plus = np.where(pairs == 0, 1.0 - gamma, plain)
    p_minus = np.where(pairs == 0, 1.0 + gamma, plain)
    q_term = np.where(pairs == 0, 0.0, gamma * np.sin(theta))
    bound = np.sqrt(np.maximum(p_plus, p_minus) ** 2 + q_term**2) * SIGMA_TOP + CURL_TOP
    return np.stack([p_plus, p_minus, q_term, 1.0 / bound**2]).astype(np.float32)


def chebyshev_terms(count):
    center = (UPPER + LOWER) / 2.0
    radius = (UPPER - LOWER) / 2.0
    spread_ratio = center / radius
    weight_now = 1.0 / spread_ratio
    carry_terms, push_terms = ([], [])
    for _ in range(count):
        weight_next = 1.0 / (2.0 * spread_ratio - weight_now)
        carry_terms.append(weight_next * weight_now)
        push_terms.append(2.0 * weight_next / radius)
        weight_now = weight_next
    return (carry_terms, push_terms, center)


def material(region, cond):
    return jnp.where(
        region == 0,
        cond[0],
        jnp.where(region == 1, cond[1], jnp.where(region == 2, cond[2], 0.0)),
    )


def pack_kernel(cond, forcing, start, latest, region, out):
    steps, comps, _, ny, _ = forcing.shape
    rows = out.shape[0] // ny
    is_first = (lax.axis_index("yh") == 0) & (lax.axis_index("z") == 0)
    sigma = material(region[0], cond)
    for c in range(comps):
        head = forcing[0, c, 0]
        head = head + jnp.where(is_first, sigma * start[c, 0], 0.0)
        out[pl.ds(c * steps, ny, stride=rows), :] = head
        for b in range(1, steps):
            out[pl.ds(c * steps + b, ny, stride=rows), :] = forcing[b, c, 0]
        out[pl.ds(comps * steps + c, ny, stride=rows), :] = -ALPHA * (sigma * latest[0, c, 0])
    for pad in range(comps * steps + comps, rows):
        out[pl.ds(pad, ny, stride=rows), :] = jnp.zeros_like(sigma)


def forward_kernel(cond, got, tables, region, out):
    groups, _, nz = got.shape
    window = tables.shape[1]
    steps = window // groups
    comps = 3
    half = window // 2
    head = lax.broadcasted_iota(jnp.int32, (window, nz), 0) == 0
    parts = []
    for c in range(comps):
        part = got[:, c * steps : (c + 1) * steps, :].reshape(window, nz)
        row = got[groups - 1, comps * steps + c : comps * steps + c + 1, :]
        parts.append(part + jnp.where(head, row, 0.0))
    spectrum = product(tables[0], jnp.concatenate(parts, axis=1))
    width = comps * nz
    line = region[lax.axis_index("yh"), pl.ds(lax.axis_index("z"), 1), :]
    weight = jnp.broadcast_to(material(line, cond), (8, nz))
    cols = out.shape[0] // half
    for at in range(half // 8):
        begin = place_of(at) * 8
        for k in range(2 * comps):
            block = spectrum[
                k // comps * half + at * 8 : k // comps * half + at * 8 + 8,
                k % comps * nz : (k % comps + 1) * nz,
            ]
            out[pl.ds(begin * cols + k, 8, stride=cols), :] = block
        out[pl.ds(begin * cols + 2 * comps, 8, stride=cols), :] = weight


def inverse_kernel(got, tables, out):
    groups, rows, nz = out.shape
    _, window, _ = tables.shape
    half = window // 2
    steps = window // groups
    cols = got.shape[0] // half
    def member(f):
        return jnp.concatenate(
            [
                jnp.concatenate(
                    [
                        got[pl.ds(place_of(at) * 8 * cols + k, 8, stride=cols), :]
                        for at in range(half // 8)
                    ],
                    axis=0,
                )
                for k in range(f * cols // 2, (f + 1) * cols // 2)
            ],
            axis=1,
        )

    result = product(tables[1], jnp.concatenate([member(0), member(1)], axis=0))
    for c in range(rows // steps):
        out[:, c * steps : (c + 1) * steps, :] = result[:, c * nz : (c + 1) * nz].reshape(
            groups, steps, nz
        )


def unpack_kernel(got, out):
    steps, comps, _, ny, _ = out.shape
    rows = got.shape[0] // ny
    for c in range(comps):
        for b in range(steps):
            out[b, c, 0] = got[pl.ds(c * steps + b, ny, stride=rows), :]


def operator(sigma):
    ny, nz = sigma.shape[2:]
    row = lax.broadcasted_iota(jnp.int32, (ny, nz), 0)
    lane = lax.broadcasted_iota(jnp.int32, (ny, nz), 1)
    row_first, row_last = row == 0, row == ny - 1
    lane_first, lane_last = lane == 0, lane == nz - 1

    def ahead_y(f):
        return jnp.where(row_last, 0.0, pltpu.roll(f, ny - 1, 0))

    def ahead_z(f):
        return jnp.where(lane_last, 0.0, pltpu.roll(f, nz - 1, 1))

    def behind_y(f):
        return jnp.where(row_first, 0.0, pltpu.roll(f, 1, 0))

    def behind_z(f):
        return jnp.where(lane_first, 0.0, pltpu.roll(f, 1, 1))

    def curls(now, after):
        flux = []
        for f in (0, 3):
            ex, ey, ez = now[f : f + 3]
            _, ey_after, ez_after = after[f : f + 3]
            flux += [
                (ahead_y(ez) - ez) - (ahead_z(ey) - ey),
                (ahead_z(ex) - ex) - (ez_after - ez),
                (ey_after - ey) - (ahead_y(ex) - ex),
            ]
        return flux

    def tails(now, after):
        flux = []
        for f in (0, 3):
            ex, ey, ez = now[f : f + 3]
            _, ey_after, ez_after = after[f : f + 3]
            flux += [
                (ahead_z(ex) - ex) - (ez_after - ez),
                (ey_after - ey) - (ahead_y(ex) - ex),
            ]
        return flux

    def adjoints(flux, before):
        field = []
        for f, g in ((0, 0), (3, 2)):
            bx, by, bz = flux[f : f + 3]
            by_before, bz_before = before[g : g + 2]
            field += [
                (behind_z(by) - by) - (behind_y(bz) - bz),
                (bz_before - bz) - (behind_z(bx) - bx),
                (behind_y(bx) - bx) - (by_before - by),
            ]
        return field

    def add_couple(field, values, weight, sign):
        sp, sm, sq = weight
        if sign > 0:
            return [
                field[c] + (sp * values[c] - sq * values[3 + c]) for c in range(3)
            ] + [field[3 + c] + (sm * values[3 + c] + sq * values[c]) for c in range(3)]
        return [
            field[c] + (sp * values[c] + sq * values[3 + c]) for c in range(3)
        ] + [field[3 + c] + (sm * values[3 + c] - sq * values[c]) for c in range(3)]

    def lift(flux, source, begin, edge):
        now = load(source, begin)
        before = tails(load(source, begin - 1), now)
        for k, v in zip((1, 2, 4, 5), before):
            flux[0, k] = v if edge is None else jnp.where(edge, 0.0, v)
        for u in range(flux.shape[0] - 1):
            after = load(source, begin + u + 1)
            for k, v in enumerate(curls(now, after)):
                flux[u + 1, k] = v
            now = after

    def drop(flux, source, begin, sign, finish):
        before = [flux[0, k] for k in (1, 2, 4, 5)]
        for u in range(flux.shape[0] - 1):
            i = begin + u
            now = [flux[u + 1, k] for k in range(6)]
            value = adjoints(now, before)
            finish(i, add_couple(value, load(source, i), [sigma[i + GUARD, k] for k in range(3)], sign))
            before = [now[k] for k in (1, 2, 4, 5)]

    return lift, drop


def load(ref, at):
    return [ref[at + GUARD, k] for k in range(6)]


def store(ref, at, values):
    for k in range(6):
        ref[at + GUARD, k] = values[k]


def finishers(terms, field, first, resid, total, place):
    inv_scale = terms[3, pair_index()]
    center = chebyshev_terms(SWEEPS - 1)[2]

    def begin_with(i, value):
        step = [v * (inv_scale * (1.0 / center)) for v in value]
        store(resid, place(i), value)
        store(field, place(i), step)
        store(total, place(i), step)

    def keep_first(i, value):
        store(first, place(i), value)

    def update(carry_term, push_term):
        push_term = push_term * inv_scale

        def do(i, value):
            rest = [r - v for r, v in zip(load(resid, i), value)]
            step = [carry_term * d + push_term * r for d, r in zip(load(field, i), rest)]
            store(resid, place(i), rest)
            store(field, place(i), step)
            store(total, place(i), [x + d for x, d in zip(load(total, i), step)])

        return do

    return begin_with, keep_first, update


def fill(terms, first, sigma, source, rows, begins):
    ny, nz = sigma.shape[2:]
    cols = 7
    pair = pair_index()
    for row, (x_at, y_at, p) in rows:
        i = begins[x_at] + 2 * STRIPE * y_at + p
        parts = [source[pl.ds(row * cols * ny + k, ny, stride=cols), :] for k in range(cols)]
        store(first, i, parts[:6])
        for k in range(3):
            sigma[i + GUARD, k] = parts[6] * terms[k, pair]


def brick_rows():
    order = itertools.product(range(4), range(STRIPE), range(2))
    return [(row, (x_at, y_at, p)) for row, (y_at, p, x_at) in enumerate(order)]


def halo_rows():
    order = [(0, y_at, p) for y_at in range(4) for p in range(STRIPE)]
    order += [(1, y_at, p) for y_at in range(2) for p in range(STRIPE)]
    return list(enumerate(order))


def inner_kernel(sweeps, terms, weights, *refs):
    *given, field, first, resid, total, sigma, flux_a, flux_b = refs
    ny, nz = sigma.shape[2:]
    blank = jnp.zeros((ny, nz), jnp.float32)
    half_at, core_at = lax.axis_index("xh"), lax.axis_index("c")
    lift, drop = operator(sigma)
    size = flux_a.shape[0] - 1

    begins_all = sweeps.start == 0
    for ref in (first, field):
        store(ref, -1, [blank] * 6)
        store(ref, HALF, [blank] * 6)
    if begins_all:
        for source, core in zip(given, (core_at, 1 - core_at)):
            begin = STRIPE * core
            fill(terms, first, sigma, source, brick_rows(), (begin, begin + HALF // 2))
    else:
        for ref, old in zip((field, first, resid, total), given):
            for i in range(HALF):
                store(ref, i, load(old, i))
        for i in range(HALF):
            for k in range(3):
                sigma[i + GUARD, k] = given[4][i + GUARD, k]

    def begin_of(level):
        count = (HALF - level + size - 1) // size
        return half_at * (HALF - count * size), count

    def run(level, flux, source, sign, finish, other_flux, other_source, beside):
        low, count = begin_of(level)
        other_low, _ = begin_of(level + 1)

        def at_edge(begin):
            return (begin == 0) & (half_at == 0)

        def step(t, _):
            begin = low + t * size
            drop(flux, source, begin, sign, finish)
            lift(flux, source, begin + size, None)
            return 0

        lax.fori_loop(0, count - 1, step, 0)
        if beside:
            lift(other_flux, other_source, other_low, at_edge(other_low))
        drop(flux, source, low + (count - 1) * size, sign, finish)
        if not beside:
            lift(other_flux, other_source, other_low, at_edge(other_low))

    def placed(level):
        low, high = half_at * level, HALF - level + half_at * level
        return lambda i: jnp.where((i >= low) & (i < high), i, HALF + 1)

    begin_with, _, _ = finishers(terms, field, first, resid, total, placed(1))
    if begins_all:
        lift(flux_b, first, begin_of(1)[0], half_at == 0)
        run(1, flux_b, first, -1.0, begin_with, flux_a, field, True)
    else:
        low, _ = begin_of(2 + 2 * sweeps.start)
        lift(flux_a, field, low, (low == 0) & (half_at == 0))

    def sweep(s, beside):
        _, keep_first, _ = finishers(terms, field, first, resid, total, placed(2 + 2 * s))
        _, _, update = finishers(terms, field, first, resid, total, placed(3 + 2 * s))
        run(2 + 2 * s, flux_a, field, 1.0, keep_first, flux_b, first, beside)
        run(
            3 + 2 * s,
            flux_b,
            first,
            -1.0,
            update(weights[0, s], weights[1, s]),
            flux_a,
            field,
            beside,
        )

    def early(s, _):
        sweep(s, True)
        return 0

    def late(s, _):
        sweep(s, False)
        return 0

    apart = max(s for s in range(SWEEPS) if (HALF - 4 - 2 * s + size - 1) // size >= 3) + 1
    between = min(max(apart, sweeps.start), sweeps.stop)
    lax.fori_loop(sweeps.start, between, early, 0)
    lax.fori_loop(between, sweeps.stop, late, 0)


def outer_kernel(
    terms, weights, part, part_mate, *refs
):
    given, out, state, (flux_a, flux_b) = refs[:5], refs[5], refs[6:11], refs[11:]
    field, first, resid, total, sigma = state
    ny, nz = sigma.shape[2:]
    half_at, core_at = lax.axis_index("xh"), lax.axis_index("c")
    lift, drop = operator(sigma)
    size = flux_a.shape[0] - 1

    own_low = REACH * half_at
    for ref, old in zip(state[:4], given[:4]):
        for i in range(HALF):
            store(ref, own_low + i, load(old, i))
    for i in range(HALF):
        for k in range(3):
            sigma[own_low + i + GUARD, k] = given[4][i + GUARD, k]
    halo_low = HALF * (1 - half_at)
    for source, core in ((part, core_at), (part_mate, 1 - core_at)):
        begin = halo_low + STRIPE * core
        whole_x = begin + (REACH - HALF // 2) * half_at
        half_x = begin + HALF // 2 * (1 - half_at)
        fill(terms, first, sigma, source, halo_rows(), (whole_x, half_x))

    def begin_of(level, turn):
        low = jnp.where(half_at == 0, HALF - level, level)
        return low + jnp.where(half_at == 0, turn, 1 - turn) * size

    def run(level, source, sign, finish, other_source):
        drop(flux_a, source, begin_of(level, 0), sign, finish)
        lift(flux_b, source, begin_of(level, 1), None)
        lift(flux_a, other_source, begin_of(level + 1, 0), None)
        drop(flux_b, source, begin_of(level, 1), sign, finish)

    begin_with, keep_first, update = finishers(terms, field, first, resid, total, lambda i: i)
    lift(flux_a, first, begin_of(1, 0), None)
    run(1, first, -1.0, begin_with, field)

    def sweep(s, _):
        run(2 + 2 * s, field, 1.0, keep_first, first)
        run(3 + 2 * s, first, -1.0, update(weights[0, s], weights[1, s]), field)
        return 0

    lax.fori_loop(0, SWEEPS - 1, sweep, 0)

    own_begin = own_low + STRIPE * core_at
    for row, (x_at, y_at, p) in brick_rows():
        i = own_begin + HALF // 2 * x_at + 2 * STRIPE * y_at + p
        for k, v in enumerate(load(total, i)):
            out[pl.ds(row * 6 * ny + k, ny, stride=6), :] = v


def per_device(forcing, start_field, iterate, region, conductance):
    steps, comps, planes, ny, nz = forcing.shape
    groups = lax.axis_size(TM)
    window = steps * groups
    half = window // 2
    both = jnp.asarray(np.stack(tables(window)))
    vmem = pl.BlockSpec(memory_space=pltpu.VMEM)
    smem = pl.BlockSpec(memory_space=pltpu.SMEM)
    f32 = jnp.float32
    params = pltpu.CompilerParams(vmem_limit_bytes=14 * 1024 * 1024)

    rows = comps * steps + 8
    plane_of = pl.BlockSpec((steps, comps, 1, ny, nz), lambda p: (0, 0, p, 0, 0))
    packed = pl.pallas_call(
        pack_kernel,
        out_shape=jax.ShapeDtypeStruct((groups * rows, nz), f32),
        grid=(planes,),
        in_specs=[
            smem,
            plane_of,
            pl.BlockSpec((comps, 1, ny, nz), lambda p: (0, p, 0, 0)),
            pl.BlockSpec((1, comps, 1, ny, nz), lambda p: (steps - 1, 0, p, 0, 0)),
            pl.BlockSpec((1, ny, nz), lambda p: (p, 0, 0)),
        ],
        out_specs=pl.BlockSpec((ny * rows, nz), lambda p: (p, 0)),
        compiler_params=pltpu.CompilerParams(vmem_limit_bytes=60 * 1024 * 1024),
        name="pack",
    )(conductance, forcing, start_field, iterate, region)

    got = lax.all_to_all(packed.reshape(groups, rows, nz), TM, 0, 0, tiled=True)

    spectrum = pl.pallas_call(
        forward_kernel,
        out_shape=jax.ShapeDtypeStruct((half * (2 * comps + 1), nz), f32),
        in_specs=[smem, vmem, vmem, vmem],
        out_specs=vmem,
        compiler_params=params,
        name="forward",
    )(conductance, got, both, region)

    mine = lax.all_to_all(
        spectrum.reshape(half, 1, (2 * comps + 1) * nz), GROUP, 0, 0, tiled=True
    )

    half_at = lax.axis_index("xh")
    bricks = mine.reshape(4, planes, 2, ny * (2 * comps + 1), nz)
    near = lax.dynamic_index_in_dim(bricks, 1 - half_at, 2, keepdims=False)
    beyond = lax.dynamic_slice(
        bricks, (2 * (1 - half_at), 0, half_at, 0, 0), (2, planes, 1) + bricks.shape[3:]
    )
    part = jnp.concatenate([near, beyond[:, :, 0]], axis=0).reshape(-1, nz)
    mine = mine.reshape(half * (2 * comps + 1), nz)
    blocks = lax.axis_size(("xh", "xl"))
    part = lax.ppermute(part, ("xh", "xl"), [(i, blocks - 1 - i) for i in range(blocks)])
    mate = lax.ppermute(mine, "c", [(0, 1), (1, 0)])

    terms = jnp.asarray(pair_table(window))
    weights = jnp.asarray(np.array(chebyshev_terms(SWEEPS - 1)[:2], np.float32))

    def state(places):
        return [(places, 2 * comps, ny, nz)] * 4 + [(places, 3, ny, nz)]

    def flux(planes):
        return pltpu.VMEM((planes + 1, 2 * comps, ny, nz), f32)

    def inner(sweeps, given):
        return pl.pallas_call(
            functools.partial(inner_kernel, sweeps),
            out_shape=[jax.ShapeDtypeStruct(shape, f32) for shape in state(HALF + 3 * GUARD)],
            in_specs=[smem, smem] + [vmem] * len(given),
            out_specs=[vmem] * 5,
            scratch_shapes=[flux(INNER)] * 2,
            compiler_params=params,
            cost_estimate=pl.CostEstimate(
                flops=10**10, bytes_accessed=2 * 10**7, transcendentals=0
            ),
            name="inner",
        )(terms, weights, *given)

    early = inner(range(0, EARLY), (mine, mate))
    part, early = lax.optimization_barrier((part, early))
    part_mate = lax.ppermute(part, "c", [(0, 1), (1, 0)])
    late = inner(range(EARLY, SWEEPS - 1), early)
    solved = pl.pallas_call(
        outer_kernel,
        out_shape=jax.ShapeDtypeStruct((half * 2 * comps, nz), f32),
        in_specs=[smem, smem] + [vmem] * 7,
        out_specs=vmem,
        scratch_shapes=[pltpu.VMEM(shape, f32) for shape in state(HALF + REACH + 2 * GUARD)]
        + [flux(OUTER)] * 2,
        compiler_params=params,
        name="outer",
    )(terms, weights, part, part_mate, *late)

    back = lax.all_to_all(
        solved.reshape(half, 1, 2 * comps * nz), GROUP, 0, 0, tiled=True
    ).reshape(half * 2 * comps, nz)

    pencil = pl.pallas_call(
        inverse_kernel,
        out_shape=jax.ShapeDtypeStruct((groups, comps * steps, nz), f32),
        in_specs=[vmem, vmem],
        out_specs=vmem,
        compiler_params=params,
        name="inverse",
    )(back, both)

    home = lax.all_to_all(pencil, TM, 0, 0, tiled=True)

    return pl.pallas_call(
        unpack_kernel,
        out_shape=jax.ShapeDtypeStruct(forcing.shape, f32),
        grid=(planes,),
        in_specs=[pl.BlockSpec((ny * comps * steps, nz), lambda p: (p, 0))],
        out_specs=plane_of,
        compiler_params=params,
        name="unpack",
    )(home.reshape(groups * comps * steps, nz))


def solution(mesh):
    names = ("yh", "z", "xh", "xl", "yl", "c")
    fine = Mesh(mesh.devices.reshape(2, 8, 2, 2, 4, 2), names)
    space = ("xh", "xl", "yl", "c")
    placed = (
        P(TM, None, space, None, None),
        P(None, space, None, None),
        P(TM, None, space, None, None),
        P(space, None, None),
        P(),
    )
    return jax.shard_map(
        per_device,
        mesh=fine,
        in_specs=placed,
        out_specs=P(TM, None, space, None, None),
        check_vma=False,
    )
```

```python
import functools
import itertools
import math

import jax
import jax.numpy as jnp
import numpy as np
from jax import lax
from jax.experimental import pallas as pl
from jax.experimental.pallas import tpu as pltpu
from jax.sharding import Mesh
from jax.sharding import PartitionSpec as P

SWEEPS = 12
ALPHA = 0.1
LOWER = 0.02
UPPER = 1.0
SIGMA_TOP = 4.0
CURL_TOP = 12.0

TM = ("yh", "z")
GROUP = ("yl", "yh", "xl", "z")
HALF = 32
REACH = 24
STRIPE = 2
GUARD = 1
INNER = 8
OUTER = 12
EARLY = 9


def pair_index():
    index = 0
    for name in GROUP:
        at = lax.axis_index(name)
        if name == "xl":
            at = (at + lax.axis_index("xh")) % 2
        index = index * lax.axis_size(name) + at
    return index


def place_of(block):
    flip = lax.axis_index("xh")
    return block + (flip if block % 2 == 0 else -flip)


def tables(window):
    gamma = ALPHA ** (1.0 / window)
    half = window // 2
    pairs = np.arange(half)
    freqs = np.concatenate([pairs, np.where(pairs == 0, half, window - pairs)])
    moments = np.arange(window)
    angle = 2.0 * math.pi * (freqs[:, None] * moments[None, :] % window) / window
    cas = np.cos(angle) + np.sin(angle)
    forward = cas * gamma ** moments[None, :]
    inverse = cas.T * gamma ** (-moments[:, None]) / window
    return forward.astype(np.float32), inverse.astype(np.float32)


def product(table, values):
    def parts(array):
        high = array.astype(jnp.bfloat16)
        return high, (array - high.astype(jnp.float32)).astype(jnp.bfloat16)

    (table_high, table_low), (high, low) = parts(table), parts(values)
    return jnp.dot(
        jnp.concatenate([table_high, table_low, table_high], axis=1),
        jnp.concatenate([high, high, low], axis=0),
        preferred_element_type=jnp.float32,
    )


def pair_table(window):
    gamma = ALPHA ** (1.0 / window)
    pairs = np.arange(window // 2)
    theta = 2.0 * math.pi * pairs / window
    plain = 1.0 - gamma * np.cos(theta)
    p_plus = np.where(pairs == 0, 1.0 - gamma, plain)
    p_minus = np.where(pairs == 0, 1.0 + gamma, plain)
    q_term = np.where(pairs == 0, 0.0, gamma * np.sin(theta))
    bound = np.sqrt(np.maximum(p_plus, p_minus) ** 2 + q_term**2) * SIGMA_TOP + CURL_TOP
    return np.stack([p_plus, p_minus, q_term, 1.0 / bound**2]).astype(np.float32)


def chebyshev_terms(count):
    center = (UPPER + LOWER) / 2.0
    radius = (UPPER - LOWER) / 2.0
    spread_ratio = center / radius
    weight_now = 1.0 / spread_ratio
    carry_terms, push_terms = ([], [])
    for _ in range(count):
        weight_next = 1.0 / (2.0 * spread_ratio - weight_now)
        carry_terms.append(weight_next * weight_now)
        push_terms.append(2.0 * weight_next / radius)
        weight_now = weight_next
    return (carry_terms, push_terms, center)


def material(region, cond):
    return jnp.where(
        region == 0,
        cond[0],
        jnp.where(region == 1, cond[1], jnp.where(region == 2, cond[2], 0.0)),
    )


def pack_kernel(cond, forcing, start, latest, region, out):
    steps, comps, _, ny, _ = forcing.shape
    rows = out.shape[0] // ny
    is_first = (lax.axis_index("yh") == 0) & (lax.axis_index("z") == 0)
    sigma = material(region[0], cond)
    for c in range(comps):
        head = forcing[0, c, 0]
        head = head + jnp.where(is_first, sigma * start[c, 0], 0.0)
        out[pl.ds(c * steps, ny, stride=rows), :] = head
        for b in range(1, steps):
            out[pl.ds(c * steps + b, ny, stride=rows), :] = forcing[b, c, 0]
        out[pl.ds(comps * steps + c, ny, stride=rows), :] = -ALPHA * (sigma * latest[0, c, 0])
    for pad in range(comps * steps + comps, rows):
        out[pl.ds(pad, ny, stride=rows), :] = jnp.zeros_like(sigma)


def forward_kernel(cond, got, tables, region, out):
    groups, _, nz = got.shape
    window = tables.shape[1]
    steps = window // groups
    comps = 3
    half = window // 2
    head = lax.broadcasted_iota(jnp.int32, (window, nz), 0) == 0
    parts = []
    for c in range(comps):
        part = got[:, c * steps : (c + 1) * steps, :].reshape(window, nz)
        row = got[groups - 1, comps * steps + c : comps * steps + c + 1, :]
        parts.append(part + jnp.where(head, row, 0.0))
    spectrum = product(tables[0], jnp.concatenate(parts, axis=1))
    width = comps * nz
    line = region[lax.axis_index("yh"), pl.ds(lax.axis_index("z"), 1), :]
    weight = jnp.broadcast_to(material(line, cond), (8, nz))
    cols = out.shape[0] // half
    for at in range(half // 8):
        begin = place_of(at) * 8
        for k in range(2 * comps):
            block = spectrum[
                k // comps * half + at * 8 : k // comps * half + at * 8 + 8,
                k % comps * nz : (k % comps + 1) * nz,
            ]
            out[pl.ds(begin * cols + k, 8, stride=cols), :] = block
        out[pl.ds(begin * cols + 2 * comps, 8, stride=cols), :] = weight


def inverse_kernel(got, tables, out):
    groups, rows, nz = out.shape
    _, window, _ = tables.shape
    half = window // 2
    steps = window // groups
    cols = got.shape[0] // half
    def member(f):
        return jnp.concatenate(
            [
                jnp.concatenate(
                    [
                        got[pl.ds(place_of(at) * 8 * cols + k, 8, stride=cols), :]
                        for at in range(half // 8)
                    ],
                    axis=0,
                )
                for k in range(f * cols // 2, (f + 1) * cols // 2)
            ],
            axis=1,
        )

    result = product(tables[1], jnp.concatenate([member(0), member(1)], axis=0))
    for c in range(rows // steps):
        out[:, c * steps : (c + 1) * steps, :] = result[:, c * nz : (c + 1) * nz].reshape(
            groups, steps, nz
        )


def unpack_kernel(got, out):
    steps, comps, _, ny, _ = out.shape
    rows = got.shape[0] // ny
    for c in range(comps):
        for b in range(steps):
            out[b, c, 0] = got[pl.ds(c * steps + b, ny, stride=rows), :]


def operator(terms, sigma):
    ny, nz = sigma.shape[1:]
    pair = pair_index()
    p_plus, p_minus, q_term = terms[0, pair], terms[1, pair], terms[2, pair]

    row = lax.broadcasted_iota(jnp.int32, (ny, nz), 0)
    lane = lax.broadcasted_iota(jnp.int32, (ny, nz), 1)
    row_first, row_last = row == 0, row == ny - 1
    lane_first, lane_last = lane == 0, lane == nz - 1

    def ahead_y(f):
        return jnp.where(row_last, 0.0, pltpu.roll(f, ny - 1, 0))

    def ahead_z(f):
        return jnp.where(lane_last, 0.0, pltpu.roll(f, nz - 1, 1))

    def behind_y(f):
        return jnp.where(row_first, 0.0, pltpu.roll(f, 1, 0))

    def behind_z(f):
        return jnp.where(lane_first, 0.0, pltpu.roll(f, 1, 1))

    def curls(now, after):
        flux = []
        for f in (0, 3):
            ex, ey, ez = now[f : f + 3]
            _, ey_after, ez_after = after[f : f + 3]
            flux += [
                (ahead_y(ez) - ez) - (ahead_z(ey) - ey),
                (ahead_z(ex) - ex) - (ez_after - ez),
                (ey_after - ey) - (ahead_y(ex) - ex),
            ]
        return flux

    def tails(now, after):
        flux = []
        for f in (0, 3):
            ex, ey, ez = now[f : f + 3]
            _, ey_after, ez_after = after[f : f + 3]
            flux += [
                (ahead_z(ex) - ex) - (ez_after - ez),
                (ey_after - ey) - (ahead_y(ex) - ex),
            ]
        return flux

    def adjoints(flux, before):
        field = []
        for f, g in ((0, 0), (3, 2)):
            bx, by, bz = flux[f : f + 3]
            by_before, bz_before = before[g : g + 2]
            field += [
                (behind_z(by) - by) - (behind_y(bz) - bz),
                (bz_before - bz) - (behind_z(bx) - bx),
                (behind_y(bx) - bx) - (by_before - by),
            ]
        return field

    def add_couple(field, values, weight, sign):
        sp, sm, sq = weight * p_plus, weight * p_minus, weight * (sign * q_term)
        return [
            field[c] + (sp * values[c] - sq * values[3 + c]) for c in range(3)
        ] + [field[3 + c] + (sm * values[3 + c] + sq * values[c]) for c in range(3)]

    def lift(flux, source, begin, edge):
        now = load(source, begin)
        before = tails(load(source, begin - 1), now)
        for k, v in zip((1, 2, 4, 5), before):
            flux[0, k] = v if edge is None else jnp.where(edge, 0.0, v)
        for u in range(flux.shape[0] - 1):
            after = load(source, begin + u + 1)
            for k, v in enumerate(curls(now, after)):
                flux[u + 1, k] = v
            now = after

    def drop(flux, source, begin, sign, finish):
        before = [flux[0, k] for k in (1, 2, 4, 5)]
        for u in range(flux.shape[0] - 1):
            i = begin + u
            now = [flux[u + 1, k] for k in range(6)]
            value = adjoints(now, before)
            finish(i, add_couple(value, load(source, i), sigma[i + GUARD], sign))
            before = [now[k] for k in (1, 2, 4, 5)]

    return lift, drop


def load(ref, at):
    return [ref[at + GUARD, k] for k in range(6)]


def store(ref, at, values):
    for k in range(6):
        ref[at + GUARD, k] = values[k]


def finishers(terms, field, first, resid, total, place):
    inv_scale = terms[3, pair_index()]
    center = chebyshev_terms(SWEEPS - 1)[2]

    def begin_with(i, value):
        step = [v * (inv_scale * (1.0 / center)) for v in value]
        store(resid, place(i), value)
        store(field, place(i), step)
        store(total, place(i), step)

    def keep_first(i, value):
        store(first, place(i), value)

    def update(carry_term, push_term):
        push_term = push_term * inv_scale

        def do(i, value):
            rest = [r - v for r, v in zip(load(resid, i), value)]
            step = [carry_term * d + push_term * r for d, r in zip(load(field, i), rest)]
            store(resid, place(i), rest)
            store(field, place(i), step)
            store(total, place(i), [x + d for x, d in zip(load(total, i), step)])

        return do

    return begin_with, keep_first, update


def fill(first, sigma, source, rows, begins):
    ny, nz = sigma.shape[1:]
    cols = 7
    for row, (x_at, y_at, p) in rows:
        i = begins[x_at] + 2 * STRIPE * y_at + p
        parts = [source[pl.ds(row * cols * ny + k, ny, stride=cols), :] for k in range(cols)]
        store(first, i, parts[:6])
        sigma[i + GUARD] = parts[6]


def brick_rows():
    order = itertools.product(range(4), range(STRIPE), range(2))
    return [(row, (x_at, y_at, p)) for row, (y_at, p, x_at) in enumerate(order)]


def halo_rows():
    order = [(0, y_at, p) for y_at in range(4) for p in range(STRIPE)]
    order += [(1, y_at, p) for y_at in range(2) for p in range(STRIPE)]
    return list(enumerate(order))


def inner_kernel(sweeps, terms, weights, *refs):
    *given, field, first, resid, total, sigma, flux_a, flux_b = refs
    ny, nz = sigma.shape[1:]
    blank = jnp.zeros((ny, nz), jnp.float32)
    half_at, core_at = lax.axis_index("xh"), lax.axis_index("c")
    lift, drop = operator(terms, sigma)
    size = flux_a.shape[0] - 1

    begins_all = sweeps.start == 0
    for ref in (first, field):
        store(ref, -1, [blank] * 6)
        store(ref, HALF, [blank] * 6)
    if begins_all:
        for source, core in zip(given, (core_at, 1 - core_at)):
            begin = STRIPE * core
            fill(first, sigma, source, brick_rows(), (begin, begin + HALF // 2))
    else:
        for ref, old in zip((field, first, resid, total), given):
            for i in range(HALF):
                store(ref, i, load(old, i))
        for i in range(HALF):
            sigma[i + GUARD] = given[4][i + GUARD]

    def begin_of(level):
        count = (HALF - level + size - 1) // size
        return half_at * (HALF - count * size), count

    def run(level, flux, source, sign, finish, other_flux, other_source, beside):
        low, count = begin_of(level)
        other_low, _ = begin_of(level + 1)

        def at_edge(begin):
            return (begin == 0) & (half_at == 0)

        def step(t, _):
            begin = low + t * size
            drop(flux, source, begin, sign, finish)
            lift(flux, source, begin + size, None)
            return 0

        lax.fori_loop(0, count - 1, step, 0)
        if beside:
            lift(other_flux, other_source, other_low, at_edge(other_low))
        drop(flux, source, low + (count - 1) * size, sign, finish)
        if not beside:
            lift(other_flux, other_source, other_low, at_edge(other_low))

    def placed(level):
        low, high = half_at * level, HALF - level + half_at * level
        return lambda i: jnp.where((i >= low) & (i < high), i, HALF + 1)

    begin_with, _, _ = finishers(terms, field, first, resid, total, placed(1))
    if begins_all:
        lift(flux_b, first, begin_of(1)[0], half_at == 0)
        run(1, flux_b, first, -1.0, begin_with, flux_a, field, True)
    else:
        low, _ = begin_of(2 + 2 * sweeps.start)
        lift(flux_a, field, low, (low == 0) & (half_at == 0))

    def sweep(s, beside):
        _, keep_first, _ = finishers(terms, field, first, resid, total, placed(2 + 2 * s))
        _, _, update = finishers(terms, field, first, resid, total, placed(3 + 2 * s))
        run(2 + 2 * s, flux_a, field, 1.0, keep_first, flux_b, first, beside)
        run(
            3 + 2 * s,
            flux_b,
            first,
            -1.0,
            update(weights[0, s], weights[1, s]),
            flux_a,
            field,
            beside,
        )

    def early(s, _):
        sweep(s, True)
        return 0

    def late(s, _):
        sweep(s, False)
        return 0

    apart = max(s for s in range(SWEEPS) if (HALF - 4 - 2 * s + size - 1) // size >= 3) + 1
    between = min(max(apart, sweeps.start), sweeps.stop)
    lax.fori_loop(sweeps.start, between, early, 0)
    lax.fori_loop(between, sweeps.stop, late, 0)


def outer_kernel(
    terms, weights, part, part_mate, *refs
):
    given, out, state, (flux_a, flux_b) = refs[:5], refs[5], refs[6:11], refs[11:]
    field, first, resid, total, sigma = state
    ny, nz = sigma.shape[1:]
    half_at, core_at = lax.axis_index("xh"), lax.axis_index("c")
    lift, drop = operator(terms, sigma)
    size = flux_a.shape[0] - 1

    own_low = REACH * half_at
    for ref, old in zip(state[:4], given[:4]):
        for i in range(HALF):
            store(ref, own_low + i, load(old, i))
    for i in range(HALF):
        sigma[own_low + i + GUARD] = given[4][i + GUARD]
    halo_low = HALF * (1 - half_at)
    for source, core in ((part, core_at), (part_mate, 1 - core_at)):
        begin = halo_low + STRIPE * core
        whole_x = begin + (REACH - HALF // 2) * half_at
        half_x = begin + HALF // 2 * (1 - half_at)
        fill(first, sigma, source, halo_rows(), (whole_x, half_x))

    def begin_of(level, turn):
        low = jnp.where(half_at == 0, HALF - level, level)
        return low + jnp.where(half_at == 0, turn, 1 - turn) * size

    def run(level, source, sign, finish, other_source):
        drop(flux_a, source, begin_of(level, 0), sign, finish)
        lift(flux_b, source, begin_of(level, 1), None)
        lift(flux_a, other_source, begin_of(level + 1, 0), None)
        drop(flux_b, source, begin_of(level, 1), sign, finish)

    begin_with, keep_first, update = finishers(terms, field, first, resid, total, lambda i: i)
    lift(flux_a, first, begin_of(1, 0), None)
    run(1, first, -1.0, begin_with, field)

    def sweep(s, _):
        run(2 + 2 * s, field, 1.0, keep_first, first)
        run(3 + 2 * s, first, -1.0, update(weights[0, s], weights[1, s]), field)
        return 0

    lax.fori_loop(0, SWEEPS - 1, sweep, 0)

    own_begin = own_low + STRIPE * core_at
    for row, (x_at, y_at, p) in brick_rows():
        i = own_begin + HALF // 2 * x_at + 2 * STRIPE * y_at + p
        for k, v in enumerate(load(total, i)):
            out[pl.ds(row * 6 * ny + k, ny, stride=6), :] = v


def per_device(forcing, start_field, iterate, region, conductance):
    steps, comps, planes, ny, nz = forcing.shape
    groups = lax.axis_size(TM)
    window = steps * groups
    half = window // 2
    both = jnp.asarray(np.stack(tables(window)))
    vmem = pl.BlockSpec(memory_space=pltpu.VMEM)
    smem = pl.BlockSpec(memory_space=pltpu.SMEM)
    f32 = jnp.float32
    params = pltpu.CompilerParams(vmem_limit_bytes=14 * 1024 * 1024)

    rows = comps * steps + 8
    plane_of = pl.BlockSpec((steps, comps, 1, ny, nz), lambda p: (0, 0, p, 0, 0))
    packed = pl.pallas_call(
        pack_kernel,
        out_shape=jax.ShapeDtypeStruct((groups * rows, nz), f32),
        grid=(planes,),
        in_specs=[
            smem,
            plane_of,
            pl.BlockSpec((comps, 1, ny, nz), lambda p: (0, p, 0, 0)),
            pl.BlockSpec((1, comps, 1, ny, nz), lambda p: (steps - 1, 0, p, 0, 0)),
            pl.BlockSpec((1, ny, nz), lambda p: (p, 0, 0)),
        ],
        out_specs=pl.BlockSpec((ny * rows, nz), lambda p: (p, 0)),
        compiler_params=pltpu.CompilerParams(vmem_limit_bytes=60 * 1024 * 1024),
        name="pack",
    )(conductance, forcing, start_field, iterate, region)

    got = lax.all_to_all(packed.reshape(groups, rows, nz), TM, 0, 0, tiled=True)

    spectrum = pl.pallas_call(
        forward_kernel,
        out_shape=jax.ShapeDtypeStruct((half * (2 * comps + 1), nz), f32),
        in_specs=[smem, vmem, vmem, vmem],
        out_specs=vmem,
        compiler_params=params,
        name="forward",
    )(conductance, got, both, region)

    mine = lax.all_to_all(
        spectrum.reshape(half, 1, (2 * comps + 1) * nz), GROUP, 0, 0, tiled=True
    )

    half_at = lax.axis_index("xh")
    bricks = mine.reshape(4, planes, 2, ny * (2 * comps + 1), nz)
    near = lax.dynamic_index_in_dim(bricks, 1 - half_at, 2, keepdims=False)
    beyond = lax.dynamic_slice(
        bricks, (2 * (1 - half_at), 0, half_at, 0, 0), (2, planes, 1) + bricks.shape[3:]
    )
    part = jnp.concatenate([near, beyond[:, :, 0]], axis=0).reshape(-1, nz)
    mine = mine.reshape(half * (2 * comps + 1), nz)
    blocks = lax.axis_size(("xh", "xl"))
    part = lax.ppermute(part, ("xh", "xl"), [(i, blocks - 1 - i) for i in range(blocks)])
    mate = lax.ppermute(mine, "c", [(0, 1), (1, 0)])

    terms = jnp.asarray(pair_table(window))
    weights = jnp.asarray(np.array(chebyshev_terms(SWEEPS - 1)[:2], np.float32))

    def state(places):
        return [(places, 2 * comps, ny, nz)] * 4 + [(places, ny, nz)]

    def flux(planes):
        return pltpu.VMEM((planes + 1, 2 * comps, ny, nz), f32)

    def inner(sweeps, given):
        return pl.pallas_call(
            functools.partial(inner_kernel, sweeps),
            out_shape=[jax.ShapeDtypeStruct(shape, f32) for shape in state(HALF + 3 * GUARD)],
            in_specs=[smem, smem] + [vmem] * len(given),
            out_specs=[vmem] * 5,
            scratch_shapes=[flux(INNER)] * 2,
            compiler_params=params,
            cost_estimate=pl.CostEstimate(
                flops=10**10, bytes_accessed=2 * 10**7, transcendentals=0
            ),
            name="inner",
        )(terms, weights, *given)

    early = inner(range(0, EARLY), (mine, mate))
    part, early = lax.optimization_barrier((part, early))
    part_mate = lax.ppermute(part, "c", [(0, 1), (1, 0)])
    late = inner(range(EARLY, SWEEPS - 1), early)
    solved = pl.pallas_call(
        outer_kernel,
        out_shape=jax.ShapeDtypeStruct((half * 2 * comps, nz), f32),
        in_specs=[smem, smem] + [vmem] * 7,
        out_specs=vmem,
        scratch_shapes=[pltpu.VMEM(shape, f32) for shape in state(HALF + REACH + 2 * GUARD)]
        + [flux(OUTER)] * 2,
        compiler_params=params,
        name="outer",
    )(terms, weights, part, part_mate, *late)

    back = lax.all_to_all(
        solved.reshape(half, 1, 2 * comps * nz), GROUP, 0, 0, tiled=True
    ).reshape(half * 2 * comps, nz)

    pencil = pl.pallas_call(
        inverse_kernel,
        out_shape=jax.ShapeDtypeStruct((groups, comps * steps, nz), f32),
        in_specs=[vmem, vmem],
        out_specs=vmem,
        compiler_params=params,
        name="inverse",
    )(back, both)

    home = lax.all_to_all(pencil, TM, 0, 0, tiled=True)

    return pl.pallas_call(
        unpack_kernel,
        out_shape=jax.ShapeDtypeStruct(forcing.shape, f32),
        grid=(planes,),
        in_specs=[pl.BlockSpec((ny * comps * steps, nz), lambda p: (p, 0))],
        out_specs=plane_of,
        compiler_params=params,
        name="unpack",
    )(home.reshape(groups * comps * steps, nz))


def solution(mesh):
    names = ("yh", "z", "xh", "xl", "yl", "c")
    fine = Mesh(mesh.devices.reshape(2, 8, 2, 2, 4, 2), names)
    space = ("xh", "xl", "yl", "c")
    placed = (
        P(TM, None, space, None, None),
        P(None, space, None, None),
        P(TM, None, space, None, None),
        P(space, None, None),
        P(),
    )
    return jax.shard_map(
        per_device,
        mesh=fine,
        in_specs=placed,
        out_specs=P(TM, None, space, None, None),
        check_vma=False,
    )
```
